32 devices in a mesh: tok: 8 (over z, x), hd: 4 (over y, core).
Axes of the slice: x: 2, y: 2, z: 4, core: 2. Of those that a mesh axis runs over, the one named last changes fastest.
Arguments:
- hidden: bfloat16 [8192, 1024], P(('tok', 'hd')), may hold values from -6 to 6
- encoder: bfloat16 [1, 256, 1024], P(None, 'hd'), may hold values from -6 to 6
- cotangent: bfloat16 [8192, 1024], P(('tok', 'hd')), may hold values from -6 to 6
- block_ids: int32 [8192], P('tok'), may hold values from 0 to 63, as said below
- self_qkv: bfloat16 [1024, 3, 1024], P('tok', None, 'hd'), may hold values from -0.1875 to 0.1875
- self_out: bfloat16 [1024, 1024], P('hd', 'tok'), may hold values from -3 to 3
- cross_qkv: bfloat16 [1024, 3, 1024], P('tok', None, 'hd'), may hold values from -0.1875 to 0.1875
- cross_out: bfloat16 [1024, 1024], P('hd', 'tok'), may hold values from -3 to 3
- up_weight: bfloat16 [1024, 8192], P('tok', 'hd'), may hold values from -0.1875 to 0.1875
- down_weight: bfloat16 [8192, 1024], P('hd', 'tok'), may hold values from -0.0625 to 0.0625
- proj_bias: bfloat16 [1024, 7], P(('tok', 'hd')), may hold values from -1.796875 to 1.796875
- up_bias: bfloat16 [8192], P(('tok', 'hd')), may hold values from -1.796875 to 1.796875
- norm_gain: bfloat16 [1024, 3], P(('tok', 'hd')), may hold values from 0.5 to 1.5
- norm_shift: bfloat16 [1024, 3], P(('tok', 'hd')), may hold values from -1.796875 to 1.796875
Outputs:
- output: bfloat16 [8192, 1024], P(('tok', 'hd'))
- grad_hidden: float32 [8192, 1024], P(('tok', 'hd'))
- grad_encoder: float32 [1, 256, 1024], P(None, 'hd')
- grad_self_qkv: float32 [1024, 3, 1024], P('tok', None, 'hd')
- grad_self_out: float32 [1024, 1024], P('hd', 'tok')
- grad_cross_qkv: float32 [1024, 3, 1024], P('tok', None, 'hd')
- grad_cross_out: float32 [1024, 1024], P('hd', 'tok')
- grad_up_weight: float32 [1024, 8192], P('tok', 'hd')
- grad_down_weight: float32 [8192, 1024], P('hd', 'tok')
- grad_proj_bias: float32 [1024, 7], P(('tok', 'hd'))
- grad_up_bias: float32 [8192], P(('tok', 'hd'))
- grad_norm_gain: float32 [1024, 3], P(('tok', 'hd'))
- grad_norm_shift: float32 [1024, 3], P(('tok', 'hd'))
The draws below stay inside these ranges and needn't reach their ends.
Inputs may be any that keep to these rules, and one draw needn't show every extreme that they name: block_ids never fall along the stream; each block has 1 to 256 tokens and lies within one aligned window of 256 tokens; one block has exactly 256.
All inputs are finite; a program needn't handle non-finite values.
Results may differ from the reference program's by a relative error of at most 0.03.
Values may be sent and summed in bfloat16 or wider, within the bound.
No kernel may reach another device: no remote copies, remote signals or barrier semaphores. Data moves between devices by JAX's collectives and lax.ppermute only.
A program may use at most 576 MiB of HBM per device.

```python
import jax
import jax.numpy as jnp
from jax import lax

D = 1024
H = 16
HDIM = 64
FF = 8192
SEQ = 8192
BLOCK = 256
ENC = 256
TOKENS = 8192
NSEQ = 1


def draw_block_ids(key, part):
    key = jax.random.fold_in(key, 11)
    windows = TOKENS // BLOCK
    cuts = jax.random.randint(key, (windows,), 0, BLOCK).astype(jnp.int32)
    cuts = cuts.at[0].set(BLOCK)
    cuts = cuts.at[windows - 1].set(jnp.maximum(cuts[windows - 1], 1))
    position = jnp.arange(BLOCK, dtype=jnp.int32)
    later = (position[None, :] >= cuts[:, None]).astype(jnp.int32)
    window_ids = 2 * jnp.arange(windows, dtype=jnp.int32)
    return (window_ids[:, None] + later).reshape(TOKENS).astype(jnp.int32)


def levels(rng, extent, shards, least, top_value):
    loudness, own = 1.0, jax.random.fold_in(rng, 6)
    for axis_at, blocks in shards:
        draws = jnp.exp(jax.random.uniform(jax.random.fold_in(own, axis_at), (blocks,), jnp.float32, least / len(shards), top_value / len(shards)))
        loudness = loudness * jnp.repeat(draws, extent[axis_at] // blocks).reshape([-1 if axis == axis_at else 1 for axis in range(len(extent))])
    return loudness


def gaussian(key, dims, width, bound, split=(), kind=jnp.bfloat16):
    gain = levels(key, dims, split, -0.22, 0.18) if split else 1.0
    array = jax.random.normal(key, dims, jnp.float32) * width * gain
    return jnp.minimum(jnp.maximum(array, -bound), bound).astype(kind)


def setup_inputs(seed: int = 0) -> dict:
    seeds = jax.random.split(jax.random.key(seed), 15)
    hidden = gaussian(seeds[0], (TOKENS, D), 1.0, 6.0, ((0, 32),))
    encoder = gaussian(seeds[1], (NSEQ, ENC, D), 1.0, 6.0, ((1, 4),))
    cotangent = gaussian(seeds[2], (TOKENS, D), 1.0, 6.0, ((0, 32),))
    block_ids = draw_block_ids(jax.random.fold_in(seeds[14], 71), 0)
    self_qkv = gaussian(seeds[4], (D, 3, D), D ** -0.5, 0.1875, ((0, 8), (2, 4)))
    self_out = gaussian(seeds[5], (D, D), (D // 256) ** -0.5, 3.0, ((0, 4), (1, 8)))
    cross_qkv = gaussian(seeds[6], (D, 3, D), D ** -0.5, 0.1875, ((0, 8), (2, 4)))
    cross_out = gaussian(seeds[7], (D, D), (D // 256) ** -0.5, 3.0, ((0, 4), (1, 8)))
    up_weight = gaussian(seeds[8], (D, FF), D ** -0.5, 0.1875, ((0, 8), (1, 4)))
    down_weight = gaussian(seeds[9], (FF, D), FF ** -0.5, 0.0625, ((0, 4), (1, 8)))
    proj_bias = gaussian(seeds[10], (D, 7), 0.3, 1.796875, ((0, 32),))
    up_bias = gaussian(seeds[11], (FF,), 0.3, 1.796875, ((0, 32),))
    norm_gain = jnp.clip(1.0 + 0.1 * jax.random.normal(seeds[12], (D, 3), jnp.float32), 0.5, 1.5).astype(jnp.bfloat16)
    norm_shift = gaussian(seeds[13], (D, 3), 0.3, 1.796875, ((0, 32),))
    return {"hidden": hidden, "encoder": encoder, "cotangent": cotangent, "block_ids": block_ids, "self_qkv": self_qkv, "self_out": self_out, "cross_qkv": cross_qkv, "cross_out": cross_out, "up_weight": up_weight, "down_weight": down_weight, "proj_bias": proj_bias, "up_bias": up_bias, "norm_gain": norm_gain, "norm_shift": norm_shift}


norm_eps = 1e-05
neg_large = -1e+30
highest = lax.Precision.HIGHEST

@jax.custom_vjp
def low(v):
    return lax.optimization_barrier(v.astype(jnp.bfloat16)).astype(jnp.float32)

@jax.custom_vjp
def low_back(v):
    return v

def low_keep(v):
    return (low(v), None)

def low_pass(kept, grad):
    return (grad,)

def back_keep(v):
    return (v, None)

def back_low(kept, grad):
    return (low(grad),)
low.defvjp(low_keep, low_pass)
low_back.defvjp(back_keep, back_low)

def matmul(left, right):
    return jnp.dot(left, right, precision=highest)

def layer_norm(value, gain_vec, shift_vec):
    center = value - lax.optimization_barrier(jnp.mean(value, axis=-1, keepdims=True))
    variance = lax.optimization_barrier(jnp.mean(center * center, axis=-1, keepdims=True))
    return center * lax.rsqrt(variance + norm_eps) * gain_vec + shift_vec

def attend(queries, key_heads, value_heads, allowed):
    scores = low_back(jnp.einsum('qhd,khd->hqk', queries, key_heads, precision=highest))
    scores = jnp.where(allowed[None], scores, neg_large)
    row_max = lax.optimization_barrier(jnp.max(scores, axis=-1, keepdims=True))
    expo_val = jnp.exp(scores - row_max)
    soft_probs = expo_val / lax.optimization_barrier(jnp.sum(expo_val, axis=-1, keepdims=True))
    return jnp.einsum('hqk,khd->qhd', low(soft_probs), value_heads, precision=highest)

def self_attention(queries, key_rows, value_rows, block_of):
    tile_rows = min(512, SEQ)
    tile_total = SEQ // tile_rows
    key_heads = key_rows.reshape(SEQ, H, HDIM)
    value_heads = value_rows.reshape(SEQ, H, HDIM)

    def query_tile(tile_args):
        tile_query, tile_ids = tile_args
        allowed = block_of[None, :] <= tile_ids[:, None]
        return attend(tile_query, key_heads, value_heads, allowed)
    result = lax.map(jax.checkpoint(query_tile), (queries.reshape(tile_total, tile_rows, H, HDIM), block_of.reshape(tile_total, tile_rows)))
    return result.reshape(SEQ, H * HDIM)

def cross_attention(queries, key_rows, value_rows):
    tile_rows = min(512, SEQ)
    tile_total = SEQ // tile_rows
    key_heads = key_rows.reshape(ENC, H, HDIM)
    value_heads = value_rows.reshape(ENC, H, HDIM)
    allowed = jnp.ones((tile_rows, ENC), jnp.bool_)

    def query_tile(tile_query):
        return attend(tile_query, key_heads, value_heads, allowed)
    result = lax.map(jax.checkpoint(query_tile), queries.reshape(tile_total, tile_rows, H, HDIM))
    return result.reshape(SEQ, H * HDIM)

def sequence_layer(resid_zero, encoded, block_of, self_qkv, self_out, cross_qkv, cross_out, up_weight, down_weight, proj_bias, up_bias, norm_gain, norm_shift):
    model_width = H * HDIM
    self_flat = self_qkv.reshape(model_width, 3 * model_width)
    cross_flat = cross_qkv.reshape(model_width, 3 * model_width)
    h_one = low(layer_norm(resid_zero, norm_gain[:, 0], norm_shift[:, 0]))
    projected = matmul(h_one, self_flat)
    queries = low_back(low((projected[:, :model_width] + proj_bias[:, 0]) * 0.125))
    key_rows = low_back(low(projected[:, model_width:2 * model_width]))
    value_rows = low_back(low(projected[:, 2 * model_width:] + proj_bias[:, 1]))
    context = low_back(low(self_attention(queries, key_rows, value_rows, block_of)))
    resid_one = resid_zero + low_back(matmul(context, self_out) + proj_bias[:, 2])
    h_two = low(layer_norm(resid_one, norm_gain[:, 1], norm_shift[:, 1]))
    query_two = low_back(low((matmul(h_two, cross_flat[:, :model_width]) + proj_bias[:, 3]) * 0.125))
    kv_two = matmul(encoded, cross_flat[:, model_width:])
    keys_two = low_back(low(kv_two[:, :model_width]))
    values_two = low_back(low(kv_two[:, model_width:] + proj_bias[:, 4]))
    context_two = low_back(low(cross_attention(query_two, keys_two, values_two)))
    resid_two = resid_one + low_back(matmul(context_two, cross_out) + proj_bias[:, 5])
    h_three = low(layer_norm(resid_two, norm_gain[:, 2], norm_shift[:, 2]))
    inner_pre = low_back(matmul(h_three, up_weight) + up_bias)
    act_low = low(jax.nn.gelu(inner_pre, approximate=False))
    mlp_out = low_back(matmul(act_low, down_weight) + proj_bias[:, 6])
    return resid_two + mlp_out

def reference(hidden, encoder, cotangent, block_ids, self_qkv, self_out, cross_qkv, cross_out, up_weight, down_weight, proj_bias, up_bias, norm_gain, norm_shift):
    params = tuple((weight.astype(jnp.float32) for weight in (self_qkv, self_out, cross_qkv, cross_out, up_weight, down_weight, proj_bias, up_bias, norm_gain, norm_shift)))
    seq_hidden = hidden.astype(jnp.float32).reshape(NSEQ, SEQ, D)
    seq_cot = cotangent.astype(jnp.float32).reshape(NSEQ, SEQ, D)
    seq_ids = block_ids.reshape(NSEQ, SEQ)
    encoded_all = encoder.astype(jnp.float32)

    def scan_step(totals, inputs):
        resid_zero, encoded, block_of, cot_rows = inputs

        def forward(resid_in, encoded_in, *weights):
            return sequence_layer(resid_in, encoded_in, block_of, *weights)
        result, pullback = jax.vjp(forward, resid_zero, encoded, *params)
        gradients = pullback(cot_rows)
        totals = tuple((running + grad_item for running, grad_item in zip(totals, gradients[2:])))
        return (totals, (result, gradients[0], gradients[1]))
    start_totals = tuple((jnp.zeros_like(weight) for weight in params))
    totals, (outputs, grad_rows, grad_enc) = lax.scan(scan_step, start_totals, (seq_hidden, encoded_all, seq_ids, seq_cot))
    return (outputs.reshape(TOKENS, D).astype(jnp.bfloat16), grad_rows.reshape(TOKENS, D), grad_enc, totals[0], totals[1], totals[2], totals[3], totals[4], totals[5], totals[6], totals[7], totals[8], totals[9])
```

```python
import functools

import jax
import jax.numpy as jnp
from jax import lax
from jax.experimental import pallas as pl
from jax.experimental.pallas import tpu as pltpu
from jax.sharding import PartitionSpec as P

HDIM = 64
SEQ = 8192
TILE = 512
norm_eps = 1e-05
neg_large = -1e30
f32 = jnp.float32
bf16 = jnp.bfloat16


def dot(left, right, left_dim, right_dim):
    return lax.dot_general(
        left, right, (((left_dim,), (right_dim,)), ((), ())), preferred_element_type=f32
    )


def swap(value, axis, mask):
    return lax.ppermute(value, axis, [(i, i ^ mask) for i in range(lax.axis_size(axis))])


def hd_masks():
    mask, masks = lax.axis_size("hd") // 2, []
    while mask:
        masks.append(mask)
        mask //= 2
    return masks


def gather_xor(value):
    have = {0: value}
    for mask in hd_masks():
        for index in list(have):
            have[index ^ mask] = swap(have[index], "hd", mask)
    return [have[index] for index in range(len(have))]


def reduce_xor(parts):
    have = dict(enumerate(parts))
    for mask in reversed(hd_masks()):
        for index in sorted(have, reverse=True):
            if index & mask:
                got = swap(have.pop(index).astype(bf16), "hd", mask)
                have[index ^ mask] = have[index ^ mask] + got.astype(f32)
    return have[0]


def exchange_xor(parts):
    have = {index: {0: part} for index, part in enumerate(parts)}
    for mask in hd_masks():
        gone = [index for index in have if index & mask]
        keys = [(index, source) for index in gone for source in have[index]]
        got = swap(jnp.stack([have[index][source] for index, source in keys]), "hd", mask)
        for slot, (index, source) in enumerate(keys):
            have[index ^ mask][source ^ mask] = got[slot]
        for index in gone:
            del have[index]
    return [have[0][index] for index in range(len(parts))]


def pick(stacked, index):
    return lax.dynamic_index_in_dim(stacked, index, 0, keepdims=False)


def normalize(value):
    center = value - jnp.mean(value, axis=-1, keepdims=True)
    inverse = lax.rsqrt(jnp.mean(center * center, axis=-1, keepdims=True) + norm_eps)
    return center * inverse, inverse


def norm_backward(grad, unit, inverse, gain):
    scaled = grad * gain
    back = (
        scaled
        - jnp.mean(scaled, axis=-1, keepdims=True)
        - unit * jnp.mean(scaled * unit, axis=-1, keepdims=True)
    ) * inverse
    return back, jnp.sum(grad * unit, axis=0), jnp.sum(grad, axis=0)


def column(row, rows):
    return jnp.swapaxes(jnp.broadcast_to(row, (128, rows)), 0, 1)[:, :1]


VMEM = pl.BlockSpec(memory_space=pltpu.VMEM)
LIMIT = 48 * 2**20


def self_forward_kernel(heads, others, info, *refs):
    refs = list(refs)
    q_refs = [refs.pop(0) for _ in range(heads)]
    kv_refs = [[refs.pop(0) for _ in range(heads)] for _ in range(others)]
    id_refs = [refs.pop(0) for _ in range(heads)]
    o_ref, l_ref, q_all, k_all, v_all, id_all = refs
    piece_rows = q_all.shape[2]
    per = piece_rows // TILE
    step = pl.program_id(0)
    at, beside = info[0], info[1]

    @pl.when(step == 0)
    def _():
        for slot in range(heads):
            q_all[slot] = q_refs[slot][...]
            id_all[slot] = id_refs[slot][...]
            for other in range(others):
                k_all[other, slot] = jnp.swapaxes(kv_refs[other][slot][0], 0, 1)
                v_all[other, slot] = kv_refs[other][slot][1]

    slot = step // per
    tile = lax.rem(step, per)
    piece = jnp.bitwise_xor(slot, at) * others + beside
    cols = pl.ds(pl.multiple_of(tile * TILE, TILE), TILE)
    q = q_all[slot, :, cols]

    def update(state, k, v, mask):
        top, total, acc = state
        scores = dot(k, q, 1, 0)
        if mask is not None:
            scores = jnp.where(mask, scores, neg_large)
        new_top = jnp.maximum(top, jnp.max(scores, axis=0, keepdims=True))
        probs = jnp.exp(scores - new_top)
        fade = jnp.exp(top - new_top)
        total = total * fade + jnp.sum(probs, axis=0, keepdims=True)
        acc = acc * fade + dot(v, probs.astype(bf16), 1, 0)
        return new_top, total, acc

    def earlier_piece(index, state):
        place = jnp.bitwise_xor(index // others, at)
        other = jnp.bitwise_xor(lax.rem(index, others), beside)
        return update(state, k_all[other, place], v_all[other, place], None)

    def earlier_tile(index, state):
        rows = pl.ds(pl.multiple_of(index * TILE, TILE), TILE)
        return update(state, k_all[0, slot, rows, :], v_all[0, slot, :, rows], None)

    state = (
        jnp.full((1, TILE), neg_large, f32),
        jnp.zeros((1, TILE), f32),
        jnp.zeros((HDIM, TILE), f32),
    )
    state = lax.fori_loop(0, piece, earlier_piece, state)
    state = lax.fori_loop(0, tile, earlier_tile, state)
    ids = id_all[slot, :, cols].astype(f32)
    mask = column(ids, TILE) <= ids
    top, total, acc = update(state, k_all[0, slot, cols, :], v_all[0, slot, :, cols], mask)
    o_ref[slot, :, cols] = (acc / total).astype(o_ref.dtype)
    l_ref[slot, :, cols] = top + jnp.log(total)


def self_forward(info, q, kv, ids):
    heads, others = len(q), len(kv)
    depth, rows = q[0].shape
    flat = list(q) + [block for line in kv for block in line] + list(ids)
    area = heads * rows * heads * others * rows // 2
    return pl.pallas_call(
        functools.partial(self_forward_kernel, heads, others),
        grid_spec=pltpu.PrefetchScalarGridSpec(
            num_scalar_prefetch=1,
            grid=(heads * rows // TILE,),
            in_specs=[VMEM] * len(flat),
            out_specs=[VMEM] * 2,
            scratch_shapes=[
                pltpu.VMEM((heads, depth, rows), bf16),
                pltpu.VMEM((others, heads, rows, depth), bf16),
                pltpu.VMEM((others, heads, depth, rows), bf16),
                pltpu.VMEM((heads, 1, rows), jnp.int32),
            ],
        ),
        out_shape=[
            jax.ShapeDtypeStruct((heads, depth, rows), bf16),
            jax.ShapeDtypeStruct((heads, 1, rows), f32),
        ],
        compiler_params=pltpu.CompilerParams(vmem_limit_bytes=LIMIT),
        cost_estimate=pl.CostEstimate(
            flops=area * 1024, bytes_accessed=8 * 2**20, transcendentals=area
        ),
        name="self_forward",
    )(info, *flat)


def self_backward_kernel(heads, others, info, *refs):
    refs = list(refs)
    q_refs = [refs.pop(0) for _ in range(heads)]
    kv_refs = [[refs.pop(0) for _ in range(heads)] for _ in range(others)]
    id_refs = [refs.pop(0) for _ in range(heads)]
    g_refs = [refs.pop(0) for _ in range(heads)]
    o_ref, l_ref, dq_ref, dkv_ref, q_all, g_all, id_all, kt_all, k_all, v_all, dk, dv = refs
    piece_rows = q_all.shape[2]
    per = piece_rows // TILE
    step = pl.program_id(0)
    at, beside = info[0], info[1]

    @pl.when(step == 0)
    def _():
        for slot in range(heads):
            q_all[slot] = q_refs[slot][...]
            g_all[slot] = g_refs[slot][...]
            id_all[slot] = id_refs[slot][...]
            for other in range(others):
                kt_all[other, slot] = kv_refs[other][slot][0]
                k_all[other, slot] = jnp.swapaxes(kv_refs[other][slot][0], 0, 1)
                v_all[other, slot] = jnp.swapaxes(kv_refs[other][slot][1], 0, 1)
        dk[...] = jnp.zeros_like(dk)
        dv[...] = jnp.zeros_like(dv)

    slot = step // per
    tile = lax.rem(step, per)
    piece = jnp.bitwise_xor(slot, at) * others + beside
    cols = pl.ds(pl.multiple_of(tile * TILE, TILE), TILE)
    q = q_all[slot, :, cols]
    grad = g_all[slot, :, cols]
    q_rows = jnp.swapaxes(q, 0, 1)
    grad_rows = jnp.swapaxes(grad, 0, 1)
    log_total = l_ref[slot, :, cols]
    inner = jnp.sum(o_ref[slot, :, cols].astype(f32) * grad.astype(f32), axis=0, keepdims=True)

    def update(dq, other, place, rows, mask):
        scores = dot(k_all[other, place, rows, :], q, 1, 0)
        if mask is not None:
            scores = jnp.where(mask, scores, neg_large)
        probs = jnp.exp(scores - log_total)
        grad_probs = dot(v_all[other, place, rows, :], grad, 1, 0)
        grad_scores = (probs * (grad_probs - inner)).astype(bf16)
        dv[other, place, rows, :] += dot(probs.astype(bf16), grad_rows, 1, 0)
        dk[other, place, rows, :] += dot(grad_scores, q_rows, 1, 0)
        return dq + dot(kt_all[other, place, :, rows], grad_scores, 1, 0)

    def earlier(index, dq):
        other_piece = index // per
        rows = pl.ds(pl.multiple_of(lax.rem(index, per) * TILE, TILE), TILE)
        place = jnp.bitwise_xor(other_piece // others, at)
        other = jnp.bitwise_xor(lax.rem(other_piece, others), beside)
        return update(dq, other, place, rows, None)

    dq = lax.fori_loop(0, piece * per + tile, earlier, jnp.zeros((HDIM, TILE), f32))
    ids = id_all[slot, :, cols].astype(f32)
    mask = column(ids, TILE) <= ids
    dq = update(dq, 0, slot, cols, mask)
    dq_ref[slot, :, cols] = (dq * 0.125).astype(dq_ref.dtype)

    @pl.when(step == heads * per - 1)
    def _():
        for other in range(others):
            for place in range(heads):
                dkv_ref[other, place, 0] = jnp.swapaxes(dk[other, place], 0, 1).astype(dkv_ref.dtype)
                dkv_ref[other, place, 1] = jnp.swapaxes(dv[other, place], 0, 1).astype(dkv_ref.dtype)


def self_backward(info, q, kv, ids, grad, context, log_total):
    heads, others = len(q), len(kv)
    depth, rows = q[0].shape
    flat = list(q) + [block for line in kv for block in line] + list(ids) + list(grad)
    flat += [context, log_total]
    area = heads * rows * heads * others * rows // 2
    return pl.pallas_call(
        functools.partial(self_backward_kernel, heads, others),
        grid_spec=pltpu.PrefetchScalarGridSpec(
            num_scalar_prefetch=1,
            grid=(heads * rows // TILE,),
            in_specs=[VMEM] * len(flat),
            out_specs=[VMEM] * 2,
            scratch_shapes=[
                pltpu.VMEM((heads, depth, rows), bf16),
                pltpu.VMEM((heads, depth, rows), bf16),
                pltpu.VMEM((heads, 1, rows), jnp.int32),
                pltpu.VMEM((others, heads, depth, rows), bf16),
                pltpu.VMEM((others, heads, rows, depth), bf16),
                pltpu.VMEM((others, heads, rows, depth), bf16),
                pltpu.VMEM((others, heads, rows, depth), f32),
                pltpu.VMEM((others, heads, rows, depth), f32),
            ],
        ),
        out_shape=[
            jax.ShapeDtypeStruct((heads, depth, rows), bf16),
            jax.ShapeDtypeStruct((others, heads, 2, depth, rows), bf16),
        ],
        compiler_params=pltpu.CompilerParams(vmem_limit_bytes=LIMIT),
        cost_estimate=pl.CostEstimate(
            flops=area * 2560, bytes_accessed=12 * 2**20, transcendentals=area
        ),
        name="self_backward",
    )(info, *flat)


def cross_forward_kernel(q_ref, kv_ref, o_ref, l_ref):
    def head(index, _):
        rows = pl.ds(pl.multiple_of(index * HDIM, HDIM), HDIM)
        scores = dot(jnp.swapaxes(kv_ref[0, rows, :], 0, 1), q_ref[rows, :], 1, 0)
        top = jnp.max(scores, axis=0, keepdims=True)
        probs = jnp.exp(scores - top)
        total = jnp.sum(probs, axis=0, keepdims=True)
        probs = (probs / total).astype(bf16)
        o_ref[rows, :] = dot(kv_ref[1, rows, :], probs, 1, 0).astype(bf16)
        l_ref[index] = top + jnp.log(total)
        return 0

    lax.fori_loop(0, q_ref.shape[0] // HDIM, head, 0)


def cross_forward(q, kv):
    width, rows = q.shape
    return pl.pallas_call(
        cross_forward_kernel,
        in_specs=[VMEM] * 2,
        out_specs=[VMEM] * 2,
        out_shape=[
            jax.ShapeDtypeStruct((width, rows), bf16),
            jax.ShapeDtypeStruct((width // HDIM, 1, rows), f32),
        ],
        compiler_params=pltpu.CompilerParams(vmem_limit_bytes=LIMIT),
        name="cross_forward",
    )(q, kv)


def cross_backward_kernel(q_ref, kv_ref, g_ref, o_ref, l_ref, dq_ref, dkv_ref):
    def head(index, _):
        rows = pl.ds(pl.multiple_of(index * HDIM, HDIM), HDIM)
        q, grad = q_ref[rows, :], g_ref[rows, :]
        inner = jnp.sum(o_ref[rows, :].astype(f32) * grad.astype(f32), axis=0, keepdims=True)
        k_t = kv_ref[0, rows, :]
        scores = dot(jnp.swapaxes(k_t, 0, 1), q, 1, 0)
        probs = jnp.exp(scores - l_ref[index])
        grad_probs = dot(jnp.swapaxes(kv_ref[1, rows, :], 0, 1), grad, 1, 0)
        grad_scores = (probs * (grad_probs - inner)).astype(bf16)
        dq_ref[rows, :] = (dot(k_t, grad_scores, 1, 0) * 0.125).astype(bf16)
        dkv_ref[0, rows, :] = dot(q, grad_scores, 1, 1)
        dkv_ref[1, rows, :] = dot(grad, probs.astype(bf16), 1, 1)
        return 0

    lax.fori_loop(0, q_ref.shape[0] // HDIM, head, 0)


def cross_backward(q, kv, grad, context, log_total):
    width, rows = q.shape
    return pl.pallas_call(
        cross_backward_kernel,
        in_specs=[VMEM] * 5,
        out_specs=[VMEM] * 2,
        out_shape=[jax.ShapeDtypeStruct((width, rows), bf16), jax.ShapeDtypeStruct(kv.shape, f32)],
        compiler_params=pltpu.CompilerParams(vmem_limit_bytes=LIMIT),
        name="cross_backward",
    )(q, kv, grad, context, log_total)


def gelu_parts(value):
    half = 0.5 * (1.0 + lax.erf(value * 0.7071067811865476))
    slope = half + value * jnp.exp(-0.5 * value * value) * 0.3989422804014327
    return value * half, slope


def local(
    hidden,
    encoder,
    cotangent,
    block_ids,
    self_qkv,
    self_out,
    cross_qkv,
    cross_out,
    up_weight,
    down_weight,
    proj_bias,
    up_bias,
    norm_gain,
    norm_shift,
):
    tok_size, group = lax.axis_size("tok"), lax.axis_size("hd")
    tok_index, me = lax.axis_index("tok"), lax.axis_index("hd")
    rows, model = hidden.shape
    shard = self_qkv.shape[0]
    width = self_qkv.shape[2]
    ff_local = up_weight.shape[1]
    piece_rows = rows * group
    span = SEQ // piece_rows
    heads = min(width // HDIM, span)
    others = span // heads
    assert heads * HDIM == width and heads * others == span
    seq_count, enc_rows, _ = encoder.shape
    enc_total = enc_rows * group
    own_seq = tok_index // span
    at = lax.rem(tok_index, span) // others
    beside = lax.rem(tok_index, others)
    info = jnp.stack([at, beside]).astype(jnp.int32)

    def natural(blocks):
        stacked = jnp.stack(blocks)
        return [pick(stacked, me ^ index) for index in range(group)]

    def gather_tok(block):
        return lax.all_gather(block, "tok", axis=0, tiled=True)

    w_self = gather_tok(self_qkv.reshape(shard, 3 * width))
    small = jnp.concatenate(
        [proj_bias.T.reshape(-1), norm_gain.T.reshape(-1), norm_shift.T.reshape(-1), up_bias]
    )
    total_devices = tok_size * group
    small_all = lax.all_to_all(
        jnp.broadcast_to(small[None], (total_devices, small.shape[0])),
        ("tok", "hd"), 0, 0, tiled=True,
    ).astype(f32)
    few = model // total_devices
    vectors = small_all[:, : 13 * few].reshape(total_devices, 13, few)
    vectors = vectors.transpose(1, 0, 2).reshape(13, model)
    bias, gain, shift = vectors[:7], vectors[7:10], vectors[10:13]
    bias_up = lax.dynamic_slice_in_dim(small_all[:, 13 * few :].reshape(-1), me * ff_local, ff_local)

    def own_columns(vector):
        return lax.dynamic_slice_in_dim(vector, me * width, width)

    def xor_columns(vector):
        return jnp.concatenate(
            [lax.dynamic_slice_in_dim(vector, (me ^ j) * width, width) for j in range(group)]
        )

    hidden_blocks = gather_xor(hidden)
    ids = [block_ids.reshape(1, piece_rows)]
    ids += [swap(ids[0], "tok", step * others) for step in range(1, heads)]

    w_mid = gather_tok(jnp.concatenate([self_out.T, cross_out.T, cross_qkv.reshape(shard, 3 * width)], 1))
    w_up = gather_tok(up_weight)
    w_down = gather_tok(down_weight.T)

    hidden_all = jnp.concatenate(hidden_blocks, 0).astype(f32)
    h_one = (normalize(hidden_all)[0] * gain[0] + shift[0]).astype(bf16)
    self_bias = jnp.concatenate(
        [own_columns(bias[0]), jnp.zeros((width,), f32), own_columns(bias[1])]
    )
    scale = jnp.concatenate([jnp.full((width,), 0.125, f32), jnp.ones((2 * width,), f32)])
    qkv = (dot(w_self, h_one, 0, 1) + self_bias[:, None]) * scale[:, None]
    qkv = qkv.astype(bf16).reshape(3, heads, HDIM, group, rows)

    def head_message(first, count, step):
        return jnp.concatenate(
            [
                lax.dynamic_slice(
                    qkv, (first, at ^ step, 0, me ^ j, 0), (count, 1, HDIM, 1, rows)
                ).reshape(count, HDIM, rows)
                for j in range(group)
            ],
            -1,
        )

    kv = [[head_message(1, 2, 0)]]
    q = [head_message(0, 1, 0)[0]]
    for step in range(1, heads):
        kv[0].append(swap(head_message(1, 2, step), "tok", step * others))
    for other in range(1, others):
        kv.append([swap(block, "tok", other) for block in kv[0]])
    for step in range(1, heads):
        q.append(swap(head_message(0, 1, step)[0], "tok", step * others))
    context, log_one = self_forward(info, q, kv, ids)

    def to_tokens(stacked):
        got = [stacked[0]] + [
            swap(stacked[step], "tok", step * others) for step in range(1, heads)
        ]
        got = jnp.stack(got)
        ordered = jnp.concatenate([pick(got, at ^ index) for index in range(heads)], 0)
        parts = [
            lax.dynamic_slice(ordered, (0, (me ^ j) * rows), (width, rows)) for j in range(group)
        ]
        return jnp.concatenate(exchange_xor(parts), 0)

    def to_heads(value):
        got = exchange_xor([value[j * width : (j + 1) * width] for j in range(group)])
        ordered = jnp.concatenate(natural(got), 1).reshape(heads, HDIM, piece_rows)
        return [pick(ordered, at)] + [
            swap(pick(ordered, at ^ step), "tok", step * others) for step in range(1, heads)
        ]

    out_blocks = gather_xor(
        jnp.stack([w_mid[:, :width], w_mid[:, width : 2 * width], w_mid[:, 2 * width : 3 * width]])
    )
    out_all = jnp.concatenate(out_blocks, 2)
    w_self_out, w_cross_out, w_cross_q = out_all[0], out_all[1], out_all[2]
    w_cross_kv = w_mid[:, 3 * width :]
    enc_all = jnp.concatenate(natural(gather_xor(encoder)), 1)
    kv_bias = jnp.concatenate([jnp.zeros((width,), f32), own_columns(bias[4])])
    kv_two = dot(w_cross_kv, pick(enc_all, own_seq), 0, 1) + kv_bias[:, None]
    kv_two = kv_two.astype(bf16).reshape(2, width, enc_total)
    kv_two = jnp.concatenate(gather_xor(kv_two), 1)

    ctx_one = to_tokens(context)
    resid_zero = hidden.astype(f32)
    resid_one = resid_zero + dot(ctx_one, w_self_out, 0, 1) + bias[2]
    unit_two, inverse_two = normalize(resid_one)
    h_two = (unit_two * gain[1] + shift[1]).astype(bf16)
    q_two = dot(w_cross_q, h_two, 0, 1) + xor_columns(bias[3])[:, None]
    q_two = (q_two * 0.125).astype(bf16)
    ctx_two, log_two = cross_forward(q_two, kv_two)
    resid_two = resid_one + dot(ctx_two, w_cross_out, 0, 1) + bias[5]
    unit_three, inverse_three = normalize(resid_two)
    h_three = (unit_three * gain[2] + shift[2]).astype(bf16)

    cot_all = jnp.concatenate(gather_xor(cotangent), 0)
    grad_act = dot(cot_all, w_down, 1, 0)
    h_three_all = jnp.concatenate(gather_xor(h_three), 0)
    inner_pre = dot(h_three_all, w_up, 1, 0) + bias_up
    act, slope = gelu_parts(inner_pre)
    act = act.astype(bf16)
    grad_inner = (slope * grad_act).astype(bf16)

    def block(array, index):
        return array[index * rows : (index + 1) * rows]

    grad_h_three = reduce_xor([dot(block(grad_inner, j), w_up, 1, 1) for j in range(group)])
    cot = cotangent.astype(f32)
    back, gain_three, shift_three = norm_backward(grad_h_three, unit_three, inverse_three, gain[2])
    grad_two = cot + back
    grad_two_low = grad_two.astype(bf16)
    final = reduce_xor([dot(block(act, j), w_down, 1, 1) for j in range(group)])
    output = (resid_two + final + bias[6]).astype(bf16)
    grad_up = dot(h_three_all, grad_inner, 0, 0).astype(bf16)
    grad_down = dot(cot_all, act, 0, 0).astype(bf16)

    def reduce_tok(value):
        return lax.psum_scatter(value, "tok", scatter_dimension=0, tiled=True).astype(f32)

    sent_up = reduce_tok(grad_up)
    sent_down = reduce_tok(grad_down).T

    grad_ctx_two = dot(w_cross_out, grad_two_low, 0, 1).astype(bf16)
    grad_q_two, grad_kv_two = cross_backward(q_two, kv_two, grad_ctx_two, ctx_two, log_two)
    grad_h_two = dot(grad_q_two, w_cross_q, 0, 1)
    back, gain_two, shift_two = norm_backward(grad_h_two, unit_two, inverse_two, gain[1])
    grad_one = grad_two + back
    grad_one_low = grad_one.astype(bf16)
    grad_ctx_one = dot(w_self_out, grad_one_low, 0, 1).astype(bf16)
    grad_heads = to_heads(grad_ctx_one)

    grad_mid = [
        dot(grad_one_low, ctx_one, 0, 1),
        dot(grad_two_low, ctx_two, 0, 1),
        dot(h_two, grad_q_two, 0, 1),
    ]
    grad_mid = reduce_xor(
        [
            jnp.concatenate([g[:, j * width : (j + 1) * width] for g in grad_mid], 1)
            for j in range(group)
        ]
    )
    sent_mid = reduce_tok(grad_mid.astype(bf16))
    kv_total = reduce_xor([grad_kv_two[:, j * width : (j + 1) * width] for j in range(group)])
    seq_pick = jnp.arange(seq_count) == own_seq
    kv_total = jnp.where(seq_pick[:, None, None, None], kv_total[None], 0.0).astype(bf16)
    mask = 1
    while mask < tok_size:
        kv_total = (kv_total.astype(f32) + swap(kv_total, "tok", mask).astype(f32)).astype(bf16)
        mask *= 2
    kv_flat = kv_total.reshape(seq_count, 2 * width, enc_total)
    own_enc = lax.dynamic_slice_in_dim(enc_all, tok_index * shard, shard, 2)
    sent_cross_kv = sum(dot(own_enc[n], kv_flat[n], 0, 1) for n in range(seq_count))

    def encoder_part(index):
        start = (me ^ index) * enc_rows
        return jnp.stack(
            [
                dot(lax.dynamic_slice_in_dim(kv_flat[n], start, enc_rows, 1), w_cross_kv, 0, 1)
                for n in range(seq_count)
            ]
        )

    grad_encoder = reduce_xor([encoder_part(j) for j in range(group)])

    grad_q, grad_kv = self_backward(info, q, kv, ids, grad_heads, context, log_one)
    messages = []
    for step in range(heads):
        total = grad_kv[0, step].astype(f32)
        for other in range(1, others):
            total = total + swap(grad_kv[other, step], "tok", other).astype(f32)
        message = jnp.concatenate([grad_q[step][None], total.astype(bf16)], 0)
        messages.append(swap(message, "tok", step * others) if step else message)
    messages = jnp.stack(messages)
    grad_qkv = jnp.stack([pick(messages, at ^ index) for index in range(heads)], 1)
    grad_qkv = grad_qkv.reshape(3 * width, piece_rows)
    grad_qkv = [
        lax.dynamic_slice(grad_qkv, (0, (me ^ j) * rows), (3 * width, rows)) for j in range(group)
    ]
    grad_h_one = reduce_xor([dot(grad_qkv[j], w_self, 0, 1) for j in range(group)])
    grad_qkv = jnp.concatenate(grad_qkv, 1)
    grad_self = dot(h_one, grad_qkv, 0, 1).astype(bf16)
    sent_self = reduce_tok(grad_self).reshape(shard, 3, width)
    unit_one, inverse_one = normalize(resid_zero)
    back, gain_one, shift_one = norm_backward(grad_h_one, unit_one, inverse_one, gain[0])
    grad_hidden = grad_one + back

    def place(vector):
        return lax.dynamic_update_slice_in_dim(jnp.zeros((model,), f32), vector, me * width, 0)

    def unxor(vector):
        return jnp.concatenate(natural([vector[j * width : (j + 1) * width] for j in range(group)]))

    qkv_sums = jnp.sum(grad_qkv.astype(f32), 1)
    once = (tok_index == 0).astype(f32)
    vectors = jnp.stack(
        [
            place(qkv_sums[:width]),
            place(qkv_sums[2 * width :]),
            jnp.sum(grad_one_low.astype(f32), 0),
            unxor(jnp.sum(grad_q_two.astype(f32), 1)),
            place(jnp.sum(kv_flat[:, width:].astype(f32), (0, 2)) * once),
            jnp.sum(grad_two_low.astype(f32), 0),
            jnp.sum(cot, 0),
            gain_one,
            gain_two,
            gain_three,
            shift_one,
            shift_two,
            shift_three,
        ]
    )
    vectors = vectors.reshape(13, total_devices, few).transpose(1, 0, 2).reshape(total_devices, -1)
    up_sums = lax.dynamic_update_slice_in_dim(
        jnp.zeros((group * ff_local,), f32), jnp.sum(grad_inner.astype(f32), 0), me * ff_local, 0
    )
    vectors = jnp.concatenate([vectors, up_sums.reshape(total_devices, -1)], 1)
    vectors = jnp.sum(lax.all_to_all(vectors, ("tok", "hd"), 0, 0, tiled=True), 0)
    columns = vectors[: 13 * few].reshape(13, few).T

    sent_mid = [sent_mid[:, j * width : (j + 1) * width] for j in range(3)]
    sent_cross = jnp.concatenate(
        [sent_mid[2][:, None], sent_cross_kv.reshape(shard, 2, width)], 1
    )
    return (
        output,
        grad_hidden,
        grad_encoder,
        sent_self,
        sent_mid[0].T,
        sent_cross,
        sent_mid[1].T,
        sent_up,
        sent_down,
        columns[:, :7],
        vectors[13 * few :],
        columns[:, 7:10],
        columns[:, 10:13],
    )


def solution(mesh):
    in_specs = (
        P(("tok", "hd"), None),
        P(None, "hd", None),
        P(("tok", "hd"), None),
        P("tok"),
        P("tok", None, "hd"),
        P("hd", "tok"),
        P("tok", None, "hd"),
        P("hd", "tok"),
        P("tok", "hd"),
        P("hd", "tok"),
        P(("tok", "hd"), None),
        P(("tok", "hd")),
        P(("tok", "hd"), None),
        P(("tok", "hd"), None),
    )
    out_specs = (
        P(("tok", "hd"), None),
        P(("tok", "hd"), None),
        P(None, "hd", None),
        P("tok", None, "hd"),
        P("hd", "tok"),
        P("tok", None, "hd"),
        P("hd", "tok"),
        P("tok", "hd"),
        P("hd", "tok"),
        P(("tok", "hd"), None),
        P(("tok", "hd")),
        P(("tok", "hd"), None),
        P(("tok", "hd"), None),
    )
    return jax.shard_map(local, mesh=mesh, in_specs=in_specs, out_specs=out_specs, check_vma=False)
```

```python
import functools

import jax
import jax.numpy as jnp
from jax import lax
from jax.experimental import pallas as pl
from jax.experimental.pallas import tpu as pltpu
from jax.sharding import PartitionSpec as P

HDIM = 64
SEQ = 8192
TILE = 512
norm_eps = 1e-05
neg_large = -1e30
f32 = jnp.float32
bf16 = jnp.bfloat16


def dot(left, right, left_dim, right_dim):
    return lax.dot_general(
        left, right, (((left_dim,), (right_dim,)), ((), ())), preferred_element_type=f32
    )


def swap(value, axis, mask):
    return lax.ppermute(value, axis, [(i, i ^ mask) for i in range(lax.axis_size(axis))])


def hd_masks():
    mask, masks = lax.axis_size("hd") // 2, []
    while mask:
        masks.append(mask)
        mask //= 2
    return masks


def gather_xor(value, first=lambda value: value):
    have = {0: value}
    for mask in hd_masks():
        for index in list(have):
            have[index ^ mask] = first(swap(have[index], "hd", mask))
        first = lambda value: value
    return [have[index] for index in range(len(have))]


def reduce_xor(parts, last=lambda value: value):
    have = dict(enumerate(parts))
    for mask in reversed(hd_masks()):
        for index in sorted(have, reverse=True):
            if index & mask:
                got = swap(have.pop(index).astype(bf16), "hd", mask)
                if len(have) == 1:
                    got = last(got)
                have[index ^ mask] = have[index ^ mask].astype(f32) + got.astype(f32)
    return have[0]


def pick(stacked, index):
    return lax.dynamic_index_in_dim(stacked, index, 0, keepdims=False)


def normalize(value):
    center = value - jnp.mean(value, axis=-1, keepdims=True)
    inverse = lax.rsqrt(jnp.mean(center * center, axis=-1, keepdims=True) + norm_eps)
    return center * inverse, inverse


def norm_backward(grad, unit, inverse, gain):
    scaled = grad * gain
    back = (
        scaled
        - jnp.mean(scaled, axis=-1, keepdims=True)
        - unit * jnp.mean(scaled * unit, axis=-1, keepdims=True)
    ) * inverse
    return back, jnp.sum(grad * unit, axis=0), jnp.sum(grad, axis=0)


def column(row, rows):
    return jnp.swapaxes(jnp.broadcast_to(row, (128, rows)), 0, 1)[:, :1]


VMEM = pl.BlockSpec(memory_space=pltpu.VMEM)
LIMIT = 48 * 2**20


ANY = pl.BlockSpec(memory_space=pl.ANY)


def tie(values, after):
    count = len(values)
    return pl.pallas_call(
        lambda *refs: None,
        in_specs=[ANY] * (count + len(after)),
        out_specs=[ANY] * count,
        out_shape=[jax.ShapeDtypeStruct(value.shape, value.dtype) for value in values],
        input_output_aliases={index: index for index in range(count)},
        name="tie",
    )(*values, *after)


def project_kernel(heads, group, info, *refs):
    refs = list(refs)
    w_ref, norm_ref, bias_ref = refs[:3]
    q_ref, k_ref, v_ref, h_ref = refs[-4:]
    x_refs = refs[3 : 3 + group]
    rows = x_refs[0].shape[0]
    for step, x_ref in enumerate(x_refs):
        start = pl.multiple_of(jnp.bitwise_xor(info[2], step) * rows, rows)
        cols = pl.ds(start, rows)
        x = x_ref[...].astype(f32)
        h = (normalize(x)[0] * norm_ref[0:1, :] + norm_ref[1:2, :]).astype(bf16)
        h_ref[cols, :] = h
        out = (dot(h, w_ref[...], 1, 0) + bias_ref[0:1, :]) * bias_ref[1:2, :]
        out = jnp.swapaxes(out.astype(bf16), 0, 1)
        for head in range(heads):
            for part, ref in enumerate((q_ref, k_ref, v_ref)):
                first = (head * 3 + part) * HDIM
                ref[head, :, cols] = out[first : first + HDIM]


def project(info, x, w, norm, bias, heads, after):
    rows, model = x[0].shape
    group = len(x)
    piece = rows * group
    width = w.shape[1]
    return pl.pallas_call(
        functools.partial(project_kernel, heads, group),
        grid_spec=pltpu.PrefetchScalarGridSpec(
            num_scalar_prefetch=1,
            grid=(1,),
            in_specs=[VMEM] * (group + 3) + [ANY] * len(after),
            out_specs=[VMEM] * 4,
        ),
        out_shape=[jax.ShapeDtypeStruct((heads, HDIM, piece), bf16)] * 3
        + [jax.ShapeDtypeStruct((piece, model), bf16)],
        compiler_params=pltpu.CompilerParams(vmem_limit_bytes=LIMIT),
        cost_estimate=pl.CostEstimate(
            flops=2 * piece * model * width, bytes_accessed=8 * 2**20, transcendentals=piece
        ),
        name="project",
    )(info, w, norm, bias, *x, *after)


def flip(place, others):
    return lax.rem(place, 2) * (others - 1)


def self_forward_kernel(heads, others, info, *refs):
    q_ref, id_ref = refs[:2]
    k_refs, v_refs = refs[2 : 2 + others], refs[2 + others : 2 + 2 * others]
    o_ref, l_ref, k_all, v_all = refs[-4:]
    beside = info[1]
    step = pl.program_id(0)
    piece_rows = q_ref.shape[2]
    per = piece_rows // TILE
    slot, tile = step // per, lax.rem(step, per)

    @pl.when(step == 0)
    def _():
        for other in range(others):
            for place in range(heads):
                k_all[other, place] = jnp.swapaxes(k_refs[other][place], 0, 1)
                v_all[other, place] = v_refs[other][place]

    piece = slot * others + jnp.bitwise_xor(beside, flip(slot, others))
    cols = pl.ds(pl.multiple_of(tile * TILE, TILE), TILE)
    q = q_ref[slot, :, cols]

    def update(state, k, v, mask):
        top, total, acc = state
        scores = dot(k, q, 1, 0)
        if mask is not None:
            scores = jnp.where(mask, scores, neg_large)
        new_top = jnp.maximum(top, jnp.max(scores, axis=0, keepdims=True))
        probs = jnp.exp(scores - new_top)
        fade = jnp.exp(top - new_top)
        total = total * fade + jnp.sum(probs, axis=0, keepdims=True)
        acc = acc * fade + dot(v, probs.astype(bf16), 1, 0)
        return new_top, total, acc

    def earlier_piece(index, state):
        place = index // others
        other = jnp.bitwise_xor(lax.rem(index, others), jnp.bitwise_xor(beside, flip(place, others)))
        return update(state, k_all[other, place], v_all[other, place], None)

    def earlier_tile(index, state):
        rows = pl.ds(pl.multiple_of(index * TILE, TILE), TILE)
        return update(state, k_all[0, slot, rows, :], v_all[0, slot, :, rows], None)

    state = (
        jnp.full((1, TILE), neg_large, f32),
        jnp.zeros((1, TILE), f32),
        jnp.zeros((HDIM, TILE), f32),
    )
    state = lax.fori_loop(0, piece, earlier_piece, state)
    state = lax.fori_loop(0, tile, earlier_tile, state)
    ids = id_ref[slot, :, cols]
    mask = column(ids, TILE) <= ids
    top, total, acc = update(state, k_all[0, slot, cols, :], v_all[0, slot, :, cols], mask)
    out = (acc / total).astype(o_ref.dtype)
    rows = o_ref.shape[2]
    for index in range(TILE // rows):
        place = (tile * (TILE // rows) + index) * heads + slot
        o_ref[place] = out[:, index * rows : (index + 1) * rows]
    l_ref[slot, :, cols] = top + jnp.log(total)


def self_forward(info, q, k, v, ids, rows, after):
    others = len(k)
    heads, depth, piece = q.shape
    area = heads * piece * heads * others * piece // 2
    return pl.pallas_call(
        functools.partial(self_forward_kernel, heads, others),
        grid_spec=pltpu.PrefetchScalarGridSpec(
            num_scalar_prefetch=1,
            grid=(heads * piece // TILE,),
            in_specs=[VMEM] * (2 + 2 * others) + [ANY] * len(after),
            out_specs=[VMEM] * 2,
            scratch_shapes=[
                pltpu.VMEM((others, heads, piece, depth), bf16),
                pltpu.VMEM((others, heads, depth, piece), bf16),
            ],
        ),
        out_shape=[
            jax.ShapeDtypeStruct((piece // rows * heads, depth, rows), bf16),
            jax.ShapeDtypeStruct((heads, 1, piece), f32),
        ],
        compiler_params=pltpu.CompilerParams(vmem_limit_bytes=LIMIT),
        cost_estimate=pl.CostEstimate(
            flops=area * 1024, bytes_accessed=8 * 2**20, transcendentals=area
        ),
        name="self_forward",
    )(info, q, ids, *k, *v, *after)


def self_backward_kernel(heads, sides, own, extra, info, *refs):
    refs = list(refs)
    q_ref, g_ref, o_ref, l_ref = refs[:4]
    k_refs, v_refs = refs[4 : 4 + sides], refs[4 + sides : 4 + 2 * sides]
    refs = refs[4 + 2 * sides :]
    id_ref, before_ref = (refs.pop(0), refs.pop(0)) if own else (None, None)
    dq_ref, dk_ref, dv_ref, g_all, inner_all, k_all, v_all, dk, dv = refs[extra:]
    beside = info[1]
    step = pl.program_id(0)
    piece_rows = q_ref.shape[2]
    per = piece_rows // TILE
    slot, tile = step // per, lax.rem(step, per)

    @pl.when(step == 0)
    def _():
        rows = g_ref.shape[2]
        for place in range(heads):
            for index in range(piece_rows // rows):
                at = slice(index * rows, (index + 1) * rows)
                grad = g_ref[index * heads + place]
                g_all[place, :, at] = grad
                inner_all[place, :, at] = jnp.sum(
                    o_ref[index * heads + place].astype(f32) * grad.astype(f32),
                    axis=0,
                    keepdims=True,
                )
            for side in range(sides):
                k_all[side, place] = jnp.swapaxes(k_refs[side][place], 0, 1)
                v_all[side, place] = jnp.swapaxes(v_refs[side][place], 0, 1)
        dk[...] = jnp.zeros_like(dk)
        dv[...] = jnp.zeros_like(dv)

    cols = pl.ds(pl.multiple_of(tile * TILE, TILE), TILE)
    q = q_ref[slot, :, cols]
    grad = g_all[slot, :, cols]
    q_rows = jnp.swapaxes(q, 0, 1)
    grad_rows = jnp.swapaxes(grad, 0, 1)
    log_total = l_ref[slot, :, cols]
    inner = inner_all[slot, :, cols]

    def update(dq, side, place, rows, mask):
        scores = dot(k_all[side, place, rows, :], q, 1, 0)
        if mask is not None:
            scores = jnp.where(mask, scores, neg_large)
        probs = jnp.exp(scores - log_total)
        grad_probs = dot(v_all[side, place, rows, :], grad, 1, 0)
        grad_scores = (probs * (grad_probs - inner)).astype(bf16)
        dv[side, place, rows, :] += dot(probs.astype(bf16), grad_rows, 1, 0)
        dk[side, place, rows, :] += dot(grad_scores, q_rows, 1, 0)
        return dq + dot(k_refs[side][place, :, rows], grad_scores, 1, 0)

    dq = before_ref[slot, :, cols] if own else jnp.zeros((HDIM, TILE), f32)
    for side in range(sides):

        def earlier(index, dq, side=side):
            rows = pl.ds(pl.multiple_of(lax.rem(index, per) * TILE, TILE), TILE)
            return update(dq, side, index // per, rows, None)

        if own:
            count = slot * per + tile
        else:
            here = jnp.bitwise_xor(beside, flip(slot, sides + 1))
            count = (slot + jnp.where(jnp.bitwise_xor(here, side + 1) < here, 1, 0)) * per
        dq = lax.fori_loop(0, count, earlier, dq)
    if own:
        ids = id_ref[slot, :, cols]
        mask = column(ids, TILE) <= ids
        dq = update(dq, 0, slot, cols, mask) * 0.125
    dq_ref[slot, :, cols] = dq.astype(dq_ref.dtype)

    @pl.when(step == heads * per - 1)
    def _():
        for side in range(sides):
            for place in range(heads):
                dk_ref[side, place] = jnp.swapaxes(dk[side, place], 0, 1).astype(dk_ref.dtype)
                dv_ref[side, place] = jnp.swapaxes(dv[side, place], 0, 1).astype(dv_ref.dtype)


def self_backward(info, q, k, v, ids, grad, context, log_total, before, after):
    own = ids is not None
    sides = len(k)
    heads, depth, piece = q.shape
    flat = [q, grad, context, log_total, *k, *v] + ([ids, before] if own else [])
    area = heads * piece * heads * sides * piece // 2
    return pl.pallas_call(
        functools.partial(self_backward_kernel, heads, sides, own, len(after)),
        grid_spec=pltpu.PrefetchScalarGridSpec(
            num_scalar_prefetch=1,
            grid=(heads * piece // TILE,),
            in_specs=[VMEM] * len(flat) + [ANY] * len(after),
            out_specs=[VMEM] * 3,
            scratch_shapes=[
                pltpu.VMEM((heads, depth, piece), bf16),
                pltpu.VMEM((heads, 1, piece), f32),
                pltpu.VMEM((sides, heads, piece, depth), bf16),
                pltpu.VMEM((sides, heads, piece, depth), bf16),
                pltpu.VMEM((sides, heads, piece, depth), f32),
                pltpu.VMEM((sides, heads, piece, depth), f32),
            ],
        ),
        out_shape=[jax.ShapeDtypeStruct((heads, depth, piece), bf16 if own else f32)]
        + [jax.ShapeDtypeStruct((sides, heads, depth, piece), f32 if own else bf16)] * 2,
        compiler_params=pltpu.CompilerParams(vmem_limit_bytes=LIMIT),
        cost_estimate=pl.CostEstimate(
            flops=area * 64, bytes_accessed=2**16, transcendentals=0
        ),
        name="self_backward",
    )(info, *flat, *after)


def gelu_parts(value):
    half = 0.5 * (1.0 + lax.erf(value * 0.7071067811865476))
    slope = half + value * jnp.exp(-0.5 * value * value) * 0.3989422804014327
    return value * half, slope


def middle_forward_kernel(group, heads, info, *refs):
    x_ref, ctx_ref, norm_ref, bias_ref = refs[:4]
    w_refs, kv_refs = refs[4 : 4 + group], refs[4 + group : 4 + 2 * group]
    x_two, unit_two, inv_two, unit_three, inv_three, h_two, h_three, ctx_xor, q, ctx, log = refs[-11:]
    width = heads * HDIM
    me = info[2]

    def natural(step):
        return pl.ds(pl.multiple_of(jnp.bitwise_xor(me, step) * width, width), width)

    resid = x_ref[...].astype(f32) + norm_ref[4:5, :]
    for step in range(group):
        part = ctx_ref[natural(step), :]
        ctx_xor[step * width : (step + 1) * width, :] = part
        resid = resid + dot(jnp.swapaxes(part, 0, 1), w_refs[step][0], 1, 1)
    unit, inverse = normalize(resid)
    unit_two[...] = unit
    inv_two[...] = inverse
    low = (unit * norm_ref[0:1, :] + norm_ref[1:2, :]).astype(bf16)
    h_two[...] = low
    for step in range(group):
        out = (dot(low, w_refs[step][2], 1, 0) + bias_ref[:, natural(step)]) * 0.125
        q[step * width : (step + 1) * width, :] = jnp.swapaxes(out.astype(bf16), 0, 1)
    resid = resid + norm_ref[5:6, :]
    for step in range(group):
        for head in range(heads):
            own = slice(head * HDIM, (head + 1) * HDIM)
            rows = slice(step * width + head * HDIM, step * width + (head + 1) * HDIM)
            scores = dot(jnp.swapaxes(kv_refs[step][0, own, :], 0, 1), q[rows, :], 1, 0)
            top = jnp.max(scores, axis=0, keepdims=True)
            probs = jnp.exp(scores - top)
            total = jnp.sum(probs, axis=0, keepdims=True)
            out = dot(kv_refs[step][1, own, :], probs.astype(bf16), 1, 0)
            ctx[rows, :] = (out / total).astype(bf16)
            log[step * heads + head] = top + jnp.log(total)
        part = ctx[step * width : (step + 1) * width, :]
        resid = resid + dot(jnp.swapaxes(part, 0, 1), w_refs[step][1], 1, 1)
    x_two[...] = resid
    unit, inverse = normalize(resid)
    unit_three[...] = unit
    inv_three[...] = inverse
    h_three[...] = (unit * norm_ref[2:3, :] + norm_ref[3:4, :]).astype(bf16)


def middle_forward(info, x, ctx, norm, bias, w, kv, heads, after):
    rows, model = x.shape
    group = len(w)
    total = ctx.shape[0]
    return pl.pallas_call(
        functools.partial(middle_forward_kernel, group, heads),
        grid_spec=pltpu.PrefetchScalarGridSpec(
            num_scalar_prefetch=1,
            grid=(1,),
            in_specs=[VMEM] * (4 + 2 * group) + [ANY] * len(after),
            out_specs=[VMEM] * 11,
        ),
        out_shape=[
            jax.ShapeDtypeStruct((rows, model), f32),
            jax.ShapeDtypeStruct((rows, model), f32),
            jax.ShapeDtypeStruct((rows, 1), f32),
            jax.ShapeDtypeStruct((rows, model), f32),
            jax.ShapeDtypeStruct((rows, 1), f32),
            jax.ShapeDtypeStruct((rows, model), bf16),
            jax.ShapeDtypeStruct((rows, model), bf16),
            jax.ShapeDtypeStruct((total, rows), bf16),
            jax.ShapeDtypeStruct((total, rows), bf16),
            jax.ShapeDtypeStruct((total, rows), bf16),
            jax.ShapeDtypeStruct((total // HDIM, 1, rows), f32),
        ],
        compiler_params=pltpu.CompilerParams(vmem_limit_bytes=LIMIT),
        cost_estimate=pl.CostEstimate(
            flops=6 * rows * model * total, bytes_accessed=12 * 2**20, transcendentals=2**20
        ),
        name="middle_forward",
    )(info, x, ctx, norm, bias, *w, *kv, *after)


def middle_backward_kernel(group, heads, extra, info, *refs):
    e_ref, cot_ref, unit_two, inv_two, unit_three, inv_three, norm_ref, q, ctx, log = refs[:10]
    w_refs, kv_refs = refs[10 : 10 + group], refs[10 + group : 10 + 2 * group]
    d_one, low_two, low_one, dq, dkv, d_ctx, sums = refs[10 + 2 * group + extra :]
    width = heads * HDIM
    me = info[2]

    def natural(step):
        return pl.ds(pl.multiple_of(jnp.bitwise_xor(me, step) * width, width), width)

    def add(row, value):
        sums[row : row + 1, :] = jnp.sum(value, axis=0, keepdims=True)

    def norm_back(grad, unit, inverse, gain, row):
        add(row, grad * unit)
        add(row + 1, grad)
        scaled = grad * gain
        return (
            scaled
            - jnp.mean(scaled, axis=-1, keepdims=True)
            - unit * jnp.mean(scaled * unit, axis=-1, keepdims=True)
        ) * inverse

    cot = cot_ref[...].astype(f32)
    d_two = cot + norm_back(e_ref[...], unit_three[...], inv_three[...], norm_ref[2:3, :], 0)
    low = d_two.astype(bf16)
    low_two[...] = low
    add(4, low.astype(f32))
    add(6, cot)
    e_two = jnp.zeros_like(d_two)
    for step in range(group):
        grads = jnp.swapaxes(dot(low, w_refs[step][1], 1, 0).astype(bf16), 0, 1)
        for head in range(heads):
            own = slice(head * HDIM, (head + 1) * HDIM)
            rows = slice(step * width + head * HDIM, step * width + (head + 1) * HDIM)
            grad = grads[own]
            inner = jnp.sum(ctx[rows, :].astype(f32) * grad.astype(f32), axis=0, keepdims=True)
            k_t = kv_refs[step][0, own, :]
            scores = dot(jnp.swapaxes(k_t, 0, 1), q[rows, :], 1, 0)
            probs = jnp.exp(scores - log[step * heads + head])
            grad_probs = dot(jnp.swapaxes(kv_refs[step][1, own, :], 0, 1), grad, 1, 0)
            grad_scores = (probs * (grad_probs - inner)).astype(bf16)
            dq[rows, :] = (dot(k_t, grad_scores, 1, 0) * 0.125).astype(bf16)
            dkv[step, 0, own, :] = dot(q[rows, :], grad_scores, 1, 1)
            dkv[step, 1, own, :] = dot(grad, probs.astype(bf16), 1, 1)
        part = jnp.swapaxes(dq[step * width : (step + 1) * width, :], 0, 1)
        sums[7:8, natural(step)] = jnp.sum(part.astype(f32), axis=0, keepdims=True)
        e_two = e_two + dot(part, w_refs[step][2], 1, 1)
    d_next = d_two + norm_back(e_two, unit_two[...], inv_two[...], norm_ref[0:1, :], 2)
    d_one[...] = d_next
    low = d_next.astype(bf16)
    low_one[...] = low
    add(5, low.astype(f32))
    for step in range(group):
        grads = dot(low, w_refs[step][0], 1, 0).astype(bf16)
        d_ctx[natural(step), :] = jnp.swapaxes(grads, 0, 1)


def middle_backward(info, e, cot, saved, norm, w, kv, heads, after):
    unit_two, inv_two, unit_three, inv_three, q, ctx, log = saved
    rows, model = cot.shape
    group = len(w)
    total = q.shape[0]
    enc = kv[0].shape[2]
    return pl.pallas_call(
        functools.partial(middle_backward_kernel, group, heads, len(after)),
        grid_spec=pltpu.PrefetchScalarGridSpec(
            num_scalar_prefetch=1,
            grid=(1,),
            in_specs=[VMEM] * (10 + 2 * group) + [ANY] * len(after),
            out_specs=[VMEM] * 7,
        ),
        out_shape=[
            jax.ShapeDtypeStruct((rows, model), f32),
            jax.ShapeDtypeStruct((rows, model), bf16),
            jax.ShapeDtypeStruct((rows, model), bf16),
            jax.ShapeDtypeStruct((total, rows), bf16),
            jax.ShapeDtypeStruct((group, 2, heads * HDIM, enc), f32),
            jax.ShapeDtypeStruct((total, rows), bf16),
            jax.ShapeDtypeStruct((8, model), f32),
        ],
        compiler_params=pltpu.CompilerParams(vmem_limit_bytes=LIMIT),
        cost_estimate=pl.CostEstimate(
            flops=6 * rows * model * total, bytes_accessed=16 * 2**20, transcendentals=2**20
        ),
        name="middle_backward",
    )(info, e, cot, unit_two, inv_two, unit_three, inv_three, norm, q, ctx, log, *w, *kv, *after)


CHUNK = 512


def grad_act_kernel(*refs):
    w_ref, out_ref = refs[-2:]
    rows = refs[0].shape[0]
    for index, ref in enumerate(refs[:-2]):
        for start in range(0, w_ref.shape[1], CHUNK):
            cols = slice(start, start + CHUNK)
            out_ref[index * rows : (index + 1) * rows, cols] = dot(
                ref[...], w_ref[:, cols], 1, 0
            ).astype(bf16)


def grad_act(cots, w):
    rows, ff = cots[0].shape[0] * len(cots), w.shape[1]
    return pl.pallas_call(
        grad_act_kernel,
        in_specs=[VMEM] * (len(cots) + 1),
        out_specs=VMEM,
        out_shape=jax.ShapeDtypeStruct((rows, ff), bf16),
        compiler_params=pltpu.CompilerParams(vmem_limit_bytes=LIMIT),
        cost_estimate=pl.CostEstimate(
            flops=2 * rows * ff * w.shape[0], bytes_accessed=10 * 2**20, transcendentals=0
        ),
        name="grad_act",
    )(*cots, w)


def feed_kernel(first, blocks, *refs):
    h_refs, (ga_ref, b_ref, w_ref) = refs[:blocks], refs[blocks : blocks + 3]
    refs = refs[blocks + 3 :]
    act_ref, du_ref, sum_ref, e_refs = refs[0], refs[1], refs[2], refs[3 : 3 + blocks]
    rows, ff = h_refs[0].shape[0], w_ref.shape[1]
    totals = [0.0] * blocks
    for start in range(0, ff, CHUNK):
        cols = slice(start, start + CHUNK)
        sums = 0.0
        for index in range(blocks):
            own = slice(index * rows, (index + 1) * rows)
            inner = dot(h_refs[index][...], w_ref[:, cols], 1, 0) + b_ref[:, cols]
            act, slope = gelu_parts(inner)
            act_ref[own, cols] = act.astype(bf16)
            there = slice((first + index) * rows, (first + index + 1) * rows)
            du = (slope * ga_ref[there, cols].astype(f32)).astype(bf16)
            du_ref[own, cols] = du
            sums = sums + jnp.sum(du.astype(f32), axis=0, keepdims=True)
            totals[index] = totals[index] + dot(du, w_ref[:, cols], 1, 1)
        sum_ref[:, cols] = sums
    for index in range(blocks):
        e_refs[index][...] = totals[index].astype(e_refs[index].dtype)


def feed(h, ga, w, bias, first):
    rows, model = h[0].shape
    ff = w.shape[1]
    blocks = len(h)
    return pl.pallas_call(
        functools.partial(feed_kernel, first, blocks),
        in_specs=[VMEM] * (blocks + 3),
        out_specs=[VMEM] * (3 + blocks),
        out_shape=[jax.ShapeDtypeStruct((blocks * rows, ff), bf16)] * 2
        + [jax.ShapeDtypeStruct((1, ff), f32)]
        + [
            jax.ShapeDtypeStruct((rows, model), bf16 if (first + index) % 2 else f32)
            for index in range(blocks)
        ],
        compiler_params=pltpu.CompilerParams(vmem_limit_bytes=LIMIT),
        cost_estimate=pl.CostEstimate(
            flops=4 * blocks * rows * ff * model, bytes_accessed=12 * 2**20, transcendentals=2**20
        ),
        name="feed",
    )(*h, ga, bias, w)


def outer_kernel(count, side, halves, extra, info, *refs):
    lefts, rights = refs[:count], refs[count : count + 2]
    got_ref = refs[count + 2] if extra else None
    out_ref, picked, turned = refs[-3:]
    rows, model = lefts[0].shape
    shard = out_ref.shape[0] // halves
    which = jnp.bitwise_xor(lax.rem(info[3], 2), side or 0)
    for index in range(count):
        own = slice(index * rows, (index + 1) * rows)
        if side is None:
            picked[:, own] = jnp.swapaxes(lefts[index][...], 0, 1)
            continue
        if shard % 128:
            turned[...] = jnp.swapaxes(lefts[index][...], 0, 1)
        for half in range(halves):
            start = pl.multiple_of((2 * half + which) * shard, shard)
            if shard % 128:
                part = turned[pl.ds(start, shard), :]
            else:
                part = jnp.swapaxes(lefts[index][:, pl.ds(start, shard)], 0, 1)
            picked[half * shard : (half + 1) * shard, own] = part
    middle = rights[0].shape[0]
    for start in range(0, out_ref.shape[1], CHUNK):
        cols = slice(start, start + CHUNK)
        out = dot(picked[:, :middle], rights[0][:, cols], 1, 0)
        out = out + dot(picked[:, middle:], rights[1][:, cols], 1, 0)
        if extra:
            out = out + got_ref[:, cols].astype(f32)
        out_ref[:, cols] = out.astype(bf16)


def outer(lefts, rights, info, side=None, halves=1, got=None):
    rows, model = lefts[0].shape
    count = len(lefts)
    ff = rights[0].shape[1]
    extra = [] if got is None else [got]
    size = model if side is None else model // 2
    return pl.pallas_call(
        functools.partial(outer_kernel, count, side, halves, len(extra)),
        grid_spec=pltpu.PrefetchScalarGridSpec(
            num_scalar_prefetch=1,
            grid=(1,),
            in_specs=[VMEM] * (count + 2 + len(extra)),
            out_specs=VMEM,
            scratch_shapes=[pltpu.VMEM((size, count * rows), bf16), pltpu.VMEM((model, rows), bf16)],
        ),
        out_shape=jax.ShapeDtypeStruct((size, ff), bf16),
        compiler_params=pltpu.CompilerParams(vmem_limit_bytes=LIMIT),
        cost_estimate=pl.CostEstimate(
            flops=2 * count * rows * ff * size, bytes_accessed=10 * 2**20, transcendentals=0
        ),
        name="outer",
    )(info, *lefts, *rights, *extra)


def local(
    hidden,
    encoder,
    cotangent,
    block_ids,
    self_qkv,
    self_out,
    cross_qkv,
    cross_out,
    up_weight,
    down_weight,
    proj_bias,
    up_bias,
    norm_gain,
    norm_shift,
):
    tok_size, group = lax.axis_size("tok"), lax.axis_size("hd")
    tok_index, me = lax.axis_index("tok"), lax.axis_index("hd")
    rows, model = hidden.shape
    shard = self_qkv.shape[0]
    width = self_qkv.shape[2]
    ff_local = up_weight.shape[1]
    piece_rows = rows * group
    span = SEQ // piece_rows
    heads = min(width // HDIM, span)
    others = span // heads
    assert heads * HDIM == width and heads * others == span
    seq_count, enc_rows, _ = encoder.shape
    enc_total = enc_rows * group
    own_seq = tok_index // span
    at = lax.rem(tok_index, span) // others
    beside = jnp.bitwise_xor(lax.rem(tok_index, others), lax.rem(at, 2) * (others - 1))
    info = jnp.stack([at, beside, me, tok_index]).astype(jnp.int32)

    def natural(blocks):
        stacked = jnp.stack(blocks)
        return [pick(stacked, me ^ index) for index in range(group)]

    even = lax.rem(tok_index, 2)
    halves = [[i for i in range(tok_size) if i % 2 == side] for side in range(2)]
    many = tok_size // 2

    def gather_half(block):
        return lax.all_gather(block, "tok", axis=0, tiled=True, axis_index_groups=halves)

    def gather_tok(block):
        return lax.all_gather(block, "tok", axis=0, tiled=True)

    def along_halves(block):
        return lax.all_to_all(
            jnp.broadcast_to(block[None], (many, *block.shape)),
            "tok", 0, 0, tiled=True, axis_index_groups=halves,
        )

    def merge_sides(own, got):
        sides = [jnp.where(even == 0, own, got), jnp.where(even == 0, got, own)]
        return jnp.stack(sides, 1).reshape(model, -1)

    w_self = self_qkv.reshape(shard, 3, heads, HDIM).transpose(0, 2, 1, 3)
    w_self = gather_tok(w_self.reshape(shard, 3 * width))
    w_mid = along_halves(
        jnp.concatenate([self_out.T, cross_out.T, cross_qkv.reshape(shard, 3 * width)], 1)
    )

    own_ids = lax.dynamic_slice_in_dim(block_ids, me * rows, rows).astype(bf16)
    small = jnp.concatenate(
        [
            proj_bias.T.reshape(-1),
            norm_gain.T.reshape(-1),
            norm_shift.T.reshape(-1),
            up_bias,
            own_ids,
        ]
    )
    total_devices = tok_size * group
    small_all = lax.all_to_all(
        jnp.broadcast_to(small[None], (total_devices, small.shape[0])),
        ("tok", "hd"), 0, 0, tiled=True,
    ).astype(f32)
    few = model // total_devices
    vectors = small_all[:, : 13 * few].reshape(total_devices, 13, few)
    vectors = vectors.transpose(1, 0, 2).reshape(13, model)
    bias, gain, shift = vectors[:7], vectors[7:10], vectors[10:13]
    few_up = up_bias.shape[0]
    bias_up = small_all[:, 13 * few : 13 * few + few_up].reshape(-1)
    bias_up = lax.dynamic_slice_in_dim(bias_up, me * ff_local, ff_local)
    ids = small_all[:, 13 * few + few_up :].reshape(tok_size, 1, piece_rows)
    ids = lax.dynamic_slice_in_dim(ids, own_seq * span, span).reshape(heads, others, 1, piece_rows)
    ids = jnp.stack([pick(ids[i], beside ^ (i % 2 * (others - 1))) for i in range(heads)])

    def own_columns(vector):
        return lax.dynamic_slice_in_dim(vector, me * width, width)

    hidden_blocks = gather_xor(hidden)
    self_bias = jnp.stack(
        [own_columns(bias[0]), jnp.zeros((width,), f32), own_columns(bias[1])]
    )
    scale = jnp.broadcast_to(jnp.array([0.125, 1.0, 1.0], f32)[:, None], (3, width))
    factors = jnp.stack([self_bias, scale]).reshape(2, 3, heads, HDIM)
    factors = factors.transpose(0, 2, 1, 3).reshape(2, 3 * width)

    lines = [
        [seq * span + i * others + (side ^ (i % 2 * (others - 1))) for i in range(heads)]
        for seq in range(tok_size // span)
        for side in range(others)
    ]
    wide_lines = [[i * group + h for h in range(group) for i in line] for line in lines]

    def across_lines(value):
        return lax.all_to_all(value, "tok", 0, 0, tiled=True, axis_index_groups=lines)

    def across_wide(value):
        return lax.all_to_all(
            value, ("tok", "hd"), 0, 0, tiled=True, axis_index_groups=wide_lines
        )

    q_out, k_out, v_out, h_one = project(
        info, hidden_blocks, w_self, jnp.stack([gain[0], shift[0]]), factors, heads, [w_mid]
    )
    w_up, w_down = tie([up_weight, down_weight.T], [h_one])
    w_up, w_down = gather_tok(w_up), gather_tok(w_down)
    w_mid = merge_sides(w_mid, swap(w_mid, "tok", 1))
    k = [across_lines(k_out)]
    v = [across_lines(v_out)]
    q = across_lines(q_out)
    k += [swap(k[0], "tok", other) for other in range(1, others)]
    v += [swap(v[0], "tok", other) for other in range(1, others)]
    w_cross_kv = w_mid[:, 3 * width :]
    enc_all = jnp.concatenate(natural(gather_xor(encoder)), 1)
    kv_bias = jnp.concatenate([jnp.zeros((width,), f32), own_columns(bias[4])])
    kv_two = dot(w_cross_kv, pick(enc_all, own_seq), 0, 1) + kv_bias[:, None]
    kv_two = kv_two.astype(bf16).reshape(2, width, enc_total)
    kv_two = gather_xor(kv_two)

    context, log_one = self_forward(info, q, k, v, ids, rows, kv_two)

    mid_block = jnp.stack(
        [w_mid[:, :width], w_mid[:, width : 2 * width], w_mid[:, 2 * width : 3 * width]]
    )
    w_blocks = gather_xor(mid_block, lambda value: tie([value], [log_one])[0])
    ctx_one = across_wide(context).reshape(model, rows)
    norm_rows = jnp.stack([gain[1], shift[1], gain[2], shift[2], bias[2], bias[5]])
    (
        resid_two, unit_two, inv_two, unit_three, inv_three,
        h_two, h_three, ctx_one, q_two, ctx_two, log_two,
    ) = middle_forward(
        info, hidden, ctx_one, norm_rows, bias[3:4], w_blocks, kv_two, heads, []
    )

    cot_blocks = gather_xor(cotangent)
    h_blocks = gather_xor(h_three)
    grad_a = grad_act(cot_blocks, w_down)
    near = group // 2
    bias_row = bias_up[None]
    near_out = feed(h_blocks[:near], grad_a, w_up, bias_row, 0)
    far_out = feed(h_blocks[near:], grad_a, w_up, bias_row, near)
    acts, grad_inners = [near_out[0], far_out[0]], [near_out[1], far_out[1]]
    up_sums = (near_out[2] + far_out[2])[0]
    grad_h_three = reduce_xor(list(near_out[3:]) + list(far_out[3:]))

    def half_columns(array, side):
        return jnp.concatenate(
            [
                lax.dynamic_slice_in_dim(array, (2 * i + side) * shard, shard, 1)
                for i in range(tok_size // 2)
            ],
            1,
        )

    def half_rows(array, side):
        return jnp.concatenate(
            [
                lax.dynamic_slice_in_dim(array, (2 * i + side) * shard, shard, 0)
                for i in range(tok_size // 2)
            ],
            0,
        )

    def reduce_tok(value):
        return lax.psum_scatter(value, "tok", scatter_dimension=0, tiled=True).astype(f32)

    def reduce_half(value):
        return lax.psum_scatter(
            value, "tok", scatter_dimension=0, tiled=True, axis_index_groups=halves
        ).astype(f32)

    grad_up = outer(h_blocks, grad_inners, info)
    down_away = outer(cot_blocks, acts, info, 1, many)
    sent_up = reduce_tok(grad_up)
    down_got = swap(down_away, "tok", 1)

    grad_one, grad_two_low, grad_one_low, grad_q_two, grad_kv_two, grad_ctx_one, sums = (
        middle_backward(
            info, grad_h_three, cotangent,
            (unit_two, inv_two, unit_three, inv_three, q_two, ctx_two, log_two),
            norm_rows, w_blocks, kv_two, heads, [grad_up, down_away],
        )
    )
    grad_heads = across_wide(grad_ctx_one.reshape(group * heads, HDIM, rows))
    grad_mid = [
        dot(grad_one_low, ctx_one, 0, 1),
        dot(grad_two_low, ctx_two, 0, 1),
        dot(h_two, grad_q_two, 0, 1),
    ]
    grad_mid = [
        jnp.concatenate([g[:, j * width : (j + 1) * width] for g in grad_mid], 1).astype(
            bf16 if j % 2 else f32
        )
        for j in range(group)
    ]
    masks = [1 << bit for bit in range(tok_size.bit_length() - 1)]

    def add_low(value, got):
        return (value.astype(f32) + got.astype(f32)).astype(bf16)

    grad_q_away, grad_k_away, grad_v_away = self_backward(
        info, q, k[1:], v[1:], None, grad_heads, context, log_one, None, grad_mid
    )
    grad_q_away, grad_k_away, grad_v_away, down_got = tie(
        [grad_q_away, grad_k_away, grad_v_away, down_got], []
    )
    down_sum = outer(cot_blocks, acts, info, 0, many, down_got)
    sent_down = reduce_half(tie([down_sum], [sent_up])[0]).T
    kv_total = reduce_xor(
        [grad_kv_two[j] for j in range(group)], lambda got: tie([got], [grad_q_away])[0]
    )
    seq_pick = jnp.arange(seq_count) == own_seq
    kv_total = jnp.where(seq_pick[:, None, None, None], kv_total[None], 0.0).astype(bf16)
    grad_mid = reduce_xor(grad_mid, lambda got: tie([got], [grad_q_away])[0])
    mid_got = swap(half_rows(grad_mid, 1 - even).astype(bf16), "tok", 1)
    mid_sum = (half_rows(grad_mid, even) + mid_got.astype(f32)).astype(bf16)
    sent_mid = reduce_half(tie([mid_sum], [sent_down])[0])
    grad_k_got = [swap(grad_k_away[i], "tok", i + 1) for i in range(others - 1)]
    grad_v_got = [swap(grad_v_away[i], "tok", i + 1) for i in range(others - 1)]
    grad_q, grad_k, grad_v = self_backward(
        info, q, k[:1], v[:1], ids, grad_heads, context, log_one, grad_q_away, [down_sum]
    )
    kv_got = swap(kv_total, "tok", masks[0])
    grad_q, grad_k, grad_v, sent_up, kv_got = tie([grad_q, grad_k, grad_v, sent_up, kv_got], [])
    kv_total = add_low(kv_total, kv_got)
    acts = tie(acts, [grad_q])
    def act_block(index):
        start = index % near * rows
        return acts[index // near][start : start + rows]

    final = reduce_xor([dot(act_block(j), w_down, 1, 1) for j in range(group)])
    output = (resid_two + final + bias[6]).astype(bf16)
    grad_k = grad_k[0] + sum(got.astype(f32) for got in grad_k_got)
    grad_v = grad_v[0] + sum(got.astype(f32) for got in grad_v_got)
    grad_qkv = jnp.stack([grad_q, grad_k.astype(bf16), grad_v.astype(bf16)], 1)
    grad_qkv = across_lines(grad_qkv).reshape(3 * width, piece_rows)
    kv_got = swap(kv_total, "tok", masks[1])
    grad_qkv, sent_down, kv_got = tie([grad_qkv, sent_down, kv_got], [])
    kv_total = add_low(kv_total, kv_got)
    for got_mask in masks[2:]:
        kv_total = add_low(kv_total, swap(kv_total, "tok", got_mask))
    kv_flat = kv_total.reshape(seq_count, 2 * width, enc_total)
    own_enc = lax.dynamic_slice_in_dim(enc_all, tok_index * shard, shard, 2)
    sent_cross_kv = sum(dot(own_enc[n], kv_flat[n], 0, 1) for n in range(seq_count))

    def encoder_part(index):
        start = (me ^ index) * enc_rows
        return jnp.stack(
            [
                dot(lax.dynamic_slice_in_dim(kv_flat[n], start, enc_rows, 1), w_cross_kv, 0, 1)
                for n in range(seq_count)
            ]
        )

    grad_encoder = reduce_xor([encoder_part(j) for j in range(group)])

    grad_h_one = reduce_xor(
        [
            dot(
                lax.dynamic_slice(grad_qkv, (0, (me ^ j) * rows), (3 * width, rows)), w_self, 0, 1
            )
            for j in range(group)
        ]
    )
    grad_self = dot(h_one, grad_qkv, 0, 1).astype(bf16)
    sent_self = lax.all_to_all(grad_self, "tok", 0, 0, tiled=True)
    ordered = sent_self
    sent_self = jnp.sum(sent_self.reshape(tok_size, shard, 3 * width).astype(f32), 0)
    sent_self = sent_self.reshape(shard, heads, 3, HDIM)
    sent_self = sent_self.transpose(0, 2, 1, 3).reshape(shard, 3, width)
    unit_one, inverse_one = normalize(hidden.astype(f32))
    back, gain_one, shift_one = norm_backward(grad_h_one, unit_one, inverse_one, gain[0])
    grad_hidden = grad_one + back

    def place(vector):
        return lax.dynamic_update_slice_in_dim(jnp.zeros((model,), f32), vector, me * width, 0)

    qkv_sums = jnp.sum(grad_qkv.astype(f32), 1).reshape(heads, 3, HDIM)
    once = (tok_index == 0).astype(f32)
    vectors = jnp.stack(
        [
            place(qkv_sums[:, 0].reshape(-1)),
            place(qkv_sums[:, 2].reshape(-1)),
            sums[5],
            sums[7],
            place(jnp.sum(kv_flat[:, width:].astype(f32), (0, 2)) * once),
            sums[4],
            sums[6],
            gain_one,
            sums[2],
            sums[0],
            shift_one,
            sums[3],
            sums[1],
        ]
    )
    vectors = vectors.reshape(13, total_devices, few).transpose(1, 0, 2).reshape(total_devices, -1)
    up_all = lax.dynamic_update_slice_in_dim(
        jnp.zeros((group * ff_local,), f32), up_sums, me * ff_local, 0
    )
    vectors = jnp.concatenate([vectors, up_all.reshape(total_devices, -1)], 1)
    vectors = tie([vectors], [ordered])[0]
    vectors = jnp.sum(lax.all_to_all(vectors, ("tok", "hd"), 0, 0, tiled=True), 0)
    columns = vectors[: 13 * few].reshape(13, few).T

    sent_mid = [sent_mid[:, j * width : (j + 1) * width] for j in range(3)]
    sent_cross = jnp.concatenate(
        [sent_mid[2][:, None], sent_cross_kv.reshape(shard, 2, width)], 1
    )
    return (
        output,
        grad_hidden,
        grad_encoder,
        sent_self,
        sent_mid[0].T,
        sent_cross,
        sent_mid[1].T,
        sent_up,
        sent_down,
        columns[:, :7],
        vectors[13 * few :],
        columns[:, 7:10],
        columns[:, 10:13],
    )


def solution(mesh):
    in_specs = (
        P(("tok", "hd"), None),
        P(None, "hd", None),
        P(("tok", "hd"), None),
        P("tok"),
        P("tok", None, "hd"),
        P("hd", "tok"),
        P("tok", None, "hd"),
        P("hd", "tok"),
        P("tok", "hd"),
        P("hd", "tok"),
        P(("tok", "hd"), None),
        P(("tok", "hd")),
        P(("tok", "hd"), None),
        P(("tok", "hd"), None),
    )
    out_specs = (
        P(("tok", "hd"), None),
        P(("tok", "hd"), None),
        P(None, "hd", None),
        P("tok", None, "hd"),
        P("hd", "tok"),
        P("tok", None, "hd"),
        P("hd", "tok"),
        P("tok", "hd"),
        P("hd", "tok"),
        P(("tok", "hd"), None),
        P(("tok", "hd")),
        P(("tok", "hd"), None),
        P(("tok", "hd"), None),
    )
    return jax.shard_map(local, mesh=mesh, in_specs=in_specs, out_specs=out_specs, check_vma=False)
```

```python
import functools

import jax
import jax.numpy as jnp
from jax import lax
from jax.experimental import pallas as pl
from jax.experimental.pallas import tpu as pltpu
from jax.sharding import PartitionSpec as P

HDIM = 64
SEQ = 8192
TILE = 512
norm_eps = 1e-05
neg_large = -1e30
f32 = jnp.float32
bf16 = jnp.bfloat16


def dot(left, right, left_dim, right_dim):
    return lax.dot_general(
        left, right, (((left_dim,), (right_dim,)), ((), ())), preferred_element_type=f32
    )


def swap(value, axis, mask):
    return lax.ppermute(value, axis, [(i, i ^ mask) for i in range(lax.axis_size(axis))])


def hd_masks():
    mask, masks = lax.axis_size("hd") // 2, []
    while mask:
        masks.append(mask)
        mask //= 2
    return masks


def gather_xor(value, first=lambda value: value):
    have = {0: value}
    for mask in hd_masks():
        for index in list(have):
            have[index ^ mask] = first(swap(have[index], "hd", mask))
        first = lambda value: value
    return [have[index] for index in range(len(have))]


def reduce_xor(parts, last=lambda value: value):
    have = dict(enumerate(parts))
    for mask in reversed(hd_masks()):
        for index in sorted(have, reverse=True):
            if index & mask:
                got = swap(have.pop(index).astype(bf16), "hd", mask)
                if len(have) == 1:
                    got = last(got)
                total = have[index ^ mask].astype(f32) + got.astype(f32)
                have[index ^ mask] = total if len(have) == 1 else total.astype(bf16)
    return have[0]


def pick(stacked, index):
    return lax.dynamic_index_in_dim(stacked, index, 0, keepdims=False)


def normalize(value):
    center = value - jnp.mean(value, axis=-1, keepdims=True)
    inverse = lax.rsqrt(jnp.mean(center * center, axis=-1, keepdims=True) + norm_eps)
    return center * inverse, inverse


def norm_backward(grad, unit, inverse, gain):
    scaled = grad * gain
    back = (
        scaled
        - jnp.mean(scaled, axis=-1, keepdims=True)
        - unit * jnp.mean(scaled * unit, axis=-1, keepdims=True)
    ) * inverse
    return back, jnp.sum(grad * unit, axis=0), jnp.sum(grad, axis=0)


def column(row, rows):
    return jnp.swapaxes(jnp.broadcast_to(row, (128, rows)), 0, 1)[:, :1]


VMEM = pl.BlockSpec(memory_space=pltpu.VMEM)
LIMIT = 48 * 2**20


ANY = pl.BlockSpec(memory_space=pl.ANY)


def tie(values, after):
    count = len(values)
    return pl.pallas_call(
        lambda *refs: None,
        in_specs=[ANY] * (count + len(after)),
        out_specs=[ANY] * count,
        out_shape=[jax.ShapeDtypeStruct(value.shape, value.dtype) for value in values],
        input_output_aliases={index: index for index in range(count)},
        name="tie",
    )(*values, *after)


def project_kernel(heads, group, info, *refs):
    refs = list(refs)
    w_ref, norm_ref, bias_ref = refs[:3]
    q_ref, k_ref, v_ref, h_ref = refs[-4:]
    x_refs = refs[3 : 3 + group]
    rows = x_refs[0].shape[0]
    for step, x_ref in enumerate(x_refs):
        start = pl.multiple_of(jnp.bitwise_xor(info[2], step) * rows, rows)
        cols = pl.ds(start, rows)
        x = x_ref[...].astype(f32)
        h = (normalize(x)[0] * norm_ref[0:1, :] + norm_ref[1:2, :]).astype(bf16)
        h_ref[cols, :] = h
        out = (dot(h, w_ref[...], 1, 0) + bias_ref[0:1, :]) * bias_ref[1:2, :]
        out = jnp.swapaxes(out.astype(bf16), 0, 1)
        for head in range(heads):
            for part, ref in enumerate((q_ref, k_ref, v_ref)):
                first = (head * 3 + part) * HDIM
                ref[head, :, cols] = out[first : first + HDIM]


def project(info, x, w, norm, bias, heads, after):
    rows, model = x[0].shape
    group = len(x)
    piece = rows * group
    width = w.shape[1]
    return pl.pallas_call(
        functools.partial(project_kernel, heads, group),
        grid_spec=pltpu.PrefetchScalarGridSpec(
            num_scalar_prefetch=1,
            grid=(1,),
            in_specs=[VMEM] * (group + 3) + [ANY] * len(after),
            out_specs=[VMEM] * 4,
        ),
        out_shape=[jax.ShapeDtypeStruct((heads, HDIM, piece), bf16)] * 3
        + [jax.ShapeDtypeStruct((piece, model), bf16)],
        compiler_params=pltpu.CompilerParams(vmem_limit_bytes=LIMIT),
        cost_estimate=pl.CostEstimate(
            flops=2 * piece * model * width, bytes_accessed=8 * 2**20, transcendentals=piece
        ),
        name="project",
    )(info, w, norm, bias, *x, *after)


def flip(place, others):
    return lax.rem(place, 2) * (others - 1)


def self_forward_kernel(heads, others, info, *refs):
    q_ref, id_ref = refs[:2]
    k_refs, v_refs = refs[2 : 2 + others], refs[2 + others : 2 + 2 * others]
    o_ref, l_ref, k_all, v_all = refs[-4:]
    beside = info[1]
    step = pl.program_id(0)
    piece_rows = q_ref.shape[2]
    per = piece_rows // TILE
    slot, tile = step // per, lax.rem(step, per)

    @pl.when(step == 0)
    def _():
        for other in range(others):
            for place in range(heads):
                k_all[other, place] = jnp.swapaxes(k_refs[other][place], 0, 1)
                v_all[other, place] = v_refs[other][place]

    piece = slot * others + jnp.bitwise_xor(beside, flip(slot, others))
    cols = pl.ds(pl.multiple_of(tile * TILE, TILE), TILE)
    q = q_ref[slot, :, cols]

    def update(state, k, v, mask):
        top, total, acc = state
        scores = dot(k, q, 1, 0)
        if mask is not None:
            scores = jnp.where(mask, scores, neg_large)
        new_top = jnp.maximum(top, jnp.max(scores, axis=0, keepdims=True))
        probs = jnp.exp(scores - new_top)
        fade = jnp.exp(top - new_top)
        total = total * fade + jnp.sum(probs, axis=0, keepdims=True)
        acc = acc * fade + dot(v, probs.astype(bf16), 1, 0)
        return new_top, total, acc

    def earlier_piece(index, state):
        place = index // others
        other = jnp.bitwise_xor(lax.rem(index, others), jnp.bitwise_xor(beside, flip(place, others)))
        return update(state, k_all[other, place], v_all[other, place], None)

    def earlier_tile(index, state):
        rows = pl.ds(pl.multiple_of(index * TILE, TILE), TILE)
        return update(state, k_all[0, slot, rows, :], v_all[0, slot, :, rows], None)

    state = (
        jnp.full((1, TILE), neg_large, f32),
        jnp.zeros((1, TILE), f32),
        jnp.zeros((HDIM, TILE), f32),
    )
    state = lax.fori_loop(0, piece, earlier_piece, state)
    state = lax.fori_loop(0, tile, earlier_tile, state)
    ids = id_ref[slot, :, cols]
    mask = column(ids, TILE) <= ids
    top, total, acc = update(state, k_all[0, slot, cols, :], v_all[0, slot, :, cols], mask)
    out = (acc / total).astype(o_ref.dtype)
    rows = o_ref.shape[2]
    for index in range(TILE // rows):
        place = (tile * (TILE // rows) + index) * heads + slot
        o_ref[place] = out[:, index * rows : (index + 1) * rows]
    l_ref[slot, :, cols] = top + jnp.log(total)


def self_forward(info, q, k, v, ids, rows, after):
    others = len(k)
    heads, depth, piece = q.shape
    area = heads * piece * heads * others * piece // 2
    return pl.pallas_call(
        functools.partial(self_forward_kernel, heads, others),
        grid_spec=pltpu.PrefetchScalarGridSpec(
            num_scalar_prefetch=1,
            grid=(heads * piece // TILE,),
            in_specs=[VMEM] * (2 + 2 * others) + [ANY] * len(after),
            out_specs=[VMEM] * 2,
            scratch_shapes=[
                pltpu.VMEM((others, heads, piece, depth), bf16),
                pltpu.VMEM((others, heads, depth, piece), bf16),
            ],
        ),
        out_shape=[
            jax.ShapeDtypeStruct((piece // rows * heads, depth, rows), bf16),
            jax.ShapeDtypeStruct((heads, 1, piece), f32),
        ],
        compiler_params=pltpu.CompilerParams(vmem_limit_bytes=LIMIT),
        cost_estimate=pl.CostEstimate(
            flops=area * 1024, bytes_accessed=8 * 2**20, transcendentals=area
        ),
        name="self_forward",
    )(info, q, ids, *k, *v, *after)


def self_backward_kernel(heads, sides, own, extra, info, *refs):
    refs = list(refs)
    q_ref, g_ref, o_ref, l_ref = refs[:4]
    k_refs, v_refs = refs[4 : 4 + sides], refs[4 + sides : 4 + 2 * sides]
    refs = refs[4 + 2 * sides :]
    id_ref, before_ref = (refs.pop(0), refs.pop(0)) if own else (None, None)
    dq_ref, dk_ref, dv_ref, g_all, inner_all, k_all, v_all, dk, dv = refs[extra:]
    beside = info[1]
    step = pl.program_id(0)
    piece_rows = q_ref.shape[2]
    per = piece_rows // TILE
    slot, tile = step // per, lax.rem(step, per)

    @pl.when(step == 0)
    def _():
        rows = g_ref.shape[2]
        for place in range(heads):
            for index in range(piece_rows // rows):
                at = slice(index * rows, (index + 1) * rows)
                grad = g_ref[index * heads + place]
                g_all[place, :, at] = grad
                inner_all[place, :, at] = jnp.sum(
                    o_ref[index * heads + place].astype(f32) * grad.astype(f32),
                    axis=0,
                    keepdims=True,
                )
            for side in range(sides):
                k_all[side, place] = jnp.swapaxes(k_refs[side][place], 0, 1)
                v_all[side, place] = jnp.swapaxes(v_refs[side][place], 0, 1)
        dk[...] = jnp.zeros_like(dk)
        dv[...] = jnp.zeros_like(dv)

    cols = pl.ds(pl.multiple_of(tile * TILE, TILE), TILE)
    q = q_ref[slot, :, cols]
    grad = g_all[slot, :, cols]
    q_rows = jnp.swapaxes(q, 0, 1)
    grad_rows = jnp.swapaxes(grad, 0, 1)
    log_total = l_ref[slot, :, cols]
    inner = inner_all[slot, :, cols]

    def update(dq, side, place, rows, mask):
        scores = dot(k_all[side, place, rows, :], q, 1, 0)
        if mask is not None:
            scores = jnp.where(mask, scores, neg_large)
        probs = jnp.exp(scores - log_total)
        grad_probs = dot(v_all[side, place, rows, :], grad, 1, 0)
        grad_scores = (probs * (grad_probs - inner)).astype(bf16)
        dv[side, place, rows, :] += dot(probs.astype(bf16), grad_rows, 1, 0)
        dk[side, place, rows, :] += dot(grad_scores, q_rows, 1, 0)
        return dq + dot(k_refs[side][place, :, rows], grad_scores, 1, 0)

    dq = before_ref[slot, :, cols] if own else jnp.zeros((HDIM, TILE), f32)
    for side in range(sides):

        def earlier(index, dq, side=side):
            rows = pl.ds(pl.multiple_of(lax.rem(index, per) * TILE, TILE), TILE)
            return update(dq, side, index // per, rows, None)

        if own:
            count = slot * per + tile
        else:
            here = jnp.bitwise_xor(beside, flip(slot, sides + 1))
            count = (slot + jnp.where(jnp.bitwise_xor(here, side + 1) < here, 1, 0)) * per
        dq = lax.fori_loop(0, count, earlier, dq)
    if own:
        ids = id_ref[slot, :, cols]
        mask = column(ids, TILE) <= ids
        dq = update(dq, 0, slot, cols, mask) * 0.125
    dq_ref[slot, :, cols] = dq.astype(dq_ref.dtype)

    @pl.when(step == heads * per - 1)
    def _():
        for side in range(sides):
            for place in range(heads):
                dk_ref[side, place] = jnp.swapaxes(dk[side, place], 0, 1).astype(dk_ref.dtype)
                dv_ref[side, place] = jnp.swapaxes(dv[side, place], 0, 1).astype(dv_ref.dtype)


def self_backward(info, q, k, v, ids, grad, context, log_total, before, after):
    own = ids is not None
    sides = len(k)
    heads, depth, piece = q.shape
    flat = [q, grad, context, log_total, *k, *v] + ([ids, before] if own else [])
    area = heads * piece * heads * sides * piece // 2
    return pl.pallas_call(
        functools.partial(self_backward_kernel, heads, sides, own, len(after)),
        grid_spec=pltpu.PrefetchScalarGridSpec(
            num_scalar_prefetch=1,
            grid=(heads * piece // TILE,),
            in_specs=[VMEM] * len(flat) + [ANY] * len(after),
            out_specs=[VMEM] * 3,
            scratch_shapes=[
                pltpu.VMEM((heads, depth, piece), bf16),
                pltpu.VMEM((heads, 1, piece), f32),
                pltpu.VMEM((sides, heads, piece, depth), bf16),
                pltpu.VMEM((sides, heads, piece, depth), bf16),
                pltpu.VMEM((sides, heads, piece, depth), f32),
                pltpu.VMEM((sides, heads, piece, depth), f32),
            ],
        ),
        out_shape=[jax.ShapeDtypeStruct((heads, depth, piece), bf16 if own else f32)]
        + [jax.ShapeDtypeStruct((sides, heads, depth, piece), f32 if own else bf16)] * 2,
        compiler_params=pltpu.CompilerParams(vmem_limit_bytes=LIMIT),
        cost_estimate=pl.CostEstimate(
            flops=area * 64, bytes_accessed=2**16, transcendentals=0
        ),
        name="self_backward",
    )(info, *flat, *after)


def gelu_parts(value):
    half = 0.5 * (1.0 + lax.erf(value * 0.7071067811865476))
    slope = half + value * jnp.exp(-0.5 * value * value) * 0.3989422804014327
    return value * half, slope


def middle_forward_kernel(group, heads, info, *refs):
    x_ref, ctx_ref, norm_ref, bias_ref = refs[:4]
    w_refs, kv_refs = refs[4 : 4 + group], refs[4 + group : 4 + 2 * group]
    x_two, unit_two, inv_two, unit_three, inv_three, h_two, h_three, ctx_xor, q, ctx, log = refs[-11:]
    width = heads * HDIM
    me = info[2]

    def natural(step):
        return pl.ds(pl.multiple_of(jnp.bitwise_xor(me, step) * width, width), width)

    resid = x_ref[...].astype(f32) + norm_ref[4:5, :]
    for step in range(group):
        part = ctx_ref[natural(step), :]
        ctx_xor[step * width : (step + 1) * width, :] = part
        resid = resid + dot(jnp.swapaxes(part, 0, 1), w_refs[step][0], 1, 1)
    unit, inverse = normalize(resid)
    unit_two[...] = unit
    inv_two[...] = inverse
    low = (unit * norm_ref[0:1, :] + norm_ref[1:2, :]).astype(bf16)
    h_two[...] = low
    for step in range(group):
        out = (dot(low, w_refs[step][2], 1, 0) + bias_ref[:, natural(step)]) * 0.125
        q[step * width : (step + 1) * width, :] = jnp.swapaxes(out.astype(bf16), 0, 1)
    resid = resid + norm_ref[5:6, :]
    for step in range(group):
        for head in range(heads):
            own = slice(head * HDIM, (head + 1) * HDIM)
            rows = slice(step * width + head * HDIM, step * width + (head + 1) * HDIM)
            scores = dot(jnp.swapaxes(kv_refs[step][0, own, :], 0, 1), q[rows, :], 1, 0)
            top = jnp.max(scores, axis=0, keepdims=True)
            probs = jnp.exp(scores - top)
            total = jnp.sum(probs, axis=0, keepdims=True)
            out = dot(kv_refs[step][1, own, :], probs.astype(bf16), 1, 0)
            ctx[rows, :] = (out / total).astype(bf16)
            log[step * heads + head] = top + jnp.log(total)
        part = ctx[step * width : (step + 1) * width, :]
        resid = resid + dot(jnp.swapaxes(part, 0, 1), w_refs[step][1], 1, 1)
    x_two[...] = resid
    unit, inverse = normalize(resid)
    unit_three[...] = unit
    inv_three[...] = inverse
    h_three[...] = (unit * norm_ref[2:3, :] + norm_ref[3:4, :]).astype(bf16)


def middle_forward(info, x, ctx, norm, bias, w, kv, heads, after):
    rows, model = x.shape
    group = len(w)
    total = ctx.shape[0]
    shapes = [
        jax.ShapeDtypeStruct((rows, model), f32),
        jax.ShapeDtypeStruct((rows, model), f32),
        jax.ShapeDtypeStruct((rows, 1), f32),
        jax.ShapeDtypeStruct((rows, model), f32),
        jax.ShapeDtypeStruct((rows, 1), f32),
        jax.ShapeDtypeStruct((rows, model), bf16),
        jax.ShapeDtypeStruct((rows, model), bf16),
        jax.ShapeDtypeStruct((total, rows), bf16),
        jax.ShapeDtypeStruct((total, rows), bf16),
        jax.ShapeDtypeStruct((total, rows), bf16),
        jax.ShapeDtypeStruct((total // HDIM, 1, rows), f32),
    ]
    return pl.pallas_call(
        functools.partial(middle_forward_kernel, group, heads),
        grid_spec=pltpu.PrefetchScalarGridSpec(
            num_scalar_prefetch=1,
            grid=(1,),
            in_specs=[VMEM] * (4 + 2 * group) + [ANY] * len(after),
            out_specs=[
                VMEM if index == 6 else pl.BlockSpec(shape.shape, lambda *_, n=len(shape.shape): (0,) * n)
                for index, shape in enumerate(shapes)
            ],
        ),
        out_shape=shapes,
        compiler_params=pltpu.CompilerParams(vmem_limit_bytes=LIMIT),
        cost_estimate=pl.CostEstimate(
            flops=6 * rows * model * total, bytes_accessed=12 * 2**20, transcendentals=2**20
        ),
        name="middle_forward",
    )(info, x, ctx, norm, bias, *w, *kv, *after)


def middle_backward_kernel(group, heads, extra, info, *refs):
    e_ref, cot_ref, unit_two, inv_two, unit_three, inv_three, norm_ref, q, ctx, log = refs[:10]
    w_refs, kv_refs = refs[10 : 10 + group], refs[10 + group : 10 + 2 * group]
    d_one, low_two, low_one, dq, dkv, d_ctx, sums = refs[10 + 2 * group + extra :]
    width = heads * HDIM
    me = info[2]

    def natural(step):
        return pl.ds(pl.multiple_of(jnp.bitwise_xor(me, step) * width, width), width)

    def add(row, value):
        sums[row : row + 1, :] = jnp.sum(value, axis=0, keepdims=True)

    def norm_back(grad, unit, inverse, gain, row):
        add(row, grad * unit)
        add(row + 1, grad)
        scaled = grad * gain
        return (
            scaled
            - jnp.mean(scaled, axis=-1, keepdims=True)
            - unit * jnp.mean(scaled * unit, axis=-1, keepdims=True)
        ) * inverse

    cot = cot_ref[...].astype(f32)
    d_two = cot + norm_back(e_ref[...], unit_three[...], inv_three[...], norm_ref[2:3, :], 0)
    low = d_two.astype(bf16)
    low_two[...] = low
    add(4, low.astype(f32))
    add(6, cot)
    e_two = jnp.zeros_like(d_two)
    for step in range(group):
        grads = jnp.swapaxes(dot(low, w_refs[step][1], 1, 0).astype(bf16), 0, 1)
        for head in range(heads):
            own = slice(head * HDIM, (head + 1) * HDIM)
            rows = slice(step * width + head * HDIM, step * width + (head + 1) * HDIM)
            grad = grads[own]
            inner = jnp.sum(ctx[rows, :].astype(f32) * grad.astype(f32), axis=0, keepdims=True)
            k_t = kv_refs[step][0, own, :]
            scores = dot(jnp.swapaxes(k_t, 0, 1), q[rows, :], 1, 0)
            probs = jnp.exp(scores - log[step * heads + head])
            grad_probs = dot(jnp.swapaxes(kv_refs[step][1, own, :], 0, 1), grad, 1, 0)
            grad_scores = (probs * (grad_probs - inner)).astype(bf16)
            dq[rows, :] = (dot(k_t, grad_scores, 1, 0) * 0.125).astype(bf16)
            dkv[step, 0, own, :] = dot(q[rows, :], grad_scores, 1, 1)
            dkv[step, 1, own, :] = dot(grad, probs.astype(bf16), 1, 1)
        part = jnp.swapaxes(dq[step * width : (step + 1) * width, :], 0, 1)
        sums[7:8, natural(step)] = jnp.sum(part.astype(f32), axis=0, keepdims=True)
        e_two = e_two + dot(part, w_refs[step][2], 1, 1)
    d_next = d_two + norm_back(e_two, unit_two[...], inv_two[...], norm_ref[0:1, :], 2)
    d_one[...] = d_next
    low = d_next.astype(bf16)
    low_one[...] = low
    add(5, low.astype(f32))
    for step in range(group):
        grads = dot(low, w_refs[step][0], 1, 0).astype(bf16)
        d_ctx[natural(step), :] = jnp.swapaxes(grads, 0, 1)


def middle_backward(info, e, cot, saved, norm, w, kv, heads, after):
    unit_two, inv_two, unit_three, inv_three, q, ctx, log = saved
    rows, model = cot.shape
    group = len(w)
    total = q.shape[0]
    enc = kv[0].shape[2]
    return pl.pallas_call(
        functools.partial(middle_backward_kernel, group, heads, len(after)),
        grid_spec=pltpu.PrefetchScalarGridSpec(
            num_scalar_prefetch=1,
            grid=(1,),
            in_specs=[VMEM] * (10 + 2 * group) + [ANY] * len(after),
            out_specs=[VMEM] * 7,
        ),
        out_shape=[
            jax.ShapeDtypeStruct((rows, model), f32),
            jax.ShapeDtypeStruct((rows, model), bf16),
            jax.ShapeDtypeStruct((rows, model), bf16),
            jax.ShapeDtypeStruct((total, rows), bf16),
            jax.ShapeDtypeStruct((group, 2, heads * HDIM, enc), f32),
            jax.ShapeDtypeStruct((total, rows), bf16),
            jax.ShapeDtypeStruct((8, model), f32),
        ],
        compiler_params=pltpu.CompilerParams(vmem_limit_bytes=LIMIT),
        cost_estimate=pl.CostEstimate(
            flops=6 * rows * model * total, bytes_accessed=16 * 2**20, transcendentals=2**20
        ),
        name="middle_backward",
    )(info, e, cot, unit_two, inv_two, unit_three, inv_three, norm, q, ctx, log, *w, *kv, *after)


CHUNK = 512


def grad_act_kernel(*refs):
    w_ref, out_ref = refs[-2:]
    rows = refs[0].shape[0]
    for index, ref in enumerate(refs[:-2]):
        for start in range(0, w_ref.shape[1], CHUNK):
            cols = slice(start, start + CHUNK)
            out_ref[index * rows : (index + 1) * rows, cols] = dot(
                ref[...], w_ref[:, cols], 1, 0
            ).astype(bf16)


def grad_act(cots, w):
    rows, ff = cots[0].shape[0] * len(cots), w.shape[1]
    return pl.pallas_call(
        grad_act_kernel,
        in_specs=[VMEM] * (len(cots) + 1),
        out_specs=VMEM,
        out_shape=jax.ShapeDtypeStruct((rows, ff), bf16),
        compiler_params=pltpu.CompilerParams(vmem_limit_bytes=LIMIT),
        cost_estimate=pl.CostEstimate(
            flops=2 * rows * ff * w.shape[0], bytes_accessed=10 * 2**20, transcendentals=0
        ),
        name="grad_act",
    )(*cots, w)


def feed_kernel(first, blocks, *refs):
    h_refs, (ga_ref, b_ref, w_ref) = refs[:blocks], refs[blocks : blocks + 3]
    refs = refs[blocks + 3 :]
    act_ref, du_ref, sum_ref, e_refs = refs[0], refs[1], refs[2], refs[3 : 3 + blocks]
    rows, ff = h_refs[0].shape[0], w_ref.shape[1]
    totals = [0.0] * blocks
    for start in range(0, ff, CHUNK):
        cols = slice(start, start + CHUNK)
        sums = 0.0
        for index in range(blocks):
            own = slice(index * rows, (index + 1) * rows)
            inner = dot(h_refs[index][...], w_ref[:, cols], 1, 0) + b_ref[:, cols]
            act, slope = gelu_parts(inner)
            act_ref[own, cols] = act.astype(bf16)
            there = slice((first + index) * rows, (first + index + 1) * rows)
            du = (slope * ga_ref[there, cols].astype(f32)).astype(bf16)
            du_ref[own, cols] = du
            sums = sums + jnp.sum(du.astype(f32), axis=0, keepdims=True)
            totals[index] = totals[index] + dot(du, w_ref[:, cols], 1, 1)
        sum_ref[:, cols] = sums
    for index in range(blocks):
        e_refs[index][...] = totals[index].astype(e_refs[index].dtype)


def feed(h, ga, w, bias, first):
    rows, model = h[0].shape
    ff = w.shape[1]
    blocks = len(h)
    return pl.pallas_call(
        functools.partial(feed_kernel, first, blocks),
        in_specs=[VMEM] * (blocks + 3),
        out_specs=[VMEM] * (3 + blocks),
        out_shape=[jax.ShapeDtypeStruct((blocks * rows, ff), bf16)] * 2
        + [jax.ShapeDtypeStruct((1, ff), f32)]
        + [
            jax.ShapeDtypeStruct((rows, model), bf16 if (first + index) % 2 else f32)
            for index in range(blocks)
        ],
        compiler_params=pltpu.CompilerParams(vmem_limit_bytes=LIMIT),
        cost_estimate=pl.CostEstimate(
            flops=4 * blocks * rows * ff * model, bytes_accessed=12 * 2**20, transcendentals=2**20
        ),
        name="feed",
    )(*h, ga, bias, w)


def outer_kernel(count, side, halves, extra, info, *refs):
    lefts, rights = refs[:count], refs[count : count + 2]
    got_ref = refs[count + 2] if extra else None
    out_ref, picked, turned = refs[-3:]
    rows, model = lefts[0].shape
    shard = out_ref.shape[0] // halves
    which = jnp.bitwise_xor(lax.rem(info[3], 2), side or 0)
    for index in range(count):
        own = slice(index * rows, (index + 1) * rows)
        if side is None:
            picked[:, own] = jnp.swapaxes(lefts[index][...], 0, 1)
            continue
        if shard % 128:
            turned[...] = jnp.swapaxes(lefts[index][...], 0, 1)
        for half in range(halves):
            start = pl.multiple_of((2 * half + which) * shard, shard)
            if shard % 128:
                part = turned[pl.ds(start, shard), :]
            else:
                part = jnp.swapaxes(lefts[index][:, pl.ds(start, shard)], 0, 1)
            picked[half * shard : (half + 1) * shard, own] = part
    middle = rights[0].shape[0]
    for start in range(0, out_ref.shape[1], CHUNK):
        cols = slice(start, start + CHUNK)
        out = dot(picked[:, :middle], rights[0][:, cols], 1, 0)
        out = out + dot(picked[:, middle:], rights[1][:, cols], 1, 0)
        if extra:
            out = out + got_ref[:, cols].astype(f32)
        out_ref[:, cols] = out.astype(bf16)


def outer(lefts, rights, info, side=None, halves=1, got=None):
    rows, model = lefts[0].shape
    count = len(lefts)
    ff = rights[0].shape[1]
    extra = [] if got is None else [got]
    size = model if side is None else model // 2
    return pl.pallas_call(
        functools.partial(outer_kernel, count, side, halves, len(extra)),
        grid_spec=pltpu.PrefetchScalarGridSpec(
            num_scalar_prefetch=1,
            grid=(1,),
            in_specs=[VMEM] * (count + 2 + len(extra)),
            out_specs=VMEM,
            scratch_shapes=[pltpu.VMEM((size, count * rows), bf16), pltpu.VMEM((model, rows), bf16)],
        ),
        out_shape=jax.ShapeDtypeStruct((size, ff), bf16),
        compiler_params=pltpu.CompilerParams(vmem_limit_bytes=LIMIT),
        cost_estimate=pl.CostEstimate(
            flops=2 * count * rows * ff * size, bytes_accessed=10 * 2**20, transcendentals=0
        ),
        name="outer",
    )(info, *lefts, *rights, *extra)


def middle_outer_kernel(group, *refs):
    one, ctx_one, two, ctx_two, h, dq = refs[:6]
    outs = refs[6:]
    width = dq.shape[0] // group
    for index, (left, right) in enumerate(((one, ctx_one), (two, ctx_two), (h, dq))):
        turned = jnp.swapaxes(left[...], 0, 1)
        cols = slice(index * width, (index + 1) * width)
        for step in range(group):
            part = right[step * width : (step + 1) * width, :]
            outs[step][:, cols] = dot(turned, part, 1, 1).astype(bf16)


def middle_outer(one, ctx_one, two, ctx_two, h, dq, group):
    rows, model = one.shape
    width = dq.shape[0] // group
    return pl.pallas_call(
        functools.partial(middle_outer_kernel, group),
        in_specs=[VMEM] * 6,
        out_specs=[VMEM] * group,
        out_shape=[jax.ShapeDtypeStruct((model, 3 * width), bf16)] * group,
        compiler_params=pltpu.CompilerParams(vmem_limit_bytes=LIMIT),
        cost_estimate=pl.CostEstimate(
            flops=6 * rows * model * model, bytes_accessed=9 * 2**20, transcendentals=0
        ),
        name="middle_outer",
    )(one, ctx_one, two, ctx_two, h, dq)


def combine_kernel(extra, *refs):
    dq, dk, dv = refs[:3]
    gots, out = refs[3:-1], refs[-1]
    gots = gots[: len(gots) - extra]
    out[:, 0] = dq[...]
    for index, value in enumerate((dk, dv)):
        total = value[0]
        for got in gots[index::2]:
            total = total + got[...].astype(f32)
        out[:, 1 + index] = total.astype(bf16)


def combine(dq, dk, dv, got_k, got_v, after):
    heads, depth, piece = dq.shape
    gots = [got for pair in zip(got_k, got_v) for got in pair]
    return pl.pallas_call(
        functools.partial(combine_kernel, len(after)),
        in_specs=[VMEM] * (3 + len(gots)) + [ANY] * len(after),
        out_specs=VMEM,
        out_shape=jax.ShapeDtypeStruct((heads, 3, depth, piece), bf16),
        compiler_params=pltpu.CompilerParams(vmem_limit_bytes=LIMIT),
        cost_estimate=pl.CostEstimate(flops=2**20, bytes_accessed=5 * 2**20, transcendentals=0),
        name="combine",
    )(dq, dk, dv, *gots, *after)


def local(
    hidden,
    encoder,
    cotangent,
    block_ids,
    self_qkv,
    self_out,
    cross_qkv,
    cross_out,
    up_weight,
    down_weight,
    proj_bias,
    up_bias,
    norm_gain,
    norm_shift,
):
    tok_size, group = lax.axis_size("tok"), lax.axis_size("hd")
    tok_index, me = lax.axis_index("tok"), lax.axis_index("hd")
    rows, model = hidden.shape
    shard = self_qkv.shape[0]
    width = self_qkv.shape[2]
    ff_local = up_weight.shape[1]
    piece_rows = rows * group
    span = SEQ // piece_rows
    heads = min(width // HDIM, span)
    others = span // heads
    assert heads * HDIM == width and heads * others == span
    seq_count, enc_rows, _ = encoder.shape
    enc_total = enc_rows * group
    own_seq = tok_index // span
    at = lax.rem(tok_index, span) // others
    beside = jnp.bitwise_xor(lax.rem(tok_index, others), lax.rem(at, 2) * (others - 1))
    info = jnp.stack([at, beside, me, tok_index]).astype(jnp.int32)

    def natural(blocks):
        stacked = jnp.stack(blocks)
        return [pick(stacked, me ^ index) for index in range(group)]

    even = lax.rem(tok_index, 2)
    halves = [[i for i in range(tok_size) if i % 2 == side] for side in range(2)]
    many = tok_size // 2

    def gather_half(block):
        return lax.all_gather(block, "tok", axis=0, tiled=True, axis_index_groups=halves)

    def gather_tok(block):
        return lax.all_gather(block, "tok", axis=0, tiled=True)

    def along_halves(block):
        return lax.all_to_all(
            jnp.broadcast_to(block[None], (many, *block.shape)),
            "tok", 0, 0, tiled=True, axis_index_groups=halves,
        )

    def merge_sides(own, got):
        sides = [jnp.where(even == 0, own, got), jnp.where(even == 0, got, own)]
        return jnp.stack(sides, 1).reshape(model, -1)

    w_self = self_qkv.reshape(shard, 3, heads, HDIM).transpose(0, 2, 1, 3)
    w_self = gather_tok(w_self.reshape(shard, 3 * width))
    w_mid = along_halves(
        jnp.concatenate([self_out.T, cross_out.T, cross_qkv.reshape(shard, 3 * width)], 1)
    )

    own_ids = lax.dynamic_slice_in_dim(block_ids, me * rows, rows).astype(bf16)
    small = jnp.concatenate(
        [
            proj_bias.T.reshape(-1),
            norm_gain.T.reshape(-1),
            norm_shift.T.reshape(-1),
            up_bias,
            own_ids,
        ]
    )
    total_devices = tok_size * group
    small_all = lax.all_to_all(
        jnp.broadcast_to(small[None], (total_devices, small.shape[0])),
        ("tok", "hd"), 0, 0, tiled=True,
    ).astype(f32)
    few = model // total_devices
    vectors = small_all[:, : 13 * few].reshape(total_devices, 13, few)
    vectors = vectors.transpose(1, 0, 2).reshape(13, model)
    bias, gain, shift = vectors[:7], vectors[7:10], vectors[10:13]
    few_up = up_bias.shape[0]
    bias_up = small_all[:, 13 * few : 13 * few + few_up].reshape(-1)
    bias_up = lax.dynamic_slice_in_dim(bias_up, me * ff_local, ff_local)
    ids = small_all[:, 13 * few + few_up :].reshape(tok_size, 1, piece_rows)
    ids = lax.dynamic_slice_in_dim(ids, own_seq * span, span).reshape(heads, others, 1, piece_rows)
    ids = jnp.stack([pick(ids[i], beside ^ (i % 2 * (others - 1))) for i in range(heads)])

    def own_columns(vector):
        return lax.dynamic_slice_in_dim(vector, me * width, width)

    hidden_blocks = gather_xor(hidden)
    self_bias = jnp.stack(
        [own_columns(bias[0]), jnp.zeros((width,), f32), own_columns(bias[1])]
    )
    scale = jnp.broadcast_to(jnp.array([0.125, 1.0, 1.0], f32)[:, None], (3, width))
    factors = jnp.stack([self_bias, scale]).reshape(2, 3, heads, HDIM)
    factors = factors.transpose(0, 2, 1, 3).reshape(2, 3 * width)

    lines = [
        [seq * span + i * others + (side ^ (i % 2 * (others - 1))) for i in range(heads)]
        for seq in range(tok_size // span)
        for side in range(others)
    ]
    wide_lines = [[i * group + h for h in range(group) for i in line] for line in lines]

    def across_lines(value):
        return lax.all_to_all(value, "tok", 0, 0, tiled=True, axis_index_groups=lines)

    def across_wide(value):
        return lax.all_to_all(
            value, ("tok", "hd"), 0, 0, tiled=True, axis_index_groups=wide_lines
        )

    q_out, k_out, v_out, h_one = project(
        info, hidden_blocks, w_self, jnp.stack([gain[0], shift[0]]), factors, heads, [w_mid]
    )
    w_up, w_down = tie([up_weight, down_weight], [h_one])
    w_up, w_down = gather_tok(w_up), gather_tok(w_down.T)
    w_mid = merge_sides(w_mid, swap(w_mid, "tok", 1))
    k = [across_lines(k_out)]
    v = [across_lines(v_out)]
    q = across_lines(q_out)
    k += [swap(k[0], "tok", other) for other in range(1, others)]
    v += [swap(v[0], "tok", other) for other in range(1, others)]
    w_cross_kv = w_mid[:, 3 * width :]
    enc_all = jnp.concatenate(natural(gather_xor(encoder)), 1)
    kv_bias = jnp.concatenate([jnp.zeros((width,), f32), own_columns(bias[4])])
    kv_two = dot(w_cross_kv, pick(enc_all, own_seq), 0, 1) + kv_bias[:, None]
    kv_two = kv_two.astype(bf16).reshape(2, width, enc_total)
    kv_two = gather_xor(kv_two)

    context, log_one = self_forward(info, q, k, v, ids, rows, kv_two)

    mid_block = jnp.stack(
        [w_mid[:, :width], w_mid[:, width : 2 * width], w_mid[:, 2 * width : 3 * width]]
    )
    w_blocks = gather_xor(mid_block, lambda value: tie([value], [log_one])[0])
    ctx_one = across_wide(context).reshape(model, rows)
    norm_rows = jnp.stack([gain[1], shift[1], gain[2], shift[2], bias[2], bias[5]])
    (
        resid_two, unit_two, inv_two, unit_three, inv_three,
        h_two, h_three, ctx_one, q_two, ctx_two, log_two,
    ) = middle_forward(
        info, hidden, ctx_one, norm_rows, bias[3:4], w_blocks, kv_two, heads, []
    )

    cot_blocks = gather_xor(cotangent)
    h_blocks = gather_xor(h_three)
    grad_a = grad_act(cot_blocks, w_down)
    near = group // 2
    bias_row = bias_up[None]
    near_out = feed(h_blocks[:near], grad_a, w_up, bias_row, 0)
    far_out = feed(h_blocks[near:], grad_a, w_up, bias_row, near)
    acts, grad_inners = [near_out[0], far_out[0]], [near_out[1], far_out[1]]
    up_sums = (near_out[2] + far_out[2])[0]
    grad_h_three = reduce_xor(list(near_out[3:]) + list(far_out[3:]))

    def half_columns(array, side):
        return jnp.concatenate(
            [
                lax.dynamic_slice_in_dim(array, (2 * i + side) * shard, shard, 1)
                for i in range(tok_size // 2)
            ],
            1,
        )

    def half_rows(array, side):
        return jnp.concatenate(
            [
                lax.dynamic_slice_in_dim(array, (2 * i + side) * shard, shard, 0)
                for i in range(tok_size // 2)
            ],
            0,
        )

    def reduce_tok(value):
        return lax.psum_scatter(value, "tok", scatter_dimension=0, tiled=True).astype(f32)

    def reduce_half(value):
        return lax.psum_scatter(
            value, "tok", scatter_dimension=0, tiled=True, axis_index_groups=halves
        ).astype(f32)

    grad_up = outer(h_blocks, grad_inners, info)
    down_away = outer(cot_blocks, acts, info, 1, many)
    sent_up = reduce_tok(grad_up)
    down_got = swap(down_away, "tok", 1)

    grad_one, grad_two_low, grad_one_low, grad_q_two, grad_kv_two, grad_ctx_one, sums = (
        middle_backward(
            info, grad_h_three, cotangent,
            (unit_two, inv_two, unit_three, inv_three, q_two, ctx_two, log_two),
            norm_rows, w_blocks, kv_two, heads, [grad_up, down_away],
        )
    )
    grad_heads = across_wide(grad_ctx_one.reshape(group * heads, HDIM, rows))
    grad_mid = middle_outer(
        grad_one_low, ctx_one, grad_two_low, ctx_two, h_two, grad_q_two, group
    )
    masks = [1 << bit for bit in range(tok_size.bit_length() - 1)]

    def add_low(value, got):
        return (value.astype(f32) + got.astype(f32)).astype(bf16)

    grad_q_away, grad_k_away, grad_v_away = self_backward(
        info, q, k[1:], v[1:], None, grad_heads, context, log_one, None, grad_mid
    )
    down_got = tie([down_got], [grad_q_away])[0]
    down_sum = outer(cot_blocks, acts, info, 0, many, down_got)
    sent_down = reduce_half(tie([down_sum], [sent_up])[0]).T
    kv_total = reduce_xor(
        [grad_kv_two[j] for j in range(group)], lambda got: tie([got], [grad_q_away])[0]
    )
    seq_pick = jnp.arange(seq_count) == own_seq
    kv_total = jnp.where(seq_pick[:, None, None, None], kv_total[None], 0.0).astype(bf16)
    grad_mid = reduce_xor(grad_mid, lambda got: tie([got], [grad_q_away])[0])
    mid_got = swap(half_rows(grad_mid, 1 - even).astype(bf16), "tok", 1)
    mid_sum = (half_rows(grad_mid, even) + mid_got.astype(f32)).astype(bf16)
    sent_mid = reduce_half(tie([mid_sum], [sent_down])[0])
    grad_k_got = [swap(grad_k_away[i], "tok", i + 1) for i in range(others - 1)]
    grad_v_got = [swap(grad_v_away[i], "tok", i + 1) for i in range(others - 1)]
    grad_q, grad_k, grad_v = self_backward(
        info, q, k[:1], v[:1], ids, grad_heads, context, log_one, grad_q_away, [down_sum]
    )
    kv_got = swap(kv_total, "tok", masks[0])
    grad_qkv = combine(grad_q, grad_k, grad_v, grad_k_got, grad_v_got, [sent_up, kv_got])
    kv_total = add_low(kv_total, kv_got)
    acts = tie(acts, [grad_q])
    def act_block(index):
        start = index % near * rows
        return acts[index // near][start : start + rows]

    final = reduce_xor([dot(act_block(j), w_down, 1, 1) for j in range(group)])
    output = (resid_two + final + bias[6]).astype(bf16)
    grad_qkv = across_lines(grad_qkv).reshape(3 * width, piece_rows)
    kv_got = swap(kv_total, "tok", masks[1])
    grad_qkv, sent_down, kv_got = tie([grad_qkv, sent_down, kv_got], [])
    kv_total = add_low(kv_total, kv_got)
    for got_mask in masks[2:]:
        kv_total = add_low(kv_total, swap(kv_total, "tok", got_mask))
    kv_flat = kv_total.reshape(seq_count, 2 * width, enc_total)
    own_enc = lax.dynamic_slice_in_dim(enc_all, tok_index * shard, shard, 2)
    sent_cross_kv = sum(dot(own_enc[n], kv_flat[n], 0, 1) for n in range(seq_count))

    def encoder_part(index):
        start = (me ^ index) * enc_rows
        return jnp.stack(
            [
                dot(lax.dynamic_slice_in_dim(kv_flat[n], start, enc_rows, 1), w_cross_kv, 0, 1)
                for n in range(seq_count)
            ]
        )

    grad_encoder = reduce_xor([encoder_part(j) for j in range(group)])

    grad_h_one = reduce_xor(
        [
            dot(
                lax.dynamic_slice(grad_qkv, (0, (me ^ j) * rows), (3 * width, rows)), w_self, 0, 1
            )
            for j in range(group)
        ]
    )
    grad_self = dot(h_one, grad_qkv, 0, 1).astype(bf16)
    sent_self = lax.all_to_all(grad_self, "tok", 0, 0, tiled=True)
    ordered = sent_self
    sent_self = jnp.sum(sent_self.reshape(tok_size, shard, 3 * width).astype(f32), 0)
    sent_self = sent_self.reshape(shard, heads, 3, HDIM)
    sent_self = sent_self.transpose(0, 2, 1, 3).reshape(shard, 3, width)
    unit_one, inverse_one = normalize(hidden.astype(f32))
    back, gain_one, shift_one = norm_backward(grad_h_one, unit_one, inverse_one, gain[0])
    grad_hidden = grad_one + back

    def place(vector):
        return lax.dynamic_update_slice_in_dim(jnp.zeros((model,), f32), vector, me * width, 0)

    qkv_sums = jnp.sum(grad_qkv.astype(f32), 1).reshape(heads, 3, HDIM)
    once = (tok_index == 0).astype(f32)
    late = jnp.concatenate(
        [
            place(qkv_sums[:, 0].reshape(-1)),
            place(qkv_sums[:, 2].reshape(-1)),
            place(jnp.sum(kv_flat[:, width:].astype(f32), (0, 2)) * once),
            gain_one,
            shift_one,
        ]
    )
    vectors = jnp.concatenate([sums, late.reshape(5, model)], 0)
    vectors = vectors.reshape(13, total_devices, few).transpose(1, 0, 2).reshape(total_devices, -1)
    up_all = lax.dynamic_update_slice_in_dim(
        jnp.zeros((group * ff_local,), f32), up_sums, me * ff_local, 0
    )
    vectors = jnp.concatenate([vectors, up_all.reshape(total_devices, -1)], 1)
    vectors = tie([vectors], [ordered])[0]
    vectors = jnp.sum(lax.all_to_all(vectors, ("tok", "hd"), 0, 0, tiled=True), 0)
    columns = vectors[: 13 * few].reshape(13, few)
    columns = columns[jnp.array([8, 9, 5, 7, 10, 4, 6, 11, 2, 0, 12, 3, 1])].T

    sent_mid = [sent_mid[:, j * width : (j + 1) * width] for j in range(3)]
    sent_cross = jnp.concatenate(
        [sent_mid[2][:, None], sent_cross_kv.reshape(shard, 2, width)], 1
    )
    return (
        output,
        grad_hidden,
        grad_encoder,
        sent_self,
        sent_mid[0].T,
        sent_cross,
        sent_mid[1].T,
        sent_up,
        sent_down,
        columns[:, :7],
        vectors[13 * few :],
        columns[:, 7:10],
        columns[:, 10:13],
    )


def solution(mesh):
    in_specs = (
        P(("tok", "hd"), None),
        P(None, "hd", None),
        P(("tok", "hd"), None),
        P("tok"),
        P("tok", None, "hd"),
        P("hd", "tok"),
        P("tok", None, "hd"),
        P("hd", "tok"),
        P("tok", "hd"),
        P("hd", "tok"),
        P(("tok", "hd"), None),
        P(("tok", "hd")),
        P(("tok", "hd"), None),
        P(("tok", "hd"), None),
    )
    out_specs = (
        P(("tok", "hd"), None),
        P(("tok", "hd"), None),
        P(None, "hd", None),
        P("tok", None, "hd"),
        P("hd", "tok"),
        P("tok", None, "hd"),
        P("hd", "tok"),
        P("tok", "hd"),
        P("hd", "tok"),
        P(("tok", "hd"), None),
        P(("tok", "hd")),
        P(("tok", "hd"), None),
        P(("tok", "hd"), None),
    )
    return jax.shard_map(local, mesh=mesh, in_specs=in_specs, out_specs=out_specs, check_vma=False)
```

```python
import functools

import jax
import jax.numpy as jnp
from jax import lax
from jax.experimental import pallas as pl
from jax.experimental.pallas import tpu as pltpu
from jax.sharding import PartitionSpec as P

HDIM = 64
SEQ = 8192
TILE = 512
norm_eps = 1e-05
neg_large = -1e30
f32 = jnp.float32
bf16 = jnp.bfloat16


def dot(left, right, left_dim, right_dim):
    return lax.dot_general(
        left, right, (((left_dim,), (right_dim,)), ((), ())), preferred_element_type=f32
    )


def swap(value, axis, mask):
    return lax.ppermute(value, axis, [(i, i ^ mask) for i in range(lax.axis_size(axis))])


def hd_masks():
    mask, masks = lax.axis_size("hd") // 2, []
    while mask:
        masks.append(mask)
        mask //= 2
    return masks


def gather_xor(value, first=lambda value: value):
    have = {0: value}
    for mask in hd_masks():
        for index in list(have):
            have[index ^ mask] = first(swap(have[index], "hd", mask))
        first = lambda value: value
    return [have[index] for index in range(len(have))]


def reduce_xor(parts, last=lambda value: value):
    have = dict(enumerate(parts))
    for mask in reversed(hd_masks()):
        for index in sorted(have, reverse=True):
            if index & mask:
                got = swap(have.pop(index).astype(bf16), "hd", mask)
                if len(have) == 1:
                    got = last(got)
                total = have[index ^ mask].astype(f32) + got.astype(f32)
                have[index ^ mask] = total if len(have) == 1 else total.astype(bf16)
    return have[0]


def pick(stacked, index):
    return lax.dynamic_index_in_dim(stacked, index, 0, keepdims=False)


def normalize(value):
    center = value - jnp.mean(value, axis=-1, keepdims=True)
    inverse = lax.rsqrt(jnp.mean(center * center, axis=-1, keepdims=True) + norm_eps)
    return center * inverse, inverse


def norm_backward(grad, unit, inverse, gain):
    scaled = grad * gain
    back = (
        scaled
        - jnp.mean(scaled, axis=-1, keepdims=True)
        - unit * jnp.mean(scaled * unit, axis=-1, keepdims=True)
    ) * inverse
    return back, jnp.sum(grad * unit, axis=0), jnp.sum(grad, axis=0)


def column(row, rows):
    return jnp.swapaxes(jnp.broadcast_to(row, (128, rows)), 0, 1)[:, :1]


VMEM = pl.BlockSpec(memory_space=pltpu.VMEM)
LIMIT = 48 * 2**20


ANY = pl.BlockSpec(memory_space=pl.ANY)


def tie(values, after):
    count = len(values)
    return pl.pallas_call(
        lambda *refs: None,
        in_specs=[ANY] * (count + len(after)),
        out_specs=[ANY] * count,
        out_shape=[jax.ShapeDtypeStruct(value.shape, value.dtype) for value in values],
        input_output_aliases={index: index for index in range(count)},
        name="tie",
    )(*values, *after)


def project_kernel(heads, group, info, *refs):
    refs = list(refs)
    w_ref, norm_ref, bias_ref = refs[:3]
    q_ref, k_ref, v_ref, h_ref = refs[-4:]
    x_refs = refs[3 : 3 + group]
    rows = x_refs[0].shape[0]
    for step, x_ref in enumerate(x_refs):
        start = pl.multiple_of(jnp.bitwise_xor(info[2], step) * rows, rows)
        cols = pl.ds(start, rows)
        x = x_ref[...].astype(f32)
        h = (normalize(x)[0] * norm_ref[0:1, :] + norm_ref[1:2, :]).astype(bf16)
        h_ref[cols, :] = h
        out = (dot(h, w_ref[...], 1, 0) + bias_ref[0:1, :]) * bias_ref[1:2, :]
        out = jnp.swapaxes(out.astype(bf16), 0, 1)
        for head in range(heads):
            for part, ref in enumerate((q_ref, k_ref, v_ref)):
                first = (head * 3 + part) * HDIM
                ref[head, :, cols] = out[first : first + HDIM]


def project(info, x, w, norm, bias, heads, after):
    rows, model = x[0].shape
    group = len(x)
    piece = rows * group
    width = w.shape[1]
    return pl.pallas_call(
        functools.partial(project_kernel, heads, group),
        grid_spec=pltpu.PrefetchScalarGridSpec(
            num_scalar_prefetch=1,
            grid=(1,),
            in_specs=[VMEM] * (group + 3) + [ANY] * len(after),
            out_specs=[VMEM] * 4,
        ),
        out_shape=[jax.ShapeDtypeStruct((heads, HDIM, piece), bf16)] * 3
        + [jax.ShapeDtypeStruct((piece, model), bf16)],
        compiler_params=pltpu.CompilerParams(vmem_limit_bytes=LIMIT),
        cost_estimate=pl.CostEstimate(
            flops=2 * piece * model * width, bytes_accessed=8 * 2**20, transcendentals=piece
        ),
        name="project",
    )(info, w, norm, bias, *x, *after)


def flip(place, others):
    return lax.rem(place, 2) * (others - 1)


def self_forward_kernel(heads, others, info, *refs):
    q_ref, id_ref = refs[:2]
    k_refs, v_refs = refs[2 : 2 + others], refs[2 + others : 2 + 2 * others]
    o_ref, l_ref, k_all, v_all, wait_a, wait_b = refs[-6:]
    beside = info[1]
    step = pl.program_id(0)
    piece_rows = q_ref.shape[2]
    assert piece_rows == 2 * TILE
    per = piece_rows // TILE
    slot, tile = step // per, lax.rem(step, per)

    @pl.when(step == 0)
    def _():
        for other in range(others):
            for place in range(heads):
                k_all[other, place] = jnp.swapaxes(k_refs[other][place], 0, 1)
                v_all[other, place] = v_refs[other][place]

    piece = slot * others + jnp.bitwise_xor(beside, flip(slot, others))
    cols = pl.ds(pl.multiple_of(tile * TILE, TILE), TILE)
    q = q_ref[slot, :, cols]

    def ahead(wait, keys, top, mask=None):
        scores = dot(keys, q, 1, 0)
        if mask is not None:
            scores = jnp.where(mask, scores, neg_large)
        wait[...] = scores
        return jnp.maximum(top, jnp.max(scores, axis=0, keepdims=True))

    def finish(wait, values, top, fade, total, acc):
        probs = jnp.exp(wait[...] - top)
        total = total * fade + jnp.sum(probs, axis=0, keepdims=True)
        return total, acc * fade + dot(values, probs.astype(bf16), 1, 0)

    def locate(index):
        place = index // others
        side = jnp.bitwise_xor(beside, flip(place, others))
        return jnp.bitwise_xor(lax.rem(index, others), side), place

    def waiting(index):
        other, place = locate(jnp.maximum(index - 1, 0))
        other, place = jnp.where(index == 0, 0, other), jnp.where(index == 0, slot, place)
        start = jnp.where(index == 0, 0, TILE)
        return v_all[other, place, :, pl.ds(pl.multiple_of(start, TILE), TILE)]

    def earlier_tile(state):
        top, fade, total, acc = state
        new_top = ahead(wait_b, k_all[0, slot, :TILE, :], top)
        total, acc = finish(wait_a, v_all[0, slot, :, cols], top, fade, total, acc)
        wait_a[...] = wait_b[...]
        return new_top, jnp.exp(top - new_top), total, acc

    def earlier_piece(index, state):
        top, fade, total, acc = state
        other, place = locate(index)
        new_top = ahead(wait_b, k_all[other, place, :TILE, :], top)
        total, acc = finish(wait_a, waiting(index), top, fade, total, acc)
        fade, top = jnp.exp(top - new_top), new_top
        new_top = ahead(wait_a, k_all[other, place, TILE:, :], top)
        total, acc = finish(wait_b, v_all[other, place, :, :TILE], top, fade, total, acc)
        return new_top, jnp.exp(top - new_top), total, acc

    ids = id_ref[slot, :, cols]
    mask = column(ids, TILE) <= ids
    top = ahead(wait_a, k_all[0, slot, cols, :], jnp.full((1, TILE), neg_large, f32), mask)
    state = (
        top,
        jnp.ones((1, TILE), f32),
        jnp.zeros((1, TILE), f32),
        jnp.zeros((HDIM, TILE), f32),
    )
    state = lax.cond(tile == 1, earlier_tile, lambda state: state, state)
    top, fade, total, acc = lax.fori_loop(0, piece, earlier_piece, state)
    total, acc = finish(wait_a, waiting(piece), top, fade, total, acc)
    out = (acc / total).astype(o_ref.dtype)
    rows = o_ref.shape[2]
    for index in range(TILE // rows):
        place = (tile * (TILE // rows) + index) * heads + slot
        o_ref[place] = out[:, index * rows : (index + 1) * rows]
    l_ref[slot, :, cols] = top + jnp.log(total)


def self_forward(info, q, k, v, ids, rows, after):
    others = len(k)
    heads, depth, piece = q.shape
    area = heads * piece * heads * others * piece // 2
    return pl.pallas_call(
        functools.partial(self_forward_kernel, heads, others),
        grid_spec=pltpu.PrefetchScalarGridSpec(
            num_scalar_prefetch=1,
            grid=(heads * piece // TILE,),
            in_specs=[VMEM] * (2 + 2 * others) + [ANY] * len(after),
            out_specs=[VMEM] * 2,
            scratch_shapes=[
                pltpu.VMEM((others, heads, piece, depth), bf16),
                pltpu.VMEM((others, heads, depth, piece), bf16),
                pltpu.VMEM((TILE, TILE), f32),
                pltpu.VMEM((TILE, TILE), f32),
            ],
        ),
        out_shape=[
            jax.ShapeDtypeStruct((piece // rows * heads, depth, rows), bf16),
            jax.ShapeDtypeStruct((heads, 1, piece), f32),
        ],
        compiler_params=pltpu.CompilerParams(vmem_limit_bytes=LIMIT),
        cost_estimate=pl.CostEstimate(
            flops=area * 1024, bytes_accessed=8 * 2**20, transcendentals=area
        ),
        name="self_forward",
    )(info, q, ids, *k, *v, *after)


def self_backward_kernel(heads, sides, own, extra, info, *refs):
    refs = list(refs)
    q_ref, g_ref, o_ref, l_ref = refs[:4]
    k_refs, v_refs = refs[4 : 4 + sides], refs[4 + sides : 4 + 2 * sides]
    refs = refs[4 + 2 * sides :]
    id_ref, before_ref = (refs.pop(0), refs.pop(0)) if own else (None, None)
    dq_ref, dk_ref, dv_ref, g_all, inner_all, k_all, v_all, dk, dv = refs[extra:]
    beside = info[1]
    step = pl.program_id(0)
    piece_rows = q_ref.shape[2]
    per = piece_rows // TILE
    slot, tile = step // per, lax.rem(step, per)

    @pl.when(step == 0)
    def _():
        rows = g_ref.shape[2]
        for place in range(heads):
            for index in range(piece_rows // rows):
                at = slice(index * rows, (index + 1) * rows)
                grad = g_ref[index * heads + place]
                g_all[place, :, at] = grad
                inner_all[place, :, at] = jnp.sum(
                    o_ref[index * heads + place].astype(f32) * grad.astype(f32),
                    axis=0,
                    keepdims=True,
                )
            for side in range(sides):
                k_all[side, place] = jnp.swapaxes(k_refs[side][place], 0, 1)
                v_all[side, place] = jnp.swapaxes(v_refs[side][place], 0, 1)
        dk[...] = jnp.zeros_like(dk)
        dv[...] = jnp.zeros_like(dv)

    cols = pl.ds(pl.multiple_of(tile * TILE, TILE), TILE)
    q = q_ref[slot, :, cols]
    grad = g_all[slot, :, cols]
    q_rows = jnp.swapaxes(q, 0, 1)
    grad_rows = jnp.swapaxes(grad, 0, 1)
    log_total = l_ref[slot, :, cols]
    inner = inner_all[slot, :, cols]

    def update(dq, side, place, rows, mask):
        scores = dot(k_all[side, place, rows, :], q, 1, 0)
        if mask is not None:
            scores = jnp.where(mask, scores, neg_large)
        probs = jnp.exp(scores - log_total)
        grad_probs = dot(v_all[side, place, rows, :], grad, 1, 0)
        grad_scores = (probs * (grad_probs - inner)).astype(bf16)
        dv[side, place, rows, :] += dot(probs.astype(bf16), grad_rows, 1, 0)
        dk[side, place, rows, :] += dot(grad_scores, q_rows, 1, 0)
        return dq + dot(k_refs[side][place, :, rows], grad_scores, 1, 0)

    dq = before_ref[slot, :, cols] if own else jnp.zeros((HDIM, TILE), f32)
    for side in range(sides):

        def earlier(index, dq, side=side):
            rows = pl.ds(pl.multiple_of(lax.rem(index, per) * TILE, TILE), TILE)
            return update(dq, side, index // per, rows, None)

        if own:
            count = slot * per + tile
        else:
            here = jnp.bitwise_xor(beside, flip(slot, sides + 1))
            count = (slot + jnp.where(jnp.bitwise_xor(here, side + 1) < here, 1, 0)) * per
        dq = lax.fori_loop(0, count, earlier, dq)
    if own:
        ids = id_ref[slot, :, cols]
        mask = column(ids, TILE) <= ids
        dq = update(dq, 0, slot, cols, mask) * 0.125
    dq_ref[slot, :, cols] = dq.astype(dq_ref.dtype)

    @pl.when(step == heads * per - 1)
    def _():
        for side in range(sides):
            for place in range(heads):
                dk_ref[side, place] = jnp.swapaxes(dk[side, place], 0, 1).astype(dk_ref.dtype)
                dv_ref[side, place] = jnp.swapaxes(dv[side, place], 0, 1).astype(dv_ref.dtype)


def self_backward(info, q, k, v, ids, grad, context, log_total, before, after):
    own = ids is not None
    sides = len(k)
    heads, depth, piece = q.shape
    flat = [q, grad, context, log_total, *k, *v] + ([ids, before] if own else [])
    area = heads * piece * heads * sides * piece // 2
    return pl.pallas_call(
        functools.partial(self_backward_kernel, heads, sides, own, len(after)),
        grid_spec=pltpu.PrefetchScalarGridSpec(
            num_scalar_prefetch=1,
            grid=(heads * piece // TILE,),
            in_specs=[VMEM] * len(flat) + [ANY] * len(after),
            out_specs=[VMEM] * 3,
            scratch_shapes=[
                pltpu.VMEM((heads, depth, piece), bf16),
                pltpu.VMEM((heads, 1, piece), f32),
                pltpu.VMEM((sides, heads, piece, depth), bf16),
                pltpu.VMEM((sides, heads, piece, depth), bf16),
                pltpu.VMEM((sides, heads, piece, depth), f32),
                pltpu.VMEM((sides, heads, piece, depth), f32),
            ],
        ),
        out_shape=[jax.ShapeDtypeStruct((heads, depth, piece), bf16 if own else f32)]
        + [jax.ShapeDtypeStruct((sides, heads, depth, piece), f32 if own else bf16)] * 2,
        compiler_params=pltpu.CompilerParams(vmem_limit_bytes=LIMIT),
        cost_estimate=pl.CostEstimate(
            flops=area * 64, bytes_accessed=2**16, transcendentals=0
        ),
        name="self_backward",
    )(info, *flat, *after)


def gelu_parts(value):
    half = 0.5 * (1.0 + lax.erf(value * 0.7071067811865476))
    slope = half + value * jnp.exp(-0.5 * value * value) * 0.3989422804014327
    return value * half, slope


def middle_forward_kernel(group, heads, info, *refs):
    x_ref, ctx_ref, norm_ref, bias_ref = refs[:4]
    w_refs, kv_refs = refs[4 : 4 + group], refs[4 + group : 4 + 2 * group]
    x_two, unit_two, inv_two, unit_three, inv_three, h_two, h_three, ctx_xor, q, ctx, log = refs[-11:]
    width = heads * HDIM
    me = info[2]

    def natural(step):
        return pl.ds(pl.multiple_of(jnp.bitwise_xor(me, step) * width, width), width)

    resid = x_ref[...].astype(f32) + norm_ref[4:5, :]
    for step in range(group):
        part = ctx_ref[natural(step), :]
        ctx_xor[step * width : (step + 1) * width, :] = part
        resid = resid + dot(jnp.swapaxes(part, 0, 1), w_refs[step][0], 1, 1)
    unit, inverse = normalize(resid)
    unit_two[...] = unit
    inv_two[...] = inverse
    low = (unit * norm_ref[0:1, :] + norm_ref[1:2, :]).astype(bf16)
    h_two[...] = low
    for step in range(group):
        out = (dot(low, w_refs[step][2], 1, 0) + bias_ref[:, natural(step)]) * 0.125
        q[step * width : (step + 1) * width, :] = jnp.swapaxes(out.astype(bf16), 0, 1)
    resid = resid + norm_ref[5:6, :]
    for step in range(group):
        for head in range(heads):
            own = slice(head * HDIM, (head + 1) * HDIM)
            rows = slice(step * width + head * HDIM, step * width + (head + 1) * HDIM)
            scores = dot(jnp.swapaxes(kv_refs[step][0, own, :], 0, 1), q[rows, :], 1, 0)
            top = jnp.max(scores, axis=0, keepdims=True)
            probs = jnp.exp(scores - top)
            total = jnp.sum(probs, axis=0, keepdims=True)
            out = dot(kv_refs[step][1, own, :], probs.astype(bf16), 1, 0)
            ctx[rows, :] = (out / total).astype(bf16)
            log[step * heads + head] = top + jnp.log(total)
        part = ctx[step * width : (step + 1) * width, :]
        resid = resid + dot(jnp.swapaxes(part, 0, 1), w_refs[step][1], 1, 1)
    x_two[...] = resid
    unit, inverse = normalize(resid)
    unit_three[...] = unit
    inv_three[...] = inverse
    h_three[...] = (unit * norm_ref[2:3, :] + norm_ref[3:4, :]).astype(bf16)


def middle_forward(info, x, ctx, norm, bias, w, kv, heads, after):
    rows, model = x.shape
    group = len(w)
    total = ctx.shape[0]
    shapes = [
        jax.ShapeDtypeStruct((rows, model), f32),
        jax.ShapeDtypeStruct((rows, model), f32),
        jax.ShapeDtypeStruct((rows, 1), f32),
        jax.ShapeDtypeStruct((rows, model), f32),
        jax.ShapeDtypeStruct((rows, 1), f32),
        jax.ShapeDtypeStruct((rows, model), bf16),
        jax.ShapeDtypeStruct((rows, model), bf16),
        jax.ShapeDtypeStruct((total, rows), bf16),
        jax.ShapeDtypeStruct((total, rows), bf16),
        jax.ShapeDtypeStruct((total, rows), bf16),
        jax.ShapeDtypeStruct((total // HDIM, 1, rows), f32),
    ]
    return pl.pallas_call(
        functools.partial(middle_forward_kernel, group, heads),
        grid_spec=pltpu.PrefetchScalarGridSpec(
            num_scalar_prefetch=1,
            grid=(1,),
            in_specs=[VMEM] * (4 + 2 * group) + [ANY] * len(after),
            out_specs=[
                VMEM if index == 6 else pl.BlockSpec(shape.shape, lambda *_, n=len(shape.shape): (0,) * n)
                for index, shape in enumerate(shapes)
            ],
        ),
        out_shape=shapes,
        compiler_params=pltpu.CompilerParams(vmem_limit_bytes=LIMIT),
        cost_estimate=pl.CostEstimate(
            flops=6 * rows * model * total, bytes_accessed=12 * 2**20, transcendentals=2**20
        ),
        name="middle_forward",
    )(info, x, ctx, norm, bias, *w, *kv, *after)


def middle_backward_kernel(group, heads, extra, info, *refs):
    e_ref, cot_ref, unit_two, inv_two, unit_three, inv_three, norm_ref, q, ctx, log = refs[:10]
    w_refs, kv_refs = refs[10 : 10 + group], refs[10 + group : 10 + 2 * group]
    d_one, low_two, low_one, dq, dkv, d_ctx, sums = refs[10 + 2 * group + extra :]
    width = heads * HDIM
    me = info[2]

    def natural(step):
        return pl.ds(pl.multiple_of(jnp.bitwise_xor(me, step) * width, width), width)

    def add(row, value):
        sums[row : row + 1, :] = jnp.sum(value, axis=0, keepdims=True)

    def norm_back(grad, unit, inverse, gain, row):
        add(row, grad * unit)
        add(row + 1, grad)
        scaled = grad * gain
        return (
            scaled
            - jnp.mean(scaled, axis=-1, keepdims=True)
            - unit * jnp.mean(scaled * unit, axis=-1, keepdims=True)
        ) * inverse

    cot = cot_ref[...].astype(f32)
    d_two = cot + norm_back(e_ref[...], unit_three[...], inv_three[...], norm_ref[2:3, :], 0)
    low = d_two.astype(bf16)
    low_two[...] = low
    add(4, low.astype(f32))
    add(6, cot)
    e_two = jnp.zeros_like(d_two)
    for step in range(group):
        grads = jnp.swapaxes(dot(low, w_refs[step][1], 1, 0).astype(bf16), 0, 1)
        for head in range(heads):
            own = slice(head * HDIM, (head + 1) * HDIM)
            rows = slice(step * width + head * HDIM, step * width + (head + 1) * HDIM)
            grad = grads[own]
            inner = jnp.sum(ctx[rows, :].astype(f32) * grad.astype(f32), axis=0, keepdims=True)
            k_t = kv_refs[step][0, own, :]
            scores = dot(jnp.swapaxes(k_t, 0, 1), q[rows, :], 1, 0)
            probs = jnp.exp(scores - log[step * heads + head])
            grad_probs = dot(jnp.swapaxes(kv_refs[step][1, own, :], 0, 1), grad, 1, 0)
            grad_scores = (probs * (grad_probs - inner)).astype(bf16)
            dq[rows, :] = (dot(k_t, grad_scores, 1, 0) * 0.125).astype(bf16)
            dkv[step, 0, own, :] = dot(q[rows, :], grad_scores, 1, 1)
            dkv[step, 1, own, :] = dot(grad, probs.astype(bf16), 1, 1)
        part = jnp.swapaxes(dq[step * width : (step + 1) * width, :], 0, 1)
        sums[7:8, natural(step)] = jnp.sum(part.astype(f32), axis=0, keepdims=True)
        e_two = e_two + dot(part, w_refs[step][2], 1, 1)
    d_next = d_two + norm_back(e_two, unit_two[...], inv_two[...], norm_ref[0:1, :], 2)
    d_one[...] = d_next
    low = d_next.astype(bf16)
    low_one[...] = low
    add(5, low.astype(f32))
    for step in range(group):
        grads = dot(low, w_refs[step][0], 1, 0).astype(bf16)
        d_ctx[natural(step), :] = jnp.swapaxes(grads, 0, 1)


def middle_backward(info, e, cot, saved, norm, w, kv, heads, after):
    unit_two, inv_two, unit_three, inv_three, q, ctx, log = saved
    rows, model = cot.shape
    group = len(w)
    total = q.shape[0]
    enc = kv[0].shape[2]
    return pl.pallas_call(
        functools.partial(middle_backward_kernel, group, heads, len(after)),
        grid_spec=pltpu.PrefetchScalarGridSpec(
            num_scalar_prefetch=1,
            grid=(1,),
            in_specs=[VMEM] * (10 + 2 * group) + [ANY] * len(after),
            out_specs=[VMEM] * 7,
        ),
        out_shape=[
            jax.ShapeDtypeStruct((rows, model), f32),
            jax.ShapeDtypeStruct((rows, model), bf16),
            jax.ShapeDtypeStruct((rows, model), bf16),
            jax.ShapeDtypeStruct((total, rows), bf16),
            jax.ShapeDtypeStruct((group, 2, heads * HDIM, enc), f32),
            jax.ShapeDtypeStruct((total, rows), bf16),
            jax.ShapeDtypeStruct((8, model), f32),
        ],
        compiler_params=pltpu.CompilerParams(vmem_limit_bytes=LIMIT),
        cost_estimate=pl.CostEstimate(
            flops=6 * rows * model * total, bytes_accessed=16 * 2**20, transcendentals=2**20
        ),
        name="middle_backward",
    )(info, e, cot, unit_two, inv_two, unit_three, inv_three, norm, q, ctx, log, *w, *kv, *after)


CHUNK = 512


def grad_act_kernel(*refs):
    w_ref, out_ref = refs[-2:]
    rows = refs[0].shape[0]
    for index, ref in enumerate(refs[:-2]):
        for start in range(0, w_ref.shape[1], CHUNK):
            cols = slice(start, start + CHUNK)
            out_ref[index * rows : (index + 1) * rows, cols] = dot(
                ref[...], w_ref[:, cols], 1, 0
            ).astype(bf16)


def grad_act(cots, w):
    rows, ff = cots[0].shape[0] * len(cots), w.shape[1]
    return pl.pallas_call(
        grad_act_kernel,
        in_specs=[VMEM] * (len(cots) + 1),
        out_specs=VMEM,
        out_shape=jax.ShapeDtypeStruct((rows, ff), bf16),
        compiler_params=pltpu.CompilerParams(vmem_limit_bytes=LIMIT),
        cost_estimate=pl.CostEstimate(
            flops=2 * rows * ff * w.shape[0], bytes_accessed=10 * 2**20, transcendentals=0
        ),
        name="grad_act",
    )(*cots, w)


def feed_kernel(first, blocks, *refs):
    h_refs, (ga_ref, b_ref, w_ref) = refs[:blocks], refs[blocks : blocks + 3]
    refs = refs[blocks + 3 :]
    act_ref, du_ref, sum_ref, e_refs = refs[0], refs[1], refs[2], refs[3 : 3 + blocks]
    rows, ff = h_refs[0].shape[0], w_ref.shape[1]
    totals = [0.0] * blocks
    for start in range(0, ff, CHUNK):
        cols = slice(start, start + CHUNK)
        sums = 0.0
        for index in range(blocks):
            own = slice(index * rows, (index + 1) * rows)
            inner = dot(h_refs[index][...], w_ref[:, cols], 1, 0) + b_ref[:, cols]
            act, slope = gelu_parts(inner)
            act_ref[own, cols] = act.astype(bf16)
            there = slice((first + index) * rows, (first + index + 1) * rows)
            du = (slope * ga_ref[there, cols].astype(f32)).astype(bf16)
            du_ref[own, cols] = du
            sums = sums + jnp.sum(du.astype(f32), axis=0, keepdims=True)
            totals[index] = totals[index] + dot(du, w_ref[:, cols], 1, 1)
        sum_ref[:, cols] = sums
    for index in range(blocks):
        e_refs[index][...] = totals[index].astype(e_refs[index].dtype)


def feed(h, ga, w, bias, first):
    rows, model = h[0].shape
    ff = w.shape[1]
    blocks = len(h)
    return pl.pallas_call(
        functools.partial(feed_kernel, first, blocks),
        in_specs=[VMEM] * (blocks + 3),
        out_specs=[VMEM] * (3 + blocks),
        out_shape=[jax.ShapeDtypeStruct((blocks * rows, ff), bf16)] * 2
        + [jax.ShapeDtypeStruct((1, ff), f32)]
        + [
            jax.ShapeDtypeStruct((rows, model), bf16 if (first + index) % 2 else f32)
            for index in range(blocks)
        ],
        compiler_params=pltpu.CompilerParams(vmem_limit_bytes=LIMIT),
        cost_estimate=pl.CostEstimate(
            flops=4 * blocks * rows * ff * model, bytes_accessed=12 * 2**20, transcendentals=2**20
        ),
        name="feed",
    )(*h, ga, bias, w)


def outer_kernel(count, side, halves, extra, info, *refs):
    lefts, rights = refs[:count], refs[count : count + 2]
    got_ref = refs[count + 2] if extra else None
    out_ref, picked, turned = refs[-3:]
    rows, model = lefts[0].shape
    shard = out_ref.shape[0] // halves
    which = jnp.bitwise_xor(lax.rem(info[3], 2), side or 0)
    for index in range(count):
        own = slice(index * rows, (index + 1) * rows)
        if side is None:
            picked[:, own] = jnp.swapaxes(lefts[index][...], 0, 1)
            continue
        if shard % 128:
            turned[...] = jnp.swapaxes(lefts[index][...], 0, 1)
        for half in range(halves):
            start = pl.multiple_of((2 * half + which) * shard, shard)
            if shard % 128:
                part = turned[pl.ds(start, shard), :]
            else:
                part = jnp.swapaxes(lefts[index][:, pl.ds(start, shard)], 0, 1)
            picked[half * shard : (half + 1) * shard, own] = part
    middle = rights[0].shape[0]
    for start in range(0, out_ref.shape[1], CHUNK):
        cols = slice(start, start + CHUNK)
        out = dot(picked[:, :middle], rights[0][:, cols], 1, 0)
        out = out + dot(picked[:, middle:], rights[1][:, cols], 1, 0)
        if extra:
            out = out + got_ref[:, cols].astype(f32)
        out_ref[:, cols] = out.astype(bf16)


def outer(lefts, rights, info, side=None, halves=1, got=None):
    rows, model = lefts[0].shape
    count = len(lefts)
    ff = rights[0].shape[1]
    extra = [] if got is None else [got]
    size = model if side is None else model // 2
    return pl.pallas_call(
        functools.partial(outer_kernel, count, side, halves, len(extra)),
        grid_spec=pltpu.PrefetchScalarGridSpec(
            num_scalar_prefetch=1,
            grid=(1,),
            in_specs=[VMEM] * (count + 2 + len(extra)),
            out_specs=VMEM,
            scratch_shapes=[pltpu.VMEM((size, count * rows), bf16), pltpu.VMEM((model, rows), bf16)],
        ),
        out_shape=jax.ShapeDtypeStruct((size, ff), bf16),
        compiler_params=pltpu.CompilerParams(vmem_limit_bytes=LIMIT),
        cost_estimate=pl.CostEstimate(
            flops=2 * count * rows * ff * size, bytes_accessed=10 * 2**20, transcendentals=0
        ),
        name="outer",
    )(info, *lefts, *rights, *extra)


def middle_outer_kernel(group, *refs):
    one, ctx_one, two, ctx_two, h, dq = refs[:6]
    outs = refs[6:]
    width = dq.shape[0] // group
    for index, (left, right) in enumerate(((one, ctx_one), (two, ctx_two), (h, dq))):
        turned = jnp.swapaxes(left[...], 0, 1)
        cols = slice(index * width, (index + 1) * width)
        for step in range(group):
            part = right[step * width : (step + 1) * width, :]
            outs[step][:, cols] = dot(turned, part, 1, 1).astype(bf16)


def middle_outer(one, ctx_one, two, ctx_two, h, dq, group):
    rows, model = one.shape
    width = dq.shape[0] // group
    return pl.pallas_call(
        functools.partial(middle_outer_kernel, group),
        in_specs=[VMEM] * 6,
        out_specs=[VMEM] * group,
        out_shape=[jax.ShapeDtypeStruct((model, 3 * width), bf16)] * group,
        compiler_params=pltpu.CompilerParams(vmem_limit_bytes=LIMIT),
        cost_estimate=pl.CostEstimate(
            flops=6 * rows * model * model, bytes_accessed=9 * 2**20, transcendentals=0
        ),
        name="middle_outer",
    )(one, ctx_one, two, ctx_two, h, dq)


def combine_kernel(extra, *refs):
    dq, dk, dv = refs[:3]
    gots, out = refs[3:-1], refs[-1]
    gots = gots[: len(gots) - extra]
    out[:, 0] = dq[...]
    for index, value in enumerate((dk, dv)):
        total = value[0]
        for got in gots[index::2]:
            total = total + got[...].astype(f32)
        out[:, 1 + index] = total.astype(bf16)


def combine(dq, dk, dv, got_k, got_v, after):
    heads, depth, piece = dq.shape
    gots = [got for pair in zip(got_k, got_v) for got in pair]
    return pl.pallas_call(
        functools.partial(combine_kernel, len(after)),
        in_specs=[VMEM] * (3 + len(gots)) + [ANY] * len(after),
        out_specs=VMEM,
        out_shape=jax.ShapeDtypeStruct((heads, 3, depth, piece), bf16),
        compiler_params=pltpu.CompilerParams(vmem_limit_bytes=LIMIT),
        cost_estimate=pl.CostEstimate(flops=2**20, bytes_accessed=5 * 2**20, transcendentals=0),
        name="combine",
    )(dq, dk, dv, *gots, *after)


def local(
    hidden,
    encoder,
    cotangent,
    block_ids,
    self_qkv,
    self_out,
    cross_qkv,
    cross_out,
    up_weight,
    down_weight,
    proj_bias,
    up_bias,
    norm_gain,
    norm_shift,
):
    tok_size, group = lax.axis_size("tok"), lax.axis_size("hd")
    tok_index, me = lax.axis_index("tok"), lax.axis_index("hd")
    rows, model = hidden.shape
    shard = self_qkv.shape[0]
    width = self_qkv.shape[2]
    ff_local = up_weight.shape[1]
    piece_rows = rows * group
    span = SEQ // piece_rows
    heads = min(width // HDIM, span)
    others = span // heads
    assert heads * HDIM == width and heads * others == span
    seq_count, enc_rows, _ = encoder.shape
    enc_total = enc_rows * group
    own_seq = tok_index // span
    at = lax.rem(tok_index, span) // others
    beside = jnp.bitwise_xor(lax.rem(tok_index, others), lax.rem(at, 2) * (others - 1))
    info = jnp.stack([at, beside, me, tok_index]).astype(jnp.int32)

    def natural(blocks):
        stacked = jnp.stack(blocks)
        return [pick(stacked, me ^ index) for index in range(group)]

    even = lax.rem(tok_index, 2)
    halves = [[i for i in range(tok_size) if i % 2 == side] for side in range(2)]
    many = tok_size // 2

    def gather_half(block):
        return lax.all_gather(block, "tok", axis=0, tiled=True, axis_index_groups=halves)

    def gather_tok(block):
        return lax.all_gather(block, "tok", axis=0, tiled=True)

    def along_halves(block):
        return lax.all_to_all(
            jnp.broadcast_to(block[None], (many, *block.shape)),
            "tok", 0, 0, tiled=True, axis_index_groups=halves,
        )

    def merge_sides(own, got):
        sides = [jnp.where(even == 0, own, got), jnp.where(even == 0, got, own)]
        return jnp.stack(sides, 1).reshape(model, -1)

    w_self = self_qkv.reshape(shard, 3, heads, HDIM).transpose(0, 2, 1, 3)
    w_self = gather_tok(w_self.reshape(shard, 3 * width))
    w_mid = along_halves(
        jnp.concatenate([self_out.T, cross_out.T, cross_qkv.reshape(shard, 3 * width)], 1)
    )

    own_ids = lax.dynamic_slice_in_dim(block_ids, me * rows, rows).astype(bf16)
    small = jnp.concatenate(
        [
            proj_bias.T.reshape(-1),
            norm_gain.T.reshape(-1),
            norm_shift.T.reshape(-1),
            up_bias,
            own_ids,
        ]
    )
    total_devices = tok_size * group
    small_all = lax.all_to_all(
        jnp.broadcast_to(small[None], (total_devices, small.shape[0])),
        ("tok", "hd"), 0, 0, tiled=True,
    ).astype(f32)
    few = model // total_devices
    vectors = small_all[:, : 13 * few].reshape(total_devices, 13, few)
    vectors = vectors.transpose(1, 0, 2).reshape(13, model)
    bias, gain, shift = vectors[:7], vectors[7:10], vectors[10:13]
    few_up = up_bias.shape[0]
    bias_up = small_all[:, 13 * few : 13 * few + few_up].reshape(-1)
    bias_up = lax.dynamic_slice_in_dim(bias_up, me * ff_local, ff_local)
    ids = small_all[:, 13 * few + few_up :].reshape(tok_size, 1, piece_rows)
    ids = lax.dynamic_slice_in_dim(ids, own_seq * span, span).reshape(heads, others, 1, piece_rows)
    ids = jnp.stack([pick(ids[i], beside ^ (i % 2 * (others - 1))) for i in range(heads)])

    def own_columns(vector):
        return lax.dynamic_slice_in_dim(vector, me * width, width)

    hidden_blocks = gather_xor(hidden)
    self_bias = jnp.stack(
        [own_columns(bias[0]), jnp.zeros((width,), f32), own_columns(bias[1])]
    )
    scale = jnp.broadcast_to(jnp.array([0.125, 1.0, 1.0], f32)[:, None], (3, width))
    factors = jnp.stack([self_bias, scale]).reshape(2, 3, heads, HDIM)
    factors = factors.transpose(0, 2, 1, 3).reshape(2, 3 * width)

    lines = [
        [seq * span + i * others + (side ^ (i % 2 * (others - 1))) for i in range(heads)]
        for seq in range(tok_size // span)
        for side in range(others)
    ]
    wide_lines = [[i * group + h for h in range(group) for i in line] for line in lines]

    def across_lines(value):
        return lax.all_to_all(value, "tok", 0, 0, tiled=True, axis_index_groups=lines)

    def across_wide(value):
        return lax.all_to_all(
            value, ("tok", "hd"), 0, 0, tiled=True, axis_index_groups=wide_lines
        )

    q_out, k_out, v_out, h_one = project(
        info, hidden_blocks, w_self, jnp.stack([gain[0], shift[0]]), factors, heads, [w_mid]
    )
    w_up, w_down = tie([up_weight, down_weight], [h_one])
    w_up, w_down = gather_tok(w_up), gather_tok(w_down.T)
    w_mid = merge_sides(w_mid, swap(w_mid, "tok", 1))
    k = [across_lines(k_out)]
    v = [across_lines(v_out)]
    q = across_lines(q_out)
    k += [swap(k[0], "tok", other) for other in range(1, others)]
    v += [swap(v[0], "tok", other) for other in range(1, others)]
    w_cross_kv = w_mid[:, 3 * width :]
    enc_all = jnp.concatenate(natural(gather_xor(encoder)), 1)
    kv_bias = jnp.concatenate([jnp.zeros((width,), f32), own_columns(bias[4])])
    kv_two = dot(w_cross_kv, pick(enc_all, own_seq), 0, 1) + kv_bias[:, None]
    kv_two = kv_two.astype(bf16).reshape(2, width, enc_total)
    kv_two = gather_xor(kv_two)

    context, log_one = self_forward(info, q, k, v, ids, rows, kv_two)

    mid_block = jnp.stack(
        [w_mid[:, :width], w_mid[:, width : 2 * width], w_mid[:, 2 * width : 3 * width]]
    )
    w_blocks = gather_xor(mid_block, lambda value: tie([value], [log_one])[0])
    ctx_one = across_wide(context).reshape(model, rows)
    norm_rows = jnp.stack([gain[1], shift[1], gain[2], shift[2], bias[2], bias[5]])
    (
        resid_two, unit_two, inv_two, unit_three, inv_three,
        h_two, h_three, ctx_one, q_two, ctx_two, log_two,
    ) = middle_forward(
        info, hidden, ctx_one, norm_rows, bias[3:4], w_blocks, kv_two, heads, []
    )

    cot_blocks = gather_xor(cotangent)
    h_blocks = gather_xor(h_three)
    grad_a = grad_act(cot_blocks, w_down)
    near = group // 2
    bias_row = bias_up[None]
    near_out = feed(h_blocks[:near], grad_a, w_up, bias_row, 0)
    far_out = feed(h_blocks[near:], grad_a, w_up, bias_row, near)
    acts, grad_inners = [near_out[0], far_out[0]], [near_out[1], far_out[1]]
    up_sums = (near_out[2] + far_out[2])[0]
    grad_h_three = reduce_xor(list(near_out[3:]) + list(far_out[3:]))

    def half_columns(array, side):
        return jnp.concatenate(
            [
                lax.dynamic_slice_in_dim(array, (2 * i + side) * shard, shard, 1)
                for i in range(tok_size // 2)
            ],
            1,
        )

    def half_rows(array, side):
        return jnp.concatenate(
            [
                lax.dynamic_slice_in_dim(array, (2 * i + side) * shard, shard, 0)
                for i in range(tok_size // 2)
            ],
            0,
        )

    def reduce_tok(value):
        return lax.psum_scatter(value, "tok", scatter_dimension=0, tiled=True).astype(f32)

    def reduce_half(value):
        return lax.psum_scatter(
            value, "tok", scatter_dimension=0, tiled=True, axis_index_groups=halves
        ).astype(f32)

    grad_up = outer(h_blocks, grad_inners, info)
    down_away = outer(cot_blocks, acts, info, 1, many)
    sent_up = reduce_tok(grad_up)
    down_got = swap(down_away, "tok", 1)

    grad_one, grad_two_low, grad_one_low, grad_q_two, grad_kv_two, grad_ctx_one, sums = (
        middle_backward(
            info, grad_h_three, cotangent,
            (unit_two, inv_two, unit_three, inv_three, q_two, ctx_two, log_two),
            norm_rows, w_blocks, kv_two, heads, [grad_up, down_away],
        )
    )
    grad_heads = across_wide(grad_ctx_one.reshape(group * heads, HDIM, rows))
    grad_mid = middle_outer(
        grad_one_low, ctx_one, grad_two_low, ctx_two, h_two, grad_q_two, group
    )
    masks = [1 << bit for bit in range(tok_size.bit_length() - 1)]

    def add_low(value, got):
        return (value.astype(f32) + got.astype(f32)).astype(bf16)

    grad_q_away, grad_k_away, grad_v_away = self_backward(
        info, q, k[1:], v[1:], None, grad_heads, context, log_one, None, grad_mid
    )
    down_got = tie([down_got], [grad_q_away])[0]
    down_sum = outer(cot_blocks, acts, info, 0, many, down_got)
    sent_down = reduce_half(tie([down_sum], [sent_up])[0]).T
    kv_total = reduce_xor(
        [grad_kv_two[j] for j in range(group)], lambda got: tie([got], [grad_q_away])[0]
    )
    seq_pick = jnp.arange(seq_count) == own_seq
    kv_total = jnp.where(seq_pick[:, None, None, None], kv_total[None], 0.0).astype(bf16)
    grad_mid = reduce_xor(grad_mid, lambda got: tie([got], [grad_q_away])[0])
    mid_got = swap(half_rows(grad_mid, 1 - even).astype(bf16), "tok", 1)
    mid_sum = (half_rows(grad_mid, even) + mid_got.astype(f32)).astype(bf16)
    sent_mid = reduce_half(tie([mid_sum], [sent_down])[0])
    grad_k_got = [swap(grad_k_away[i], "tok", i + 1) for i in range(others - 1)]
    grad_v_got = [swap(grad_v_away[i], "tok", i + 1) for i in range(others - 1)]
    grad_q, grad_k, grad_v = self_backward(
        info, q, k[:1], v[:1], ids, grad_heads, context, log_one, grad_q_away, [down_sum]
    )
    kv_got = swap(kv_total, "tok", masks[0])
    grad_qkv = combine(grad_q, grad_k, grad_v, grad_k_got, grad_v_got, [sent_up, kv_got])
    kv_total = add_low(kv_total, kv_got)
    acts = tie(acts, [grad_q])
    def act_block(index):
        start = index % near * rows
        return acts[index // near][start : start + rows]

    final = reduce_xor([dot(act_block(j), w_down, 1, 1) for j in range(group)])
    output = (resid_two + final + bias[6]).astype(bf16)
    grad_qkv = across_lines(grad_qkv).reshape(3 * width, piece_rows)
    kv_got = swap(kv_total, "tok", masks[1])
    grad_qkv, sent_down, kv_got = tie([grad_qkv, sent_down, kv_got], [])
    kv_total = add_low(kv_total, kv_got)
    for got_mask in masks[2:]:
        kv_total = add_low(kv_total, swap(kv_total, "tok", got_mask))
    kv_flat = kv_total.reshape(seq_count, 2 * width, enc_total)
    own_enc = lax.dynamic_slice_in_dim(enc_all, tok_index * shard, shard, 2)
    sent_cross_kv = sum(dot(own_enc[n], kv_flat[n], 0, 1) for n in range(seq_count))

    def encoder_part(index):
        start = (me ^ index) * enc_rows
        return jnp.stack(
            [
                dot(lax.dynamic_slice_in_dim(kv_flat[n], start, enc_rows, 1), w_cross_kv, 0, 1)
                for n in range(seq_count)
            ]
        )

    grad_encoder = reduce_xor([encoder_part(j) for j in range(group)])

    grad_self = dot(h_one, grad_qkv, 0, 1).astype(bf16)
    sent_self = lax.all_to_all(grad_self, "tok", 0, 0, tiled=True)
    ordered = sent_self
    sent_self = jnp.sum(sent_self.reshape(tok_size, shard, 3 * width).astype(f32), 0)
    sent_self = sent_self.reshape(shard, heads, 3, HDIM)
    sent_self = sent_self.transpose(0, 2, 1, 3).reshape(shard, 3, width)
    grad_qkv = tie([grad_qkv], [grad_self])[0]
    grad_h_one = reduce_xor(
        [
            dot(
                lax.dynamic_slice(grad_qkv, (0, (me ^ j) * rows), (3 * width, rows)), w_self, 0, 1
            )
            for j in range(group)
        ]
    )
    unit_one, inverse_one = normalize(hidden.astype(f32))
    back, gain_one, shift_one = norm_backward(grad_h_one, unit_one, inverse_one, gain[0])
    grad_hidden = grad_one + back

    def place(vector):
        return lax.dynamic_update_slice_in_dim(jnp.zeros((model,), f32), vector, me * width, 0)

    qkv_sums = jnp.sum(grad_qkv.astype(f32), 1).reshape(heads, 3, HDIM)
    once = (tok_index == 0).astype(f32)
    late = jnp.concatenate(
        [
            place(qkv_sums[:, 0].reshape(-1)),
            place(qkv_sums[:, 2].reshape(-1)),
            place(jnp.sum(kv_flat[:, width:].astype(f32), (0, 2)) * once),
            gain_one,
            shift_one,
        ]
    )
    vectors = jnp.concatenate([sums, late.reshape(5, model)], 0)
    vectors = vectors.reshape(13, total_devices, few).transpose(1, 0, 2).reshape(total_devices, -1)
    up_all = lax.dynamic_update_slice_in_dim(
        jnp.zeros((group * ff_local,), f32), up_sums, me * ff_local, 0
    )
    vectors = jnp.concatenate([vectors, up_all.reshape(total_devices, -1)], 1)
    vectors = tie([vectors], [ordered])[0]
    vectors = jnp.sum(lax.all_to_all(vectors, ("tok", "hd"), 0, 0, tiled=True), 0)
    columns = vectors[: 13 * few].reshape(13, few)
    columns = columns[jnp.array([8, 9, 5, 7, 10, 4, 6, 11, 2, 0, 12, 3, 1])].T

    sent_mid = [sent_mid[:, j * width : (j + 1) * width] for j in range(3)]
    sent_cross = jnp.concatenate(
        [sent_mid[2][:, None], sent_cross_kv.reshape(shard, 2, width)], 1
    )
    return (
        output,
        grad_hidden,
        grad_encoder,
        sent_self,
        sent_mid[0].T,
        sent_cross,
        sent_mid[1].T,
        sent_up,
        sent_down,
        columns[:, :7],
        vectors[13 * few :],
        columns[:, 7:10],
        columns[:, 10:13],
    )


def solution(mesh):
    in_specs = (
        P(("tok", "hd"), None),
        P(None, "hd", None),
        P(("tok", "hd"), None),
        P("tok"),
        P("tok", None, "hd"),
        P("hd", "tok"),
        P("tok", None, "hd"),
        P("hd", "tok"),
        P("tok", "hd"),
        P("hd", "tok"),
        P(("tok", "hd"), None),
        P(("tok", "hd")),
        P(("tok", "hd"), None),
        P(("tok", "hd"), None),
    )
    out_specs = (
        P(("tok", "hd"), None),
        P(("tok", "hd"), None),
        P(None, "hd", None),
        P("tok", None, "hd"),
        P("hd", "tok"),
        P("tok", None, "hd"),
        P("hd", "tok"),
        P("tok", "hd"),
        P("hd", "tok"),
        P(("tok", "hd"), None),
        P(("tok", "hd")),
        P(("tok", "hd"), None),
        P(("tok", "hd"), None),
    )
    return jax.shard_map(local, mesh=mesh, in_specs=in_specs, out_specs=out_specs, check_vma=False)
```

```python
import functools

import jax
import jax.numpy as jnp
from jax import lax
from jax.experimental import pallas as pl
from jax.experimental.pallas import tpu as pltpu
from jax.sharding import PartitionSpec as P

HDIM = 64
SEQ = 8192
TILE = 512
norm_eps = 1e-05
neg_large = -1e30
f32 = jnp.float32
bf16 = jnp.bfloat16


def dot(left, right, left_dim, right_dim):
    return lax.dot_general(
        left, right, (((left_dim,), (right_dim,)), ((), ())), preferred_element_type=f32
    )


def swap(value, axis, mask):
    return lax.ppermute(value, axis, [(i, i ^ mask) for i in range(lax.axis_size(axis))])


def hd_masks():
    mask, masks = lax.axis_size("hd") // 2, []
    while mask:
        masks.append(mask)
        mask //= 2
    return masks


def gather_xor(value, first=lambda value: value):
    have = {0: value}
    for mask in hd_masks():
        for index in list(have):
            have[index ^ mask] = first(swap(have[index], "hd", mask))
        first = lambda value: value
    return [have[index] for index in range(len(have))]


def reduce_xor(parts, last=lambda value: value):
    have = dict(enumerate(parts))
    for mask in reversed(hd_masks()):
        for index in sorted(have, reverse=True):
            if index & mask:
                got = swap(have.pop(index).astype(bf16), "hd", mask)
                if len(have) == 1:
                    got = last(got)
                total = have[index ^ mask].astype(f32) + got.astype(f32)
                have[index ^ mask] = total if len(have) == 1 else total.astype(bf16)
    return have[0]


def pick(stacked, index):
    return lax.dynamic_index_in_dim(stacked, index, 0, keepdims=False)


def normalize(value):
    center = value - jnp.mean(value, axis=-1, keepdims=True)
    inverse = lax.rsqrt(jnp.mean(center * center, axis=-1, keepdims=True) + norm_eps)
    return center * inverse, inverse


def norm_backward(grad, unit, inverse, gain):
    scaled = grad * gain
    back = (
        scaled
        - jnp.mean(scaled, axis=-1, keepdims=True)
        - unit * jnp.mean(scaled * unit, axis=-1, keepdims=True)
    ) * inverse
    return back, jnp.sum(grad * unit, axis=0), jnp.sum(grad, axis=0)


def column(row, rows):
    return jnp.swapaxes(jnp.broadcast_to(row, (128, rows)), 0, 1)[:, :1]


VMEM = pl.BlockSpec(memory_space=pltpu.VMEM)
LIMIT = 48 * 2**20


ANY = pl.BlockSpec(memory_space=pl.ANY)


def tie(values, after):
    count = len(values)
    return pl.pallas_call(
        lambda *refs: None,
        in_specs=[ANY] * (count + len(after)),
        out_specs=[ANY] * count,
        out_shape=[jax.ShapeDtypeStruct(value.shape, value.dtype) for value in values],
        input_output_aliases={index: index for index in range(count)},
        name="tie",
    )(*values, *after)


def project_kernel(heads, group, info, *refs):
    refs = list(refs)
    w_ref, norm_ref, bias_ref = refs[:3]
    q_ref, k_ref, v_ref, h_ref = refs[-4:]
    x_refs = refs[3 : 3 + group]
    rows = x_refs[0].shape[0]
    for step, x_ref in enumerate(x_refs):
        start = pl.multiple_of(jnp.bitwise_xor(info[2], step) * rows, rows)
        cols = pl.ds(start, rows)
        x = x_ref[...].astype(f32)
        h = (normalize(x)[0] * norm_ref[0:1, :] + norm_ref[1:2, :]).astype(bf16)
        h_ref[cols, :] = h
        out = (dot(h, w_ref[...], 1, 0) + bias_ref[0:1, :]) * bias_ref[1:2, :]
        out = jnp.swapaxes(out.astype(bf16), 0, 1)
        for head in range(heads):
            for part, ref in enumerate((q_ref, k_ref, v_ref)):
                first = (head * 3 + part) * HDIM
                ref[head, :, cols] = out[first : first + HDIM]


def project(info, x, w, norm, bias, heads, after):
    rows, model = x[0].shape
    group = len(x)
    piece = rows * group
    width = w.shape[1]
    return pl.pallas_call(
        functools.partial(project_kernel, heads, group),
        grid_spec=pltpu.PrefetchScalarGridSpec(
            num_scalar_prefetch=1,
            grid=(1,),
            in_specs=[VMEM] * (group + 3) + [ANY] * len(after),
            out_specs=[VMEM] * 4,
        ),
        out_shape=[jax.ShapeDtypeStruct((heads, HDIM, piece), bf16)] * 3
        + [jax.ShapeDtypeStruct((piece, model), bf16)],
        compiler_params=pltpu.CompilerParams(vmem_limit_bytes=LIMIT),
        cost_estimate=pl.CostEstimate(
            flops=2 * piece * model * width, bytes_accessed=8 * 2**20, transcendentals=piece
        ),
        name="project",
    )(info, w, norm, bias, *x, *after)


def flip(place, others):
    return lax.rem(place, 2) * (others - 1)


def self_forward_kernel(heads, others, info, *refs):
    q_ref, id_ref = refs[:2]
    k_refs, v_refs = refs[2 : 2 + others], refs[2 + others : 2 + 2 * others]
    o_ref, l_ref, k_all, v_all, wait_a, wait_b = refs[-6:]
    beside = info[1]
    step = pl.program_id(0)
    piece_rows = q_ref.shape[2]
    assert piece_rows == 2 * TILE
    per = piece_rows // TILE
    slot, tile = step // per, lax.rem(step, per)

    @pl.when(step == 0)
    def _():
        for other in range(others):
            for place in range(heads):
                k_all[other, place] = jnp.swapaxes(k_refs[other][place], 0, 1)
                v_all[other, place] = v_refs[other][place]

    piece = slot * others + jnp.bitwise_xor(beside, flip(slot, others))
    cols = pl.ds(pl.multiple_of(tile * TILE, TILE), TILE)
    q = q_ref[slot, :, cols]

    def ahead(wait, keys, top, mask=None):
        scores = dot(keys, q, 1, 0)
        if mask is not None:
            scores = jnp.where(mask, scores, neg_large)
        wait[...] = scores
        return jnp.maximum(top, jnp.max(scores, axis=0, keepdims=True))

    def finish(wait, values, top, fade, total, acc):
        probs = jnp.exp(wait[...] - top)
        total = total * fade + jnp.sum(probs, axis=0, keepdims=True)
        return total, acc * fade + dot(values, probs.astype(bf16), 1, 0)

    def locate(index):
        place = index // others
        side = jnp.bitwise_xor(beside, flip(place, others))
        return jnp.bitwise_xor(lax.rem(index, others), side), place

    def waiting(index):
        other, place = locate(jnp.maximum(index - 1, 0))
        other, place = jnp.where(index == 0, 0, other), jnp.where(index == 0, slot, place)
        start = jnp.where(index == 0, 0, TILE)
        return v_all[other, place, :, pl.ds(pl.multiple_of(start, TILE), TILE)]

    def earlier_tile(state):
        top, fade, total, acc = state
        new_top = ahead(wait_b, k_all[0, slot, :TILE, :], top)
        total, acc = finish(wait_a, v_all[0, slot, :, cols], top, fade, total, acc)
        wait_a[...] = wait_b[...]
        return new_top, jnp.exp(top - new_top), total, acc

    def earlier_piece(index, state):
        top, fade, total, acc = state
        other, place = locate(index)
        new_top = ahead(wait_b, k_all[other, place, :TILE, :], top)
        total, acc = finish(wait_a, waiting(index), top, fade, total, acc)
        fade, top = jnp.exp(top - new_top), new_top
        new_top = ahead(wait_a, k_all[other, place, TILE:, :], top)
        total, acc = finish(wait_b, v_all[other, place, :, :TILE], top, fade, total, acc)
        return new_top, jnp.exp(top - new_top), total, acc

    ids = id_ref[slot, :, cols]
    mask = column(ids, TILE) <= ids
    top = ahead(wait_a, k_all[0, slot, cols, :], jnp.full((1, TILE), neg_large, f32), mask)
    state = (
        top,
        jnp.ones((1, TILE), f32),
        jnp.zeros((1, TILE), f32),
        jnp.zeros((HDIM, TILE), f32),
    )
    state = lax.cond(tile == 1, earlier_tile, lambda state: state, state)
    top, fade, total, acc = lax.fori_loop(0, piece, earlier_piece, state)
    total, acc = finish(wait_a, waiting(piece), top, fade, total, acc)
    out = (acc / total).astype(o_ref.dtype)
    rows = o_ref.shape[2]
    for index in range(TILE // rows):
        place = (tile * (TILE // rows) + index) * heads + slot
        o_ref[place] = out[:, index * rows : (index + 1) * rows]
    l_ref[slot, :, cols] = top + jnp.log(total)


def self_forward(info, q, k, v, ids, rows, after):
    others = len(k)
    heads, depth, piece = q.shape
    area = heads * piece * heads * others * piece // 2
    return pl.pallas_call(
        functools.partial(self_forward_kernel, heads, others),
        grid_spec=pltpu.PrefetchScalarGridSpec(
            num_scalar_prefetch=1,
            grid=(heads * piece // TILE,),
            in_specs=[VMEM] * (2 + 2 * others) + [ANY] * len(after),
            out_specs=[VMEM] * 2,
            scratch_shapes=[
                pltpu.VMEM((others, heads, piece, depth), bf16),
                pltpu.VMEM((others, heads, depth, piece), bf16),
                pltpu.VMEM((TILE, TILE), f32),
                pltpu.VMEM((TILE, TILE), f32),
            ],
        ),
        out_shape=[
            jax.ShapeDtypeStruct((piece // rows * heads, depth, rows), bf16),
            jax.ShapeDtypeStruct((heads, 1, piece), f32),
        ],
        compiler_params=pltpu.CompilerParams(vmem_limit_bytes=LIMIT),
        cost_estimate=pl.CostEstimate(
            flops=area * 1024, bytes_accessed=8 * 2**20, transcendentals=area
        ),
        name="self_forward",
    )(info, q, ids, *k, *v, *after)


def self_backward_kernel(heads, sides, own, extra, info, *refs):
    refs = list(refs)
    q_ref, g_ref, o_ref, l_ref = refs[:4]
    k_refs, v_refs = refs[4 : 4 + sides], refs[4 + sides : 4 + 2 * sides]
    refs = refs[4 + 2 * sides :]
    id_ref, before_ref = (refs.pop(0), refs.pop(0)) if own else (None, None)
    dq_ref, dk_ref, dv_ref, g_all, inner_all, k_all, v_all, dk, dv = refs[extra:]
    beside = info[1]
    step = pl.program_id(0)
    piece_rows = q_ref.shape[2]
    per = piece_rows // TILE
    slot, tile = step // per, lax.rem(step, per)

    @pl.when(step == 0)
    def _():
        rows = g_ref.shape[2]
        for place in range(heads):
            for index in range(piece_rows // rows):
                at = slice(index * rows, (index + 1) * rows)
                grad = g_ref[index * heads + place]
                g_all[place, :, at] = grad
                inner_all[place, :, at] = jnp.sum(
                    o_ref[index * heads + place].astype(f32) * grad.astype(f32),
                    axis=0,
                    keepdims=True,
                )
            for side in range(sides):
                k_all[side, place] = jnp.swapaxes(k_refs[side][place], 0, 1)
                v_all[side, place] = jnp.swapaxes(v_refs[side][place], 0, 1)
        dk[...] = jnp.zeros_like(dk)
        dv[...] = jnp.zeros_like(dv)

    cols = pl.ds(pl.multiple_of(tile * TILE, TILE), TILE)
    q = q_ref[slot, :, cols]
    grad = g_all[slot, :, cols]
    q_rows = jnp.swapaxes(q, 0, 1)
    grad_rows = jnp.swapaxes(grad, 0, 1)
    log_total = l_ref[slot, :, cols]
    inner = inner_all[slot, :, cols]

    def update(dq, side, place, rows, mask):
        scores = dot(k_all[side, place, rows, :], q, 1, 0)
        if mask is not None:
            scores = jnp.where(mask, scores, neg_large)
        probs = jnp.exp(scores - log_total)
        grad_probs = dot(v_all[side, place, rows, :], grad, 1, 0)
        grad_scores = (probs * (grad_probs - inner)).astype(bf16)
        dv[side, place, rows, :] += dot(probs.astype(bf16), grad_rows, 1, 0)
        dk[side, place, rows, :] += dot(grad_scores, q_rows, 1, 0)
        return dq + dot(k_refs[side][place, :, rows], grad_scores, 1, 0)

    dq = before_ref[slot, :, cols] if own else jnp.zeros((HDIM, TILE), f32)
    for side in range(sides):

        def earlier(index, dq, side=side):
            rows = pl.ds(pl.multiple_of(lax.rem(index, per) * TILE, TILE), TILE)
            return update(dq, side, index // per, rows, None)

        if own:
            count = slot * per + tile
        else:
            here = jnp.bitwise_xor(beside, flip(slot, sides + 1))
            count = (slot + jnp.where(jnp.bitwise_xor(here, side + 1) < here, 1, 0)) * per
        dq = lax.fori_loop(0, count, earlier, dq)
    if own:
        ids = id_ref[slot, :, cols]
        mask = column(ids, TILE) <= ids
        dq = update(dq, 0, slot, cols, mask) * 0.125
    dq_ref[slot, :, cols] = dq.astype(dq_ref.dtype)

    @pl.when(step == heads * per - 1)
    def _():
        for side in range(sides):
            for place in range(heads):
                dk_ref[side, place] = jnp.swapaxes(dk[side, place], 0, 1).astype(dk_ref.dtype)
                dv_ref[side, place] = jnp.swapaxes(dv[side, place], 0, 1).astype(dv_ref.dtype)


def self_backward(info, q, k, v, ids, grad, context, log_total, before, after):
    own = ids is not None
    sides = len(k)
    heads, depth, piece = q.shape
    flat = [q, grad, context, log_total, *k, *v] + ([ids, before] if own else [])
    area = heads * piece * heads * sides * piece // 2
    return pl.pallas_call(
        functools.partial(self_backward_kernel, heads, sides, own, len(after)),
        grid_spec=pltpu.PrefetchScalarGridSpec(
            num_scalar_prefetch=1,
            grid=(heads * piece // TILE,),
            in_specs=[VMEM] * len(flat) + [ANY] * len(after),
            out_specs=[VMEM] * 3,
            scratch_shapes=[
                pltpu.VMEM((heads, depth, piece), bf16),
                pltpu.VMEM((heads, 1, piece), f32),
                pltpu.VMEM((sides, heads, piece, depth), bf16),
                pltpu.VMEM((sides, heads, piece, depth), bf16),
                pltpu.VMEM((sides, heads, piece, depth), f32),
                pltpu.VMEM((sides, heads, piece, depth), f32),
            ],
        ),
        out_shape=[jax.ShapeDtypeStruct((heads, depth, piece), bf16 if own else f32)]
        + [jax.ShapeDtypeStruct((sides, heads, depth, piece), f32 if own else bf16)] * 2,
        compiler_params=pltpu.CompilerParams(vmem_limit_bytes=LIMIT),
        cost_estimate=pl.CostEstimate(
            flops=area * 64, bytes_accessed=2**16, transcendentals=0
        ),
        name="self_backward",
    )(info, *flat, *after)


def gelu_parts(value):
    half = 0.5 * (1.0 + lax.erf(value * 0.7071067811865476))
    slope = half + value * jnp.exp(-0.5 * value * value) * 0.3989422804014327
    return value * half, slope


def middle_forward_kernel(group, heads, info, *refs):
    x_ref, ctx_ref, norm_ref, bias_ref = refs[:4]
    w_refs, kv_refs = refs[4 : 4 + group], refs[4 + group : 4 + 2 * group]
    x_two, unit_two, inv_two, unit_three, inv_three, h_two, h_three, ctx_xor, q, ctx, log = refs[-11:]
    width = heads * HDIM
    me = info[2]

    def natural(step):
        return pl.ds(pl.multiple_of(jnp.bitwise_xor(me, step) * width, width), width)

    resid = x_ref[...].astype(f32) + norm_ref[4:5, :]
    for step in range(group):
        part = ctx_ref[natural(step), :]
        ctx_xor[step * width : (step + 1) * width, :] = part
        resid = resid + dot(jnp.swapaxes(part, 0, 1), w_refs[step][0], 1, 1)
    unit, inverse = normalize(resid)
    unit_two[...] = unit
    inv_two[...] = inverse
    low = (unit * norm_ref[0:1, :] + norm_ref[1:2, :]).astype(bf16)
    h_two[...] = low
    for step in range(group):
        out = (dot(low, w_refs[step][2], 1, 0) + bias_ref[:, natural(step)]) * 0.125
        q[step * width : (step + 1) * width, :] = jnp.swapaxes(out.astype(bf16), 0, 1)
    resid = resid + norm_ref[5:6, :]
    for step in range(group):
        for head in range(heads):
            own = slice(head * HDIM, (head + 1) * HDIM)
            rows = slice(step * width + head * HDIM, step * width + (head + 1) * HDIM)
            scores = dot(jnp.swapaxes(kv_refs[step][0, own, :], 0, 1), q[rows, :], 1, 0)
            top = jnp.max(scores, axis=0, keepdims=True)
            probs = jnp.exp(scores - top)
            total = jnp.sum(probs, axis=0, keepdims=True)
            out = dot(kv_refs[step][1, own, :], probs.astype(bf16), 1, 0)
            ctx[rows, :] = (out / total).astype(bf16)
            log[step * heads + head] = top + jnp.log(total)
        part = ctx[step * width : (step + 1) * width, :]
        resid = resid + dot(jnp.swapaxes(part, 0, 1), w_refs[step][1], 1, 1)
    x_two[...] = resid
    unit, inverse = normalize(resid)
    unit_three[...] = unit
    inv_three[...] = inverse
    h_three[...] = (unit * norm_ref[2:3, :] + norm_ref[3:4, :]).astype(bf16)


def middle_forward(info, x, ctx, norm, bias, w, kv, heads, after):
    rows, model = x.shape
    group = len(w)
    total = ctx.shape[0]
    shapes = [
        jax.ShapeDtypeStruct((rows, model), f32),
        jax.ShapeDtypeStruct((rows, model), f32),
        jax.ShapeDtypeStruct((rows, 1), f32),
        jax.ShapeDtypeStruct((rows, model), f32),
        jax.ShapeDtypeStruct((rows, 1), f32),
        jax.ShapeDtypeStruct((rows, model), bf16),
        jax.ShapeDtypeStruct((rows, model), bf16),
        jax.ShapeDtypeStruct((total, rows), bf16),
        jax.ShapeDtypeStruct((total, rows), bf16),
        jax.ShapeDtypeStruct((total, rows), bf16),
        jax.ShapeDtypeStruct((total // HDIM, 1, rows), f32),
    ]
    return pl.pallas_call(
        functools.partial(middle_forward_kernel, group, heads),
        grid_spec=pltpu.PrefetchScalarGridSpec(
            num_scalar_prefetch=1,
            grid=(1,),
            in_specs=[VMEM] * (4 + 2 * group) + [ANY] * len(after),
            out_specs=[
                VMEM if index == 6 else pl.BlockSpec(shape.shape, lambda *_, n=len(shape.shape): (0,) * n)
                for index, shape in enumerate(shapes)
            ],
        ),
        out_shape=shapes,
        compiler_params=pltpu.CompilerParams(vmem_limit_bytes=LIMIT),
        cost_estimate=pl.CostEstimate(
            flops=6 * rows * model * total, bytes_accessed=12 * 2**20, transcendentals=2**20
        ),
        name="middle_forward",
    )(info, x, ctx, norm, bias, *w, *kv, *after)


def middle_backward_kernel(group, heads, extra, info, *refs):
    e_ref, cot_ref, unit_two, inv_two, unit_three, inv_three, norm_ref, q, ctx, log = refs[:10]
    w_refs, kv_refs = refs[10 : 10 + group], refs[10 + group : 10 + 2 * group]
    d_one, low_two, low_one, dq, dkv, d_ctx, sums = refs[10 + 2 * group + extra :]
    width = heads * HDIM
    me = info[2]

    def natural(step):
        return pl.ds(pl.multiple_of(jnp.bitwise_xor(me, step) * width, width), width)

    def add(row, value):
        sums[row : row + 1, :] = jnp.sum(value, axis=0, keepdims=True)

    def norm_back(grad, unit, inverse, gain, row):
        add(row, grad * unit)
        add(row + 1, grad)
        scaled = grad * gain
        return (
            scaled
            - jnp.mean(scaled, axis=-1, keepdims=True)
            - unit * jnp.mean(scaled * unit, axis=-1, keepdims=True)
        ) * inverse

    cot = cot_ref[...].astype(f32)
    d_two = cot + norm_back(e_ref[...], unit_three[...], inv_three[...], norm_ref[2:3, :], 0)
    low = d_two.astype(bf16)
    low_two[...] = low
    add(4, low.astype(f32))
    add(6, cot)
    e_two = jnp.zeros_like(d_two)
    for step in range(group):
        grads = jnp.swapaxes(dot(low, w_refs[step][1], 1, 0).astype(bf16), 0, 1)
        for head in range(heads):
            own = slice(head * HDIM, (head + 1) * HDIM)
            rows = slice(step * width + head * HDIM, step * width + (head + 1) * HDIM)
            grad = grads[own]
            inner = jnp.sum(ctx[rows, :].astype(f32) * grad.astype(f32), axis=0, keepdims=True)
            k_t = kv_refs[step][0, own, :]
            scores = dot(jnp.swapaxes(k_t, 0, 1), q[rows, :], 1, 0)
            probs = jnp.exp(scores - log[step * heads + head])
            grad_probs = dot(jnp.swapaxes(kv_refs[step][1, own, :], 0, 1), grad, 1, 0)
            grad_scores = (probs * (grad_probs - inner)).astype(bf16)
            dq[rows, :] = (dot(k_t, grad_scores, 1, 0) * 0.125).astype(bf16)
            dkv[step, 0, own, :] = dot(q[rows, :], grad_scores, 1, 1)
            dkv[step, 1, own, :] = dot(grad, probs.astype(bf16), 1, 1)
        part = jnp.swapaxes(dq[step * width : (step + 1) * width, :], 0, 1)
        sums[7:8, natural(step)] = jnp.sum(part.astype(f32), axis=0, keepdims=True)
        e_two = e_two + dot(part, w_refs[step][2], 1, 1)
    d_next = d_two + norm_back(e_two, unit_two[...], inv_two[...], norm_ref[0:1, :], 2)
    d_one[...] = d_next
    low = d_next.astype(bf16)
    low_one[...] = low
    add(5, low.astype(f32))
    for step in range(group):
        grads = dot(low, w_refs[step][0], 1, 0).astype(bf16)
        d_ctx[natural(step), :] = jnp.swapaxes(grads, 0, 1)


def middle_backward(info, e, cot, saved, norm, w, kv, heads, after):
    unit_two, inv_two, unit_three, inv_three, q, ctx, log = saved
    rows, model = cot.shape
    group = len(w)
    total = q.shape[0]
    enc = kv[0].shape[2]
    return pl.pallas_call(
        functools.partial(middle_backward_kernel, group, heads, len(after)),
        grid_spec=pltpu.PrefetchScalarGridSpec(
            num_scalar_prefetch=1,
            grid=(1,),
            in_specs=[VMEM] * (10 + 2 * group) + [ANY] * len(after),
            out_specs=[VMEM] * 7,
        ),
        out_shape=[
            jax.ShapeDtypeStruct((rows, model), f32),
            jax.ShapeDtypeStruct((rows, model), bf16),
            jax.ShapeDtypeStruct((rows, model), bf16),
            jax.ShapeDtypeStruct((total, rows), bf16),
            jax.ShapeDtypeStruct((group, 2, heads * HDIM, enc), f32),
            jax.ShapeDtypeStruct((total, rows), bf16),
            jax.ShapeDtypeStruct((8, model), f32),
        ],
        compiler_params=pltpu.CompilerParams(vmem_limit_bytes=LIMIT),
        cost_estimate=pl.CostEstimate(
            flops=6 * rows * model * total, bytes_accessed=16 * 2**20, transcendentals=2**20
        ),
        name="middle_backward",
    )(info, e, cot, unit_two, inv_two, unit_three, inv_three, norm, q, ctx, log, *w, *kv, *after)


CHUNK = 512


def grad_act_kernel(*refs):
    w_ref, out_ref = refs[-2:]
    rows = refs[0].shape[0]
    for index, ref in enumerate(refs[:-2]):
        for start in range(0, w_ref.shape[1], CHUNK):
            cols = slice(start, start + CHUNK)
            out_ref[index * rows : (index + 1) * rows, cols] = dot(
                ref[...], w_ref[:, cols], 1, 0
            ).astype(bf16)


def grad_act(cots, w):
    rows, ff = cots[0].shape[0] * len(cots), w.shape[1]
    return pl.pallas_call(
        grad_act_kernel,
        in_specs=[VMEM] * (len(cots) + 1),
        out_specs=VMEM,
        out_shape=jax.ShapeDtypeStruct((rows, ff), bf16),
        compiler_params=pltpu.CompilerParams(vmem_limit_bytes=LIMIT),
        cost_estimate=pl.CostEstimate(
            flops=2 * rows * ff * w.shape[0], bytes_accessed=10 * 2**20, transcendentals=0
        ),
        name="grad_act",
    )(*cots, w)


def feed_kernel(first, blocks, *refs):
    h_refs, (ga_ref, b_ref, w_ref) = refs[:blocks], refs[blocks : blocks + 3]
    refs = refs[blocks + 3 :]
    act_ref, du_ref, sum_ref, e_refs = refs[0], refs[1], refs[2], refs[3 : 3 + blocks]
    rows, ff = h_refs[0].shape[0], w_ref.shape[1]
    totals = [0.0] * blocks
    for start in range(0, ff, CHUNK):
        cols = slice(start, start + CHUNK)
        sums = 0.0
        for index in range(blocks):
            own = slice(index * rows, (index + 1) * rows)
            inner = dot(h_refs[index][...], w_ref[:, cols], 1, 0) + b_ref[:, cols]
            act, slope = gelu_parts(inner)
            act_ref[own, cols] = act.astype(bf16)
            there = slice((first + index) * rows, (first + index + 1) * rows)
            du = (slope * ga_ref[there, cols].astype(f32)).astype(bf16)
            du_ref[own, cols] = du
            sums = sums + jnp.sum(du.astype(f32), axis=0, keepdims=True)
            totals[index] = totals[index] + dot(du, w_ref[:, cols], 1, 1)
        sum_ref[:, cols] = sums
    for index in range(blocks):
        e_refs[index][...] = totals[index].astype(e_refs[index].dtype)


def feed(h, ga, w, bias, first):
    rows, model = h[0].shape
    ff = w.shape[1]
    blocks = len(h)
    return pl.pallas_call(
        functools.partial(feed_kernel, first, blocks),
        in_specs=[VMEM] * (blocks + 3),
        out_specs=[VMEM] * (3 + blocks),
        out_shape=[jax.ShapeDtypeStruct((blocks * rows, ff), bf16)] * 2
        + [jax.ShapeDtypeStruct((1, ff), f32)]
        + [
            jax.ShapeDtypeStruct((rows, model), bf16 if (first + index) % 2 else f32)
            for index in range(blocks)
        ],
        compiler_params=pltpu.CompilerParams(vmem_limit_bytes=LIMIT),
        cost_estimate=pl.CostEstimate(
            flops=4 * blocks * rows * ff * model, bytes_accessed=12 * 2**20, transcendentals=2**20
        ),
        name="feed",
    )(*h, ga, bias, w)


def outer_kernel(count, side, halves, extra, info, *refs):
    lefts, rights = refs[:count], refs[count : count + 2]
    got_ref = refs[count + 2] if extra else None
    out_ref, picked, turned = refs[-3:]
    rows, model = lefts[0].shape
    shard = out_ref.shape[0] // halves
    which = jnp.bitwise_xor(lax.rem(info[3], 2), side or 0)
    for index in range(count):
        own = slice(index * rows, (index + 1) * rows)
        if side is None:
            picked[:, own] = jnp.swapaxes(lefts[index][...], 0, 1)
            continue
        if shard % 128:
            turned[...] = jnp.swapaxes(lefts[index][...], 0, 1)
        for half in range(halves):
            start = pl.multiple_of((2 * half + which) * shard, shard)
            if shard % 128:
                part = turned[pl.ds(start, shard), :]
            else:
                part = jnp.swapaxes(lefts[index][:, pl.ds(start, shard)], 0, 1)
            picked[half * shard : (half + 1) * shard, own] = part
    middle = rights[0].shape[0]
    for start in range(0, out_ref.shape[1], CHUNK):
        cols = slice(start, start + CHUNK)
        out = dot(picked[:, :middle], rights[0][:, cols], 1, 0)
        out = out + dot(picked[:, middle:], rights[1][:, cols], 1, 0)
        if extra:
            out = out + got_ref[:, cols].astype(f32)
        out_ref[:, cols] = out.astype(bf16)


def outer(lefts, rights, info, side=None, halves=1, got=None):
    rows, model = lefts[0].shape
    count = len(lefts)
    ff = rights[0].shape[1]
    extra = [] if got is None else [got]
    size = model if side is None else model // 2
    return pl.pallas_call(
        functools.partial(outer_kernel, count, side, halves, len(extra)),
        grid_spec=pltpu.PrefetchScalarGridSpec(
            num_scalar_prefetch=1,
            grid=(1,),
            in_specs=[VMEM] * (count + 2 + len(extra)),
            out_specs=VMEM,
            scratch_shapes=[pltpu.VMEM((size, count * rows), bf16), pltpu.VMEM((model, rows), bf16)],
        ),
        out_shape=jax.ShapeDtypeStruct((size, ff), bf16),
        compiler_params=pltpu.CompilerParams(vmem_limit_bytes=LIMIT),
        cost_estimate=pl.CostEstimate(
            flops=2 * count * rows * ff * size, bytes_accessed=10 * 2**20, transcendentals=0
        ),
        name="outer",
    )(info, *lefts, *rights, *extra)


def middle_outer_kernel(group, *refs):
    one, ctx_one, two, ctx_two, h, dq = refs[:6]
    outs = refs[6:]
    width = dq.shape[0] // group
    for index, (left, right) in enumerate(((one, ctx_one), (two, ctx_two), (h, dq))):
        turned = jnp.swapaxes(left[...], 0, 1)
        cols = slice(index * width, (index + 1) * width)
        for step in range(group):
            part = right[step * width : (step + 1) * width, :]
            outs[step][:, cols] = dot(turned, part, 1, 1).astype(bf16)


def middle_outer(one, ctx_one, two, ctx_two, h, dq, group):
    rows, model = one.shape
    width = dq.shape[0] // group
    return pl.pallas_call(
        functools.partial(middle_outer_kernel, group),
        in_specs=[VMEM] * 6,
        out_specs=[VMEM] * group,
        out_shape=[jax.ShapeDtypeStruct((model, 3 * width), bf16)] * group,
        compiler_params=pltpu.CompilerParams(vmem_limit_bytes=LIMIT),
        cost_estimate=pl.CostEstimate(
            flops=6 * rows * model * model, bytes_accessed=9 * 2**20, transcendentals=0
        ),
        name="middle_outer",
    )(one, ctx_one, two, ctx_two, h, dq)


def combine_kernel(extra, *refs):
    dq, dk, dv = refs[:3]
    gots, out = refs[3:-1], refs[-1]
    gots = gots[: len(gots) - extra]
    out[:, 0] = dq[...]
    for index, value in enumerate((dk, dv)):
        total = value[0]
        for got in gots[index::2]:
            total = total + got[...].astype(f32)
        out[:, 1 + index] = total.astype(bf16)


def combine(dq, dk, dv, got_k, got_v, after):
    heads, depth, piece = dq.shape
    gots = [got for pair in zip(got_k, got_v) for got in pair]
    return pl.pallas_call(
        functools.partial(combine_kernel, len(after)),
        in_specs=[VMEM] * (3 + len(gots)) + [ANY] * len(after),
        out_specs=VMEM,
        out_shape=jax.ShapeDtypeStruct((heads, 3, depth, piece), bf16),
        compiler_params=pltpu.CompilerParams(vmem_limit_bytes=LIMIT),
        cost_estimate=pl.CostEstimate(flops=2**20, bytes_accessed=5 * 2**20, transcendentals=0),
        name="combine",
    )(dq, dk, dv, *gots, *after)


def local(
    hidden,
    encoder,
    cotangent,
    block_ids,
    self_qkv,
    self_out,
    cross_qkv,
    cross_out,
    up_weight,
    down_weight,
    proj_bias,
    up_bias,
    norm_gain,
    norm_shift,
):
    tok_size, group = lax.axis_size("tok"), lax.axis_size("hd")
    tok_index, me = lax.axis_index("tok"), lax.axis_index("hd")
    rows, model = hidden.shape
    shard = self_qkv.shape[0]
    width = self_qkv.shape[2]
    ff_local = up_weight.shape[1]
    piece_rows = rows * group
    span = SEQ // piece_rows
    heads = min(width // HDIM, span)
    others = span // heads
    assert heads * HDIM == width and heads * others == span
    seq_count, enc_rows, _ = encoder.shape
    enc_total = enc_rows * group
    own_seq = tok_index // span
    at = lax.rem(tok_index, span) // others
    beside = jnp.bitwise_xor(lax.rem(tok_index, others), lax.rem(at, 2) * (others - 1))
    info = jnp.stack([at, beside, me, tok_index]).astype(jnp.int32)

    def natural(blocks):
        stacked = jnp.stack(blocks)
        return [pick(stacked, me ^ index) for index in range(group)]

    even = lax.rem(tok_index, 2)
    halves = [[i for i in range(tok_size) if i % 2 == side] for side in range(2)]
    many = tok_size // 2

    def gather_half(block):
        return lax.all_gather(block, "tok", axis=0, tiled=True, axis_index_groups=halves)

    def gather_tok(block):
        return lax.all_gather(block, "tok", axis=0, tiled=True)

    def along_halves(block):
        return lax.all_to_all(
            jnp.broadcast_to(block[None], (many, *block.shape)),
            "tok", 0, 0, tiled=True, axis_index_groups=halves,
        )

    def merge_sides(own, got):
        sides = [jnp.where(even == 0, own, got), jnp.where(even == 0, got, own)]
        return jnp.stack(sides, 1).reshape(model, -1)

    w_self = self_qkv.reshape(shard, 3, heads, HDIM).transpose(0, 2, 1, 3)
    w_self = gather_tok(w_self.reshape(shard, 3 * width))
    w_mid = along_halves(
        jnp.concatenate([self_out.T, cross_out.T, cross_qkv.reshape(shard, 3 * width)], 1)
    )

    own_ids = lax.dynamic_slice_in_dim(block_ids, me * rows, rows).astype(bf16)
    small = jnp.concatenate(
        [
            proj_bias.T.reshape(-1),
            norm_gain.T.reshape(-1),
            norm_shift.T.reshape(-1),
            up_bias,
            own_ids,
        ]
    )
    total_devices = tok_size * group
    small_all = lax.all_to_all(
        jnp.broadcast_to(small[None], (total_devices, small.shape[0])),
        ("tok", "hd"), 0, 0, tiled=True,
    ).astype(f32)
    few = model // total_devices
    vectors = small_all[:, : 13 * few].reshape(total_devices, 13, few)
    vectors = vectors.transpose(1, 0, 2).reshape(13, model)
    bias, gain, shift = vectors[:7], vectors[7:10], vectors[10:13]
    few_up = up_bias.shape[0]
    bias_up = small_all[:, 13 * few : 13 * few + few_up].reshape(-1)
    bias_up = lax.dynamic_slice_in_dim(bias_up, me * ff_local, ff_local)
    ids = small_all[:, 13 * few + few_up :].reshape(tok_size, 1, piece_rows)
    ids = lax.dynamic_slice_in_dim(ids, own_seq * span, span).reshape(heads, others, 1, piece_rows)
    ids = jnp.stack([pick(ids[i], beside ^ (i % 2 * (others - 1))) for i in range(heads)])

    def own_columns(vector):
        return lax.dynamic_slice_in_dim(vector, me * width, width)

    hidden_blocks = gather_xor(hidden)
    self_bias = jnp.stack(
        [own_columns(bias[0]), jnp.zeros((width,), f32), own_columns(bias[1])]
    )
    scale = jnp.broadcast_to(jnp.array([0.125, 1.0, 1.0], f32)[:, None], (3, width))
    factors = jnp.stack([self_bias, scale]).reshape(2, 3, heads, HDIM)
    factors = factors.transpose(0, 2, 1, 3).reshape(2, 3 * width)

    lines = [
        [seq * span + i * others + (side ^ (i % 2 * (others - 1))) for i in range(heads)]
        for seq in range(tok_size // span)
        for side in range(others)
    ]
    wide_lines = [[i * group + h for h in range(group) for i in line] for line in lines]

    def across_lines(value):
        return lax.all_to_all(value, "tok", 0, 0, tiled=True, axis_index_groups=lines)

    def across_wide(value):
        return lax.all_to_all(
            value, ("tok", "hd"), 0, 0, tiled=True, axis_index_groups=wide_lines
        )

    q_out, k_out, v_out, h_one = project(
        info, hidden_blocks, w_self, jnp.stack([gain[0], shift[0]]), factors, heads, [w_mid]
    )
    w_up, w_down = tie([up_weight, down_weight], [h_one])
    w_up, w_down = gather_tok(w_up), gather_tok(w_down.T)
    w_mid = merge_sides(w_mid, swap(w_mid, "tok", 1))
    k = [across_lines(k_out)]
    v = [across_lines(v_out)]
    q = across_lines(q_out)
    k += [swap(k[0], "tok", other) for other in range(1, others)]
    v += [swap(v[0], "tok", other) for other in range(1, others)]
    w_cross_kv = w_mid[:, 3 * width :]
    enc_all = jnp.concatenate(natural(gather_xor(encoder)), 1)
    kv_bias = jnp.concatenate([jnp.zeros((width,), f32), own_columns(bias[4])])
    kv_two = dot(w_cross_kv, pick(enc_all, own_seq), 0, 1) + kv_bias[:, None]
    kv_two = kv_two.astype(bf16).reshape(2, width, enc_total)
    kv_two = gather_xor(kv_two)

    context, log_one = self_forward(info, q, k, v, ids, rows, kv_two)

    mid_block = jnp.stack(
        [w_mid[:, :width], w_mid[:, width : 2 * width], w_mid[:, 2 * width : 3 * width]]
    )
    w_blocks = gather_xor(mid_block, lambda value: tie([value], [log_one])[0])
    ctx_one = across_wide(context).reshape(model, rows)
    norm_rows = jnp.stack([gain[1], shift[1], gain[2], shift[2], bias[2], bias[5]])
    (
        resid_two, unit_two, inv_two, unit_three, inv_three,
        h_two, h_three, ctx_one, q_two, ctx_two, log_two,
    ) = middle_forward(
        info, hidden, ctx_one, norm_rows, bias[3:4], w_blocks, kv_two, heads, []
    )

    cot_blocks = gather_xor(cotangent)
    grad_a = grad_act(cot_blocks, w_down)
    h_blocks = gather_xor(h_three, lambda got: tie([got], [grad_a])[0])
    near = group // 2
    bias_row = bias_up[None]
    near_out = feed(h_blocks[:near], grad_a, w_up, bias_row, 0)
    far_out = feed(h_blocks[near:], grad_a, w_up, bias_row, near)
    acts, grad_inners = [near_out[0], far_out[0]], [near_out[1], far_out[1]]
    up_sums = (near_out[2] + far_out[2])[0]
    grad_h_three = reduce_xor(list(near_out[3:]) + list(far_out[3:]))

    def half_columns(array, side):
        return jnp.concatenate(
            [
                lax.dynamic_slice_in_dim(array, (2 * i + side) * shard, shard, 1)
                for i in range(tok_size // 2)
            ],
            1,
        )

    def half_rows(array, side):
        return jnp.concatenate(
            [
                lax.dynamic_slice_in_dim(array, (2 * i + side) * shard, shard, 0)
                for i in range(tok_size // 2)
            ],
            0,
        )

    def reduce_tok(value):
        return lax.psum_scatter(value, "tok", scatter_dimension=0, tiled=True)

    def reduce_half(value):
        return lax.psum_scatter(
            value, "tok", scatter_dimension=0, tiled=True, axis_index_groups=halves
        )

    grad_up = outer(h_blocks, grad_inners, info)
    down_away = outer(cot_blocks, acts, info, 1, many)
    sent_up = reduce_tok(grad_up)
    down_got = swap(down_away, "tok", 1)

    grad_one, grad_two_low, grad_one_low, grad_q_two, grad_kv_two, grad_ctx_one, sums = (
        middle_backward(
            info, grad_h_three, cotangent,
            (unit_two, inv_two, unit_three, inv_three, q_two, ctx_two, log_two),
            norm_rows, w_blocks, kv_two, heads, [grad_up, down_away],
        )
    )
    grad_heads = across_wide(grad_ctx_one.reshape(group * heads, HDIM, rows))
    grad_mid = middle_outer(
        grad_one_low, ctx_one, grad_two_low, ctx_two, h_two, grad_q_two, group
    )
    masks = [1 << bit for bit in range(tok_size.bit_length() - 1)]

    def add_low(value, got):
        return (value.astype(f32) + got.astype(f32)).astype(bf16)

    grad_q_away, grad_k_away, grad_v_away = self_backward(
        info, q, k[1:], v[1:], None, grad_heads, context, log_one, None, grad_mid
    )
    down_got = tie([down_got], [grad_q_away])[0]
    down_sum = outer(cot_blocks, acts, info, 0, many, down_got)
    sent_down = reduce_half(tie([down_sum], [sent_up])[0])
    kv_total = reduce_xor(
        [grad_kv_two[j] for j in range(group)], lambda got: tie([got], [grad_q_away])[0]
    )
    seq_pick = jnp.arange(seq_count) == own_seq
    kv_total = jnp.where(seq_pick[:, None, None, None], kv_total[None], 0.0).astype(bf16)
    grad_mid = reduce_xor(grad_mid, lambda got: tie([got], [grad_q_away])[0])
    mid_got = swap(half_rows(grad_mid, 1 - even).astype(bf16), "tok", 1)
    mid_sum = (half_rows(grad_mid, even) + mid_got.astype(f32)).astype(bf16)
    sent_mid = reduce_half(tie([mid_sum], [sent_down])[0])
    grad_k_got = [swap(grad_k_away[i], "tok", i + 1) for i in range(others - 1)]
    grad_v_got = [swap(grad_v_away[i], "tok", i + 1) for i in range(others - 1)]
    grad_q, grad_k, grad_v = self_backward(
        info, q, k[:1], v[:1], ids, grad_heads, context, log_one, grad_q_away, [down_sum]
    )
    kv_got = swap(kv_total, "tok", masks[0])
    grad_qkv = combine(grad_q, grad_k, grad_v, grad_k_got, grad_v_got, [sent_up, kv_got])
    kv_total = add_low(kv_total, kv_got)
    acts = tie(acts, [grad_q])
    def act_block(index):
        start = index % near * rows
        return acts[index // near][start : start + rows]

    final = reduce_xor([dot(act_block(j), w_down, 1, 1) for j in range(group)])
    output = (resid_two + final + bias[6]).astype(bf16)
    grad_qkv = across_lines(grad_qkv).reshape(3 * width, piece_rows)
    kv_got = swap(kv_total, "tok", masks[1])
    grad_qkv, sent_down, kv_got = tie([grad_qkv, sent_down, kv_got], [])
    kv_total = add_low(kv_total, kv_got)
    for got_mask in masks[2:]:
        kv_total = add_low(kv_total, swap(kv_total, "tok", got_mask))
    kv_flat = kv_total.reshape(seq_count, 2 * width, enc_total)
    own_enc = lax.dynamic_slice_in_dim(enc_all, tok_index * shard, shard, 2)
    sent_cross_kv = sum(dot(own_enc[n], kv_flat[n], 0, 1) for n in range(seq_count))

    def encoder_part(index):
        start = (me ^ index) * enc_rows
        return jnp.stack(
            [
                dot(lax.dynamic_slice_in_dim(kv_flat[n], start, enc_rows, 1), w_cross_kv, 0, 1)
                for n in range(seq_count)
            ]
        )

    grad_encoder = reduce_xor([encoder_part(j) for j in range(group)])

    grad_self = dot(h_one, grad_qkv, 0, 1).astype(bf16)
    sent_self = lax.all_to_all(grad_self, "tok", 0, 0, tiled=True)
    ordered = sent_self
    sent_self = jnp.sum(sent_self.reshape(tok_size, shard, 3 * width).astype(f32), 0)
    sent_self = sent_self.reshape(shard, heads, 3, HDIM)
    sent_self = sent_self.transpose(0, 2, 1, 3).reshape(shard, 3, width)
    grad_qkv = tie([grad_qkv], [grad_self])[0]
    grad_h_one = reduce_xor(
        [
            dot(
                lax.dynamic_slice(grad_qkv, (0, (me ^ j) * rows), (3 * width, rows)), w_self, 0, 1
            )
            for j in range(group)
        ]
    )
    unit_one, inverse_one = normalize(hidden.astype(f32))
    back, gain_one, shift_one = norm_backward(grad_h_one, unit_one, inverse_one, gain[0])
    grad_hidden = grad_one + back

    def place(vector):
        return lax.dynamic_update_slice_in_dim(jnp.zeros((model,), f32), vector, me * width, 0)

    qkv_sums = jnp.sum(grad_qkv.astype(f32), 1).reshape(heads, 3, HDIM)
    once = (tok_index == 0).astype(f32)
    late = jnp.concatenate(
        [
            place(qkv_sums[:, 0].reshape(-1)),
            place(qkv_sums[:, 2].reshape(-1)),
            place(jnp.sum(kv_flat[:, width:].astype(f32), (0, 2)) * once),
            gain_one,
            shift_one,
        ]
    )
    vectors = jnp.concatenate([sums, late.reshape(5, model)], 0)
    vectors = vectors.reshape(13, total_devices, few).transpose(1, 0, 2).reshape(total_devices, -1)
    up_all = lax.dynamic_update_slice_in_dim(
        jnp.zeros((group * ff_local,), f32), up_sums, me * ff_local, 0
    )
    vectors = jnp.concatenate([vectors, up_all.reshape(total_devices, -1)], 1)
    vectors = tie([vectors], [ordered])[0]
    vectors = jnp.sum(lax.all_to_all(vectors, ("tok", "hd"), 0, 0, tiled=True), 0)
    columns = vectors[: 13 * few].reshape(13, few)
    columns = columns[jnp.array([8, 9, 5, 7, 10, 4, 6, 11, 2, 0, 12, 3, 1])].T

    sent_mid = sent_mid.astype(f32)
    sent_mid = [sent_mid[:, j * width : (j + 1) * width] for j in range(3)]
    sent_cross = jnp.concatenate(
        [sent_mid[2][:, None], sent_cross_kv.reshape(shard, 2, width)], 1
    )
    return (
        output,
        grad_hidden,
        grad_encoder,
        sent_self,
        sent_mid[0].T,
        sent_cross,
        sent_mid[1].T,
        sent_up.astype(f32),
        sent_down.astype(f32).T,
        columns[:, :7],
        vectors[13 * few :],
        columns[:, 7:10],
        columns[:, 10:13],
    )


def solution(mesh):
    in_specs = (
        P(("tok", "hd"), None),
        P(None, "hd", None),
        P(("tok", "hd"), None),
        P("tok"),
        P("tok", None, "hd"),
        P("hd", "tok"),
        P("tok", None, "hd"),
        P("hd", "tok"),
        P("tok", "hd"),
        P("hd", "tok"),
        P(("tok", "hd"), None),
        P(("tok", "hd")),
        P(("tok", "hd"), None),
        P(("tok", "hd"), None),
    )
    out_specs = (
        P(("tok", "hd"), None),
        P(("tok", "hd"), None),
        P(None, "hd", None),
        P("tok", None, "hd"),
        P("hd", "tok"),
        P("tok", None, "hd"),
        P("hd", "tok"),
        P("tok", "hd"),
        P("hd", "tok"),
        P(("tok", "hd"), None),
        P(("tok", "hd")),
        P(("tok", "hd"), None),
        P(("tok", "hd"), None),
    )
    return jax.shard_map(local, mesh=mesh, in_specs=in_specs, out_specs=out_specs, check_vma=False)
```

```python
import functools

import jax
import jax.numpy as jnp
from jax import lax
from jax.experimental import pallas as pl
from jax.experimental.pallas import tpu as pltpu
from jax.sharding import PartitionSpec as P

HDIM = 64
SEQ = 8192
TILE = 512
norm_eps = 1e-05
neg_large = -1e30
f32 = jnp.float32
bf16 = jnp.bfloat16


def dot(left, right, left_dim, right_dim):
    return lax.dot_general(
        left, right, (((left_dim,), (right_dim,)), ((), ())), preferred_element_type=f32
    )


def swap(value, axis, mask):
    return lax.ppermute(value, axis, [(i, i ^ mask) for i in range(lax.axis_size(axis))])


def hd_masks():
    mask, masks = lax.axis_size("hd") // 2, []
    while mask:
        masks.append(mask)
        mask //= 2
    return masks


def gather_xor(value, first=lambda value: value):
    have = {0: value}
    for mask in hd_masks():
        for index in list(have):
            have[index ^ mask] = first(swap(have[index], "hd", mask))
        first = lambda value: value
    return [have[index] for index in range(len(have))]


def reduce_xor(parts, last=lambda value: value):
    have = dict(enumerate(parts))
    for mask in reversed(hd_masks()):
        for index in sorted(have, reverse=True):
            if index & mask:
                got = swap(have.pop(index).astype(bf16), "hd", mask)
                if len(have) == 1:
                    got = last(got)
                total = have[index ^ mask].astype(f32) + got.astype(f32)
                have[index ^ mask] = total if len(have) == 1 else total.astype(bf16)
    return have[0]


def pick(stacked, index):
    return lax.dynamic_index_in_dim(stacked, index, 0, keepdims=False)


def normalize(value):
    center = value - jnp.mean(value, axis=-1, keepdims=True)
    inverse = lax.rsqrt(jnp.mean(center * center, axis=-1, keepdims=True) + norm_eps)
    return center * inverse, inverse


def norm_backward(grad, unit, inverse, gain):
    scaled = grad * gain
    back = (
        scaled
        - jnp.mean(scaled, axis=-1, keepdims=True)
        - unit * jnp.mean(scaled * unit, axis=-1, keepdims=True)
    ) * inverse
    return back, jnp.sum(grad * unit, axis=0), jnp.sum(grad, axis=0)


def column(row, rows):
    return jnp.swapaxes(jnp.broadcast_to(row, (128, rows)), 0, 1)[:, :1]


VMEM = pl.BlockSpec(memory_space=pltpu.VMEM)
LIMIT = 48 * 2**20


ANY = pl.BlockSpec(memory_space=pl.ANY)


def tie(values, after):
    count = len(values)
    return pl.pallas_call(
        lambda *refs: None,
        in_specs=[ANY] * (count + len(after)),
        out_specs=[ANY] * count,
        out_shape=[jax.ShapeDtypeStruct(value.shape, value.dtype) for value in values],
        input_output_aliases={index: index for index in range(count)},
        name="tie",
    )(*values, *after)


def project_kernel(heads, group, info, *refs):
    refs = list(refs)
    w_ref, norm_ref, bias_ref = refs[:3]
    q_ref, k_ref, v_ref, h_ref = refs[-4:]
    x_refs = refs[3 : 3 + group]
    rows = x_refs[0].shape[0]
    for step, x_ref in enumerate(x_refs):
        start = pl.multiple_of(jnp.bitwise_xor(info[2], step) * rows, rows)
        cols = pl.ds(start, rows)
        x = x_ref[...].astype(f32)
        h = (normalize(x)[0] * norm_ref[0:1, :] + norm_ref[1:2, :]).astype(bf16)
        h_ref[cols, :] = h
        out = (dot(h, w_ref[...], 1, 0) + bias_ref[0:1, :]) * bias_ref[1:2, :]
        out = jnp.swapaxes(out.astype(bf16), 0, 1)
        for head in range(heads):
            for part, ref in enumerate((q_ref, k_ref, v_ref)):
                first = (head * 3 + part) * HDIM
                ref[head, :, cols] = out[first : first + HDIM]


def project(info, x, w, norm, bias, heads, after):
    rows, model = x[0].shape
    group = len(x)
    piece = rows * group
    width = w.shape[1]
    return pl.pallas_call(
        functools.partial(project_kernel, heads, group),
        grid_spec=pltpu.PrefetchScalarGridSpec(
            num_scalar_prefetch=1,
            grid=(1,),
            in_specs=[VMEM] * (group + 3) + [ANY] * len(after),
            out_specs=[VMEM] * 4,
        ),
        out_shape=[jax.ShapeDtypeStruct((heads, HDIM, piece), bf16)] * 3
        + [jax.ShapeDtypeStruct((piece, model), bf16)],
        compiler_params=pltpu.CompilerParams(vmem_limit_bytes=LIMIT),
        cost_estimate=pl.CostEstimate(
            flops=2 * piece * model * width, bytes_accessed=8 * 2**20, transcendentals=piece
        ),
        name="project",
    )(info, w, norm, bias, *x, *after)


def flip(place, others):
    return lax.rem(place, 2) * (others - 1)


def self_forward_kernel(heads, others, info, *refs):
    q_ref, id_ref = refs[:2]
    k_refs, v_refs = refs[2 : 2 + others], refs[2 + others : 2 + 2 * others]
    o_ref, l_ref, k_all, v_all, wait_a, wait_b = refs[-6:]
    beside = info[1]
    step = pl.program_id(0)
    piece_rows = q_ref.shape[2]
    assert piece_rows == 2 * TILE
    per = piece_rows // TILE
    slot, tile = step // per, lax.rem(step, per)

    @pl.when(step == 0)
    def _():
        for other in range(others):
            for place in range(heads):
                k_all[other, place] = jnp.swapaxes(k_refs[other][place], 0, 1)
                v_all[other, place] = v_refs[other][place]

    piece = slot * others + jnp.bitwise_xor(beside, flip(slot, others))
    cols = pl.ds(pl.multiple_of(tile * TILE, TILE), TILE)
    q = q_ref[slot, :, cols]

    def ahead(wait, keys, top, mask=None):
        scores = dot(keys, q, 1, 0)
        if mask is not None:
            scores = jnp.where(mask, scores, neg_large)
        wait[...] = scores
        return jnp.maximum(top, jnp.max(scores, axis=0, keepdims=True))

    def finish(wait, values, top, fade, total, acc):
        probs = jnp.exp(wait[...] - top)
        total = total * fade + jnp.sum(probs, axis=0, keepdims=True)
        return total, acc * fade + dot(values, probs.astype(bf16), 1, 0)

    def locate(index):
        place = index // others
        side = jnp.bitwise_xor(beside, flip(place, others))
        return jnp.bitwise_xor(lax.rem(index, others), side), place

    def waiting(index):
        other, place = locate(jnp.maximum(index - 1, 0))
        other, place = jnp.where(index == 0, 0, other), jnp.where(index == 0, slot, place)
        start = jnp.where(index == 0, 0, TILE)
        return v_all[other, place, :, pl.ds(pl.multiple_of(start, TILE), TILE)]

    def earlier_tile(state):
        top, fade, total, acc = state
        new_top = ahead(wait_b, k_all[0, slot, :TILE, :], top)
        total, acc = finish(wait_a, v_all[0, slot, :, cols], top, fade, total, acc)
        wait_a[...] = wait_b[...]
        return new_top, jnp.exp(top - new_top), total, acc

    def earlier_piece(index, state):
        top, fade, total, acc = state
        other, place = locate(index)
        new_top = ahead(wait_b, k_all[other, place, :TILE, :], top)
        total, acc = finish(wait_a, waiting(index), top, fade, total, acc)
        fade, top = jnp.exp(top - new_top), new_top
        new_top = ahead(wait_a, k_all[other, place, TILE:, :], top)
        total, acc = finish(wait_b, v_all[other, place, :, :TILE], top, fade, total, acc)
        return new_top, jnp.exp(top - new_top), total, acc

    ids = id_ref[slot, :, cols]
    mask = column(ids, TILE) <= ids
    top = ahead(wait_a, k_all[0, slot, cols, :], jnp.full((1, TILE), neg_large, f32), mask)
    state = (
        top,
        jnp.ones((1, TILE), f32),
        jnp.zeros((1, TILE), f32),
        jnp.zeros((HDIM, TILE), f32),
    )
    state = lax.cond(tile == 1, earlier_tile, lambda state: state, state)
    top, fade, total, acc = lax.fori_loop(0, piece, earlier_piece, state)
    total, acc = finish(wait_a, waiting(piece), top, fade, total, acc)
    out = (acc / total).astype(o_ref.dtype)
    rows = o_ref.shape[2]
    for index in range(TILE // rows):
        place = (tile * (TILE // rows) + index) * heads + slot
        o_ref[place] = out[:, index * rows : (index + 1) * rows]
    l_ref[slot, :, cols] = top + jnp.log(total)


def self_forward(info, q, k, v, ids, rows, after):
    others = len(k)
    heads, depth, piece = q.shape
    area = heads * piece * heads * others * piece // 2
    return pl.pallas_call(
        functools.partial(self_forward_kernel, heads, others),
        grid_spec=pltpu.PrefetchScalarGridSpec(
            num_scalar_prefetch=1,
            grid=(heads * piece // TILE,),
            in_specs=[VMEM] * (2 + 2 * others) + [ANY] * len(after),
            out_specs=[VMEM] * 2,
            scratch_shapes=[
                pltpu.VMEM((others, heads, piece, depth), bf16),
                pltpu.VMEM((others, heads, depth, piece), bf16),
                pltpu.VMEM((TILE, TILE), f32),
                pltpu.VMEM((TILE, TILE), f32),
            ],
        ),
        out_shape=[
            jax.ShapeDtypeStruct((piece // rows * heads, depth, rows), bf16),
            jax.ShapeDtypeStruct((heads, 1, piece), f32),
        ],
        compiler_params=pltpu.CompilerParams(vmem_limit_bytes=LIMIT),
        cost_estimate=pl.CostEstimate(
            flops=area * 1024, bytes_accessed=8 * 2**20, transcendentals=area
        ),
        name="self_forward",
    )(info, q, ids, *k, *v, *after)


def self_backward_kernel(heads, sides, own, extra, info, *refs):
    refs = list(refs)
    q_ref, g_ref, o_ref, l_ref = refs[:4]
    k_refs, v_refs = refs[4 : 4 + sides], refs[4 + sides : 4 + 2 * sides]
    refs = refs[4 + 2 * sides :]
    id_ref, before_ref = (refs.pop(0), refs.pop(0)) if own else (None, None)
    dq_ref, dk_ref, dv_ref, g_all, inner_all, k_all, v_all, dk, dv = refs[extra:]
    beside = info[1]
    step = pl.program_id(0)
    piece_rows = q_ref.shape[2]
    per = piece_rows // TILE
    slot, tile = step // per, lax.rem(step, per)

    @pl.when(step == 0)
    def _():
        rows = g_ref.shape[2]
        for place in range(heads):
            for index in range(piece_rows // rows):
                at = slice(index * rows, (index + 1) * rows)
                grad = g_ref[index * heads + place]
                g_all[place, :, at] = grad
                inner_all[place, :, at] = jnp.sum(
                    o_ref[index * heads + place].astype(f32) * grad.astype(f32),
                    axis=0,
                    keepdims=True,
                )
            for side in range(sides):
                k_all[side, place] = jnp.swapaxes(k_refs[side][place], 0, 1)
                v_all[side, place] = jnp.swapaxes(v_refs[side][place], 0, 1)
        dk[...] = jnp.zeros_like(dk)
        dv[...] = jnp.zeros_like(dv)

    cols = pl.ds(pl.multiple_of(tile * TILE, TILE), TILE)
    q = q_ref[slot, :, cols]
    grad = g_all[slot, :, cols]
    q_rows = jnp.swapaxes(q, 0, 1)
    grad_rows = jnp.swapaxes(grad, 0, 1)
    log_total = l_ref[slot, :, cols]
    inner = inner_all[slot, :, cols]

    def update(dq, side, place, rows, mask):
        scores = dot(k_all[side, place, rows, :], q, 1, 0)
        if mask is not None:
            scores = jnp.where(mask, scores, neg_large)
        probs = jnp.exp(scores - log_total)
        grad_probs = dot(v_all[side, place, rows, :], grad, 1, 0)
        grad_scores = (probs * (grad_probs - inner)).astype(bf16)
        dv[side, place, rows, :] += dot(probs.astype(bf16), grad_rows, 1, 0)
        dk[side, place, rows, :] += dot(grad_scores, q_rows, 1, 0)
        return dq + dot(k_refs[side][place, :, rows], grad_scores, 1, 0)

    dq = before_ref[slot, :, cols] if own else jnp.zeros((HDIM, TILE), f32)
    for side in range(sides):

        def earlier(place, dq, side=side):
            for start in range(0, piece_rows, TILE):
                dq = update(dq, side, place, slice(start, start + TILE), None)
            return dq

        if own:
            count = slot
        else:
            here = jnp.bitwise_xor(beside, flip(slot, sides + 1))
            count = slot + jnp.where(jnp.bitwise_xor(here, side + 1) < here, 1, 0)
        dq = lax.fori_loop(0, count, earlier, dq)
    if own:

        def earlier_tile(index, dq):
            rows = pl.ds(pl.multiple_of(index * TILE, TILE), TILE)
            return update(dq, 0, slot, rows, None)

        dq = lax.fori_loop(0, tile, earlier_tile, dq)
    if own:
        ids = id_ref[slot, :, cols]
        mask = column(ids, TILE) <= ids
        dq = update(dq, 0, slot, cols, mask) * 0.125
    dq_ref[slot, :, cols] = dq.astype(dq_ref.dtype)

    @pl.when(step == heads * per - 1)
    def _():
        for side in range(sides):
            for place in range(heads):
                dk_ref[side, place] = jnp.swapaxes(dk[side, place], 0, 1).astype(dk_ref.dtype)
                dv_ref[side, place] = jnp.swapaxes(dv[side, place], 0, 1).astype(dv_ref.dtype)


def self_backward(info, q, k, v, ids, grad, context, log_total, before, after):
    own = ids is not None
    sides = len(k)
    heads, depth, piece = q.shape
    flat = [q, grad, context, log_total, *k, *v] + ([ids, before] if own else [])
    area = heads * piece * heads * sides * piece // 2
    return pl.pallas_call(
        functools.partial(self_backward_kernel, heads, sides, own, len(after)),
        grid_spec=pltpu.PrefetchScalarGridSpec(
            num_scalar_prefetch=1,
            grid=(heads * piece // TILE,),
            in_specs=[VMEM] * len(flat) + [ANY] * len(after),
            out_specs=[VMEM] * 3,
            scratch_shapes=[
                pltpu.VMEM((heads, depth, piece), bf16),
                pltpu.VMEM((heads, 1, piece), f32),
                pltpu.VMEM((sides, heads, piece, depth), bf16),
                pltpu.VMEM((sides, heads, piece, depth), bf16),
                pltpu.VMEM((sides, heads, piece, depth), f32),
                pltpu.VMEM((sides, heads, piece, depth), f32),
            ],
        ),
        out_shape=[jax.ShapeDtypeStruct((heads, depth, piece), bf16 if own else f32)]
        + [jax.ShapeDtypeStruct((sides, heads, depth, piece), f32 if own else bf16)] * 2,
        compiler_params=pltpu.CompilerParams(vmem_limit_bytes=LIMIT),
        cost_estimate=pl.CostEstimate(
            flops=area * 64, bytes_accessed=2**16, transcendentals=0
        ),
        name="self_backward",
    )(info, *flat, *after)


def gelu_parts(value):
    half = 0.5 * (1.0 + lax.erf(value * 0.7071067811865476))
    slope = half + value * jnp.exp(-0.5 * value * value) * 0.3989422804014327
    return value * half, slope


def middle_forward_kernel(group, heads, info, *refs):
    x_ref, ctx_ref, norm_ref, bias_ref = refs[:4]
    w_refs, kv_refs = refs[4 : 4 + group], refs[4 + group : 4 + 2 * group]
    x_two, unit_two, inv_two, unit_three, inv_three, h_two, h_three, ctx_xor, q, ctx, log = refs[-11:]
    width = heads * HDIM
    me = info[2]

    def natural(step):
        return pl.ds(pl.multiple_of(jnp.bitwise_xor(me, step) * width, width), width)

    resid = x_ref[...].astype(f32) + norm_ref[4:5, :]
    for step in range(group):
        part = ctx_ref[natural(step), :]
        ctx_xor[step * width : (step + 1) * width, :] = part
        resid = resid + dot(jnp.swapaxes(part, 0, 1), w_refs[step][0], 1, 1)
    unit, inverse = normalize(resid)
    unit_two[...] = unit
    inv_two[...] = inverse
    low = (unit * norm_ref[0:1, :] + norm_ref[1:2, :]).astype(bf16)
    h_two[...] = low
    for step in range(group):
        out = (dot(low, w_refs[step][2], 1, 0) + bias_ref[:, natural(step)]) * 0.125
        q[step * width : (step + 1) * width, :] = jnp.swapaxes(out.astype(bf16), 0, 1)
    resid = resid + norm_ref[5:6, :]
    for step in range(group):
        for head in range(heads):
            own = slice(head * HDIM, (head + 1) * HDIM)
            rows = slice(step * width + head * HDIM, step * width + (head + 1) * HDIM)
            scores = dot(jnp.swapaxes(kv_refs[step][0, own, :], 0, 1), q[rows, :], 1, 0)
            top = jnp.max(scores, axis=0, keepdims=True)
            probs = jnp.exp(scores - top)
            total = jnp.sum(probs, axis=0, keepdims=True)
            out = dot(kv_refs[step][1, own, :], probs.astype(bf16), 1, 0)
            ctx[rows, :] = (out / total).astype(bf16)
            log[step * heads + head] = top + jnp.log(total)
        part = ctx[step * width : (step + 1) * width, :]
        resid = resid + dot(jnp.swapaxes(part, 0, 1), w_refs[step][1], 1, 1)
    x_two[...] = resid
    unit, inverse = normalize(resid)
    unit_three[...] = unit
    inv_three[...] = inverse
    h_three[...] = (unit * norm_ref[2:3, :] + norm_ref[3:4, :]).astype(bf16)


def middle_forward(info, x, ctx, norm, bias, w, kv, heads, after):
    rows, model = x.shape
    group = len(w)
    total = ctx.shape[0]
    shapes = [
        jax.ShapeDtypeStruct((rows, model), f32),
        jax.ShapeDtypeStruct((rows, model), f32),
        jax.ShapeDtypeStruct((rows, 1), f32),
        jax.ShapeDtypeStruct((rows, model), f32),
        jax.ShapeDtypeStruct((rows, 1), f32),
        jax.ShapeDtypeStruct((rows, model), bf16),
        jax.ShapeDtypeStruct((rows, model), bf16),
        jax.ShapeDtypeStruct((total, rows), bf16),
        jax.ShapeDtypeStruct((total, rows), bf16),
        jax.ShapeDtypeStruct((total, rows), bf16),
        jax.ShapeDtypeStruct((total // HDIM, 1, rows), f32),
    ]
    return pl.pallas_call(
        functools.partial(middle_forward_kernel, group, heads),
        grid_spec=pltpu.PrefetchScalarGridSpec(
            num_scalar_prefetch=1,
            grid=(1,),
            in_specs=[VMEM] * (4 + 2 * group) + [ANY] * len(after),
            out_specs=[
                VMEM if index == 6 else pl.BlockSpec(shape.shape, lambda *_, n=len(shape.shape): (0,) * n)
                for index, shape in enumerate(shapes)
            ],
        ),
        out_shape=shapes,
        compiler_params=pltpu.CompilerParams(vmem_limit_bytes=LIMIT),
        cost_estimate=pl.CostEstimate(
            flops=6 * rows * model * total, bytes_accessed=12 * 2**20, transcendentals=2**20
        ),
        name="middle_forward",
    )(info, x, ctx, norm, bias, *w, *kv, *after)


def middle_backward_kernel(group, heads, extra, info, *refs):
    e_ref, cot_ref, unit_two, inv_two, unit_three, inv_three, norm_ref, q, ctx, log = refs[:10]
    w_refs, kv_refs = refs[10 : 10 + group], refs[10 + group : 10 + 2 * group]
    d_one, low_two, low_one, dq, dkv, d_ctx, sums = refs[10 + 2 * group + extra :]
    width = heads * HDIM
    me = info[2]

    def natural(step):
        return pl.ds(pl.multiple_of(jnp.bitwise_xor(me, step) * width, width), width)

    def add(row, value):
        sums[row : row + 1, :] = jnp.sum(value, axis=0, keepdims=True)

    def norm_back(grad, unit, inverse, gain, row):
        add(row, grad * unit)
        add(row + 1, grad)
        scaled = grad * gain
        return (
            scaled
            - jnp.mean(scaled, axis=-1, keepdims=True)
            - unit * jnp.mean(scaled * unit, axis=-1, keepdims=True)
        ) * inverse

    cot = cot_ref[...].astype(f32)
    d_two = cot + norm_back(e_ref[...], unit_three[...], inv_three[...], norm_ref[2:3, :], 0)
    low = d_two.astype(bf16)
    low_two[...] = low
    add(4, low.astype(f32))
    add(6, cot)
    e_two = jnp.zeros_like(d_two)
    for step in range(group):
        grads = jnp.swapaxes(dot(low, w_refs[step][1], 1, 0).astype(bf16), 0, 1)
        for head in range(heads):
            own = slice(head * HDIM, (head + 1) * HDIM)
            rows = slice(step * width + head * HDIM, step * width + (head + 1) * HDIM)
            grad = grads[own]
            inner = jnp.sum(ctx[rows, :].astype(f32) * grad.astype(f32), axis=0, keepdims=True)
            k_t = kv_refs[step][0, own, :]
            scores = dot(jnp.swapaxes(k_t, 0, 1), q[rows, :], 1, 0)
            probs = jnp.exp(scores - log[step * heads + head])
            grad_probs = dot(jnp.swapaxes(kv_refs[step][1, own, :], 0, 1), grad, 1, 0)
            grad_scores = (probs * (grad_probs - inner)).astype(bf16)
            dq[rows, :] = (dot(k_t, grad_scores, 1, 0) * 0.125).astype(bf16)
            dkv[step, 0, own, :] = dot(q[rows, :], grad_scores, 1, 1)
            dkv[step, 1, own, :] = dot(grad, probs.astype(bf16), 1, 1)
        part = jnp.swapaxes(dq[step * width : (step + 1) * width, :], 0, 1)
        sums[7:8, natural(step)] = jnp.sum(part.astype(f32), axis=0, keepdims=True)
        e_two = e_two + dot(part, w_refs[step][2], 1, 1)
    d_next = d_two + norm_back(e_two, unit_two[...], inv_two[...], norm_ref[0:1, :], 2)
    d_one[...] = d_next
    low = d_next.astype(bf16)
    low_one[...] = low
    add(5, low.astype(f32))
    for step in range(group):
        grads = dot(low, w_refs[step][0], 1, 0).astype(bf16)
        d_ctx[natural(step), :] = jnp.swapaxes(grads, 0, 1)


def middle_backward(info, e, cot, saved, norm, w, kv, heads, after):
    unit_two, inv_two, unit_three, inv_three, q, ctx, log = saved
    rows, model = cot.shape
    group = len(w)
    total = q.shape[0]
    enc = kv[0].shape[2]
    return pl.pallas_call(
        functools.partial(middle_backward_kernel, group, heads, len(after)),
        grid_spec=pltpu.PrefetchScalarGridSpec(
            num_scalar_prefetch=1,
            grid=(1,),
            in_specs=[VMEM] * (10 + 2 * group) + [ANY] * len(after),
            out_specs=[VMEM] * 7,
        ),
        out_shape=[
            jax.ShapeDtypeStruct((rows, model), f32),
            jax.ShapeDtypeStruct((rows, model), bf16),
            jax.ShapeDtypeStruct((rows, model), bf16),
            jax.ShapeDtypeStruct((total, rows), bf16),
            jax.ShapeDtypeStruct((group, 2, heads * HDIM, enc), f32),
            jax.ShapeDtypeStruct((total, rows), bf16),
            jax.ShapeDtypeStruct((8, model), f32),
        ],
        compiler_params=pltpu.CompilerParams(vmem_limit_bytes=LIMIT),
        cost_estimate=pl.CostEstimate(
            flops=6 * rows * model * total, bytes_accessed=16 * 2**20, transcendentals=2**20
        ),
        name="middle_backward",
    )(info, e, cot, unit_two, inv_two, unit_three, inv_three, norm, q, ctx, log, *w, *kv, *after)


CHUNK = 512


def grad_act_kernel(*refs):
    w_ref, out_ref = refs[-2:]
    rows = refs[0].shape[0]
    for index, ref in enumerate(refs[:-2]):
        for start in range(0, w_ref.shape[1], CHUNK):
            cols = slice(start, start + CHUNK)
            out_ref[index * rows : (index + 1) * rows, cols] = dot(
                ref[...], w_ref[:, cols], 1, 0
            ).astype(bf16)


def grad_act(cots, w):
    rows, ff = cots[0].shape[0] * len(cots), w.shape[1]
    return pl.pallas_call(
        grad_act_kernel,
        in_specs=[VMEM] * (len(cots) + 1),
        out_specs=VMEM,
        out_shape=jax.ShapeDtypeStruct((rows, ff), bf16),
        compiler_params=pltpu.CompilerParams(vmem_limit_bytes=LIMIT),
        cost_estimate=pl.CostEstimate(
            flops=2 * rows * ff * w.shape[0], bytes_accessed=10 * 2**20, transcendentals=0
        ),
        name="grad_act",
    )(*cots, w)


def feed_kernel(first, blocks, *refs):
    h_refs, (ga_ref, b_ref, w_ref) = refs[:blocks], refs[blocks : blocks + 3]
    refs = refs[blocks + 3 :]
    act_ref, du_ref, sum_ref, e_refs = refs[0], refs[1], refs[2], refs[3 : 3 + blocks]
    rows, ff = h_refs[0].shape[0], w_ref.shape[1]
    totals = [0.0] * blocks
    for start in range(0, ff, CHUNK):
        cols = slice(start, start + CHUNK)
        sums = 0.0
        for index in range(blocks):
            own = slice(index * rows, (index + 1) * rows)
            inner = dot(h_refs[index][...], w_ref[:, cols], 1, 0) + b_ref[:, cols]
            act, slope = gelu_parts(inner)
            act_ref[own, cols] = act.astype(bf16)
            there = slice((first + index) * rows, (first + index + 1) * rows)
            du = (slope * ga_ref[there, cols].astype(f32)).astype(bf16)
            du_ref[own, cols] = du
            sums = sums + jnp.sum(du.astype(f32), axis=0, keepdims=True)
            totals[index] = totals[index] + dot(du, w_ref[:, cols], 1, 1)
        sum_ref[:, cols] = sums
    for index in range(blocks):
        e_refs[index][...] = totals[index].astype(e_refs[index].dtype)


def feed(h, ga, w, bias, first):
    rows, model = h[0].shape
    ff = w.shape[1]
    blocks = len(h)
    return pl.pallas_call(
        functools.partial(feed_kernel, first, blocks),
        in_specs=[VMEM] * (blocks + 3),
        out_specs=[VMEM] * (3 + blocks),
        out_shape=[jax.ShapeDtypeStruct((blocks * rows, ff), bf16)] * 2
        + [jax.ShapeDtypeStruct((1, ff), f32)]
        + [
            jax.ShapeDtypeStruct((rows, model), bf16 if (first + index) % 2 else f32)
            for index in range(blocks)
        ],
        compiler_params=pltpu.CompilerParams(vmem_limit_bytes=LIMIT),
        cost_estimate=pl.CostEstimate(
            flops=4 * blocks * rows * ff * model, bytes_accessed=12 * 2**20, transcendentals=2**20
        ),
        name="feed",
    )(*h, ga, bias, w)


def outer_kernel(count, side, halves, extra, info, *refs):
    lefts, rights = refs[:count], refs[count : count + 2]
    got_ref = refs[count + 2] if extra else None
    out_ref, picked, turned = refs[-3:]
    rows, model = lefts[0].shape
    shard = out_ref.shape[0] // halves
    which = jnp.bitwise_xor(lax.rem(info[3], 2), side or 0)
    for index in range(count):
        own = slice(index * rows, (index + 1) * rows)
        if side is None:
            picked[:, own] = jnp.swapaxes(lefts[index][...], 0, 1)
            continue
        if shard % 128:
            turned[...] = jnp.swapaxes(lefts[index][...], 0, 1)
        for half in range(halves):
            start = pl.multiple_of((2 * half + which) * shard, shard)
            if shard % 128:
                part = turned[pl.ds(start, shard), :]
            else:
                part = jnp.swapaxes(lefts[index][:, pl.ds(start, shard)], 0, 1)
            picked[half * shard : (half + 1) * shard, own] = part
    middle = rights[0].shape[0]
    for start in range(0, out_ref.shape[1], CHUNK):
        cols = slice(start, start + CHUNK)
        out = dot(picked[:, :middle], rights[0][:, cols], 1, 0)
        out = out + dot(picked[:, middle:], rights[1][:, cols], 1, 0)
        if extra:
            out = out + got_ref[:, cols].astype(f32)
        out_ref[:, cols] = out.astype(bf16)


def outer(lefts, rights, info, side=None, halves=1, got=None):
    rows, model = lefts[0].shape
    count = len(lefts)
    ff = rights[0].shape[1]
    extra = [] if got is None else [got]
    size = model if side is None else model // 2
    return pl.pallas_call(
        functools.partial(outer_kernel, count, side, halves, len(extra)),
        grid_spec=pltpu.PrefetchScalarGridSpec(
            num_scalar_prefetch=1,
            grid=(1,),
            in_specs=[VMEM] * (count + 2 + len(extra)),
            out_specs=VMEM,
            scratch_shapes=[pltpu.VMEM((size, count * rows), bf16), pltpu.VMEM((model, rows), bf16)],
        ),
        out_shape=jax.ShapeDtypeStruct((size, ff), bf16),
        compiler_params=pltpu.CompilerParams(vmem_limit_bytes=LIMIT),
        cost_estimate=pl.CostEstimate(
            flops=2 * count * rows * ff * size, bytes_accessed=10 * 2**20, transcendentals=0
        ),
        name="outer",
    )(info, *lefts, *rights, *extra)


def middle_outer_kernel(group, *refs):
    one, ctx_one, two, ctx_two, h, dq = refs[:6]
    outs = refs[6:]
    width = dq.shape[0] // group
    for index, (left, right) in enumerate(((one, ctx_one), (two, ctx_two), (h, dq))):
        turned = jnp.swapaxes(left[...], 0, 1)
        cols = slice(index * width, (index + 1) * width)
        for step in range(group):
            part = right[step * width : (step + 1) * width, :]
            outs[step][:, cols] = dot(turned, part, 1, 1).astype(bf16)


def middle_outer(one, ctx_one, two, ctx_two, h, dq, group):
    rows, model = one.shape
    width = dq.shape[0] // group
    return pl.pallas_call(
        functools.partial(middle_outer_kernel, group),
        in_specs=[VMEM] * 6,
        out_specs=[VMEM] * group,
        out_shape=[jax.ShapeDtypeStruct((model, 3 * width), bf16)] * group,
        compiler_params=pltpu.CompilerParams(vmem_limit_bytes=LIMIT),
        cost_estimate=pl.CostEstimate(
            flops=6 * rows * model * model, bytes_accessed=9 * 2**20, transcendentals=0
        ),
        name="middle_outer",
    )(one, ctx_one, two, ctx_two, h, dq)


def combine_kernel(extra, *refs):
    dq, dk, dv = refs[:3]
    gots, out = refs[3:-1], refs[-1]
    gots = gots[: len(gots) - extra]
    out[:, 0] = dq[...]
    for index, value in enumerate((dk, dv)):
        total = value[0]
        for got in gots[index::2]:
            total = total + got[...].astype(f32)
        out[:, 1 + index] = total.astype(bf16)


def combine(dq, dk, dv, got_k, got_v, after):
    heads, depth, piece = dq.shape
    gots = [got for pair in zip(got_k, got_v) for got in pair]
    return pl.pallas_call(
        functools.partial(combine_kernel, len(after)),
        in_specs=[VMEM] * (3 + len(gots)) + [ANY] * len(after),
        out_specs=VMEM,
        out_shape=jax.ShapeDtypeStruct((heads, 3, depth, piece), bf16),
        compiler_params=pltpu.CompilerParams(vmem_limit_bytes=LIMIT),
        cost_estimate=pl.CostEstimate(flops=2**20, bytes_accessed=5 * 2**20, transcendentals=0),
        name="combine",
    )(dq, dk, dv, *gots, *after)


def local(
    hidden,
    encoder,
    cotangent,
    block_ids,
    self_qkv,
    self_out,
    cross_qkv,
    cross_out,
    up_weight,
    down_weight,
    proj_bias,
    up_bias,
    norm_gain,
    norm_shift,
):
    tok_size, group = lax.axis_size("tok"), lax.axis_size("hd")
    tok_index, me = lax.axis_index("tok"), lax.axis_index("hd")
    rows, model = hidden.shape
    shard = self_qkv.shape[0]
    width = self_qkv.shape[2]
    ff_local = up_weight.shape[1]
    piece_rows = rows * group
    span = SEQ // piece_rows
    heads = min(width // HDIM, span)
    others = span // heads
    assert heads * HDIM == width and heads * others == span
    seq_count, enc_rows, _ = encoder.shape
    enc_total = enc_rows * group
    own_seq = tok_index // span
    at = lax.rem(tok_index, span) // others
    beside = jnp.bitwise_xor(lax.rem(tok_index, others), lax.rem(at, 2) * (others - 1))
    info = jnp.stack([at, beside, me, tok_index]).astype(jnp.int32)

    def natural(blocks):
        stacked = jnp.stack(blocks)
        return [pick(stacked, me ^ index) for index in range(group)]

    even = lax.rem(tok_index, 2)
    halves = [[i for i in range(tok_size) if i % 2 == side] for side in range(2)]
    many = tok_size // 2

    def gather_half(block):
        return lax.all_gather(block, "tok", axis=0, tiled=True, axis_index_groups=halves)

    def gather_tok(block):
        return lax.all_gather(block, "tok", axis=0, tiled=True)

    def along_halves(block):
        return lax.all_to_all(
            jnp.broadcast_to(block[None], (many, *block.shape)),
            "tok", 0, 0, tiled=True, axis_index_groups=halves,
        )

    def merge_sides(own, got):
        sides = [jnp.where(even == 0, own, got), jnp.where(even == 0, got, own)]
        return jnp.stack(sides, 1).reshape(model, -1)

    w_self = self_qkv.reshape(shard, 3, heads, HDIM).transpose(0, 2, 1, 3)
    w_self = gather_tok(w_self.reshape(shard, 3 * width))
    w_mid = along_halves(
        jnp.concatenate([self_out.T, cross_out.T, cross_qkv.reshape(shard, 3 * width)], 1)
    )

    own_ids = lax.dynamic_slice_in_dim(block_ids, me * rows, rows).astype(bf16)
    small = jnp.concatenate(
        [
            proj_bias.T.reshape(-1),
            norm_gain.T.reshape(-1),
            norm_shift.T.reshape(-1),
            up_bias,
            own_ids,
        ]
    )
    total_devices = tok_size * group
    small_all = lax.all_to_all(
        jnp.broadcast_to(small[None], (total_devices, small.shape[0])),
        ("tok", "hd"), 0, 0, tiled=True,
    ).astype(f32)
    few = model // total_devices
    vectors = small_all[:, : 13 * few].reshape(total_devices, 13, few)
    vectors = vectors.transpose(1, 0, 2).reshape(13, model)
    bias, gain, shift = vectors[:7], vectors[7:10], vectors[10:13]
    few_up = up_bias.shape[0]
    bias_up = small_all[:, 13 * few : 13 * few + few_up].reshape(-1)
    bias_up = lax.dynamic_slice_in_dim(bias_up, me * ff_local, ff_local)
    ids = small_all[:, 13 * few + few_up :].reshape(tok_size, 1, piece_rows)
    ids = lax.dynamic_slice_in_dim(ids, own_seq * span, span).reshape(heads, others, 1, piece_rows)
    ids = jnp.stack([pick(ids[i], beside ^ (i % 2 * (others - 1))) for i in range(heads)])

    def own_columns(vector):
        return lax.dynamic_slice_in_dim(vector, me * width, width)

    hidden_blocks = gather_xor(hidden)
    self_bias = jnp.stack(
        [own_columns(bias[0]), jnp.zeros((width,), f32), own_columns(bias[1])]
    )
    scale = jnp.broadcast_to(jnp.array([0.125, 1.0, 1.0], f32)[:, None], (3, width))
    factors = jnp.stack([self_bias, scale]).reshape(2, 3, heads, HDIM)
    factors = factors.transpose(0, 2, 1, 3).reshape(2, 3 * width)

    lines = [
        [seq * span + i * others + (side ^ (i % 2 * (others - 1))) for i in range(heads)]
        for seq in range(tok_size // span)
        for side in range(others)
    ]
    wide_lines = [[i * group + h for h in range(group) for i in line] for line in lines]

    def across_lines(value):
        return lax.all_to_all(value, "tok", 0, 0, tiled=True, axis_index_groups=lines)

    def across_wide(value):
        return lax.all_to_all(
            value, ("tok", "hd"), 0, 0, tiled=True, axis_index_groups=wide_lines
        )

    q_out, k_out, v_out, h_one = project(
        info, hidden_blocks, w_self, jnp.stack([gain[0], shift[0]]), factors, heads, [w_mid]
    )
    w_up, w_down = tie([up_weight, down_weight], [h_one])
    w_up, w_down = gather_tok(w_up), gather_tok(w_down.T)
    w_mid = merge_sides(w_mid, swap(w_mid, "tok", 1))
    k = [across_lines(k_out)]
    v = [across_lines(v_out)]
    q = across_lines(q_out)
    k += [swap(k[0], "tok", other) for other in range(1, others)]
    v += [swap(v[0], "tok", other) for other in range(1, others)]
    w_cross_kv = w_mid[:, 3 * width :]
    enc_all = jnp.concatenate(natural(gather_xor(encoder)), 1)
    kv_bias = jnp.concatenate([jnp.zeros((width,), f32), own_columns(bias[4])])
    kv_two = dot(w_cross_kv, pick(enc_all, own_seq), 0, 1) + kv_bias[:, None]
    kv_two = kv_two.astype(bf16).reshape(2, width, enc_total)
    kv_two = gather_xor(kv_two)

    context, log_one = self_forward(info, q, k, v, ids, rows, kv_two)

    mid_block = jnp.stack(
        [w_mid[:, :width], w_mid[:, width : 2 * width], w_mid[:, 2 * width : 3 * width]]
    )
    w_blocks = gather_xor(mid_block, lambda value: tie([value], [log_one])[0])
    ctx_one = across_wide(context).reshape(model, rows)
    norm_rows = jnp.stack([gain[1], shift[1], gain[2], shift[2], bias[2], bias[5]])
    (
        resid_two, unit_two, inv_two, unit_three, inv_three,
        h_two, h_three, ctx_one, q_two, ctx_two, log_two,
    ) = middle_forward(
        info, hidden, ctx_one, norm_rows, bias[3:4], w_blocks, kv_two, heads, []
    )

    cot_blocks = gather_xor(cotangent)
    grad_a = grad_act(cot_blocks, w_down)
    h_blocks = gather_xor(h_three, lambda got: tie([got], [grad_a])[0])
    near = group // 2
    bias_row = bias_up[None]
    near_out = feed(h_blocks[:near], grad_a, w_up, bias_row, 0)
    far_out = feed(h_blocks[near:], grad_a, w_up, bias_row, near)
    acts, grad_inners = [near_out[0], far_out[0]], [near_out[1], far_out[1]]
    up_sums = (near_out[2] + far_out[2])[0]
    grad_h_three = reduce_xor(list(near_out[3:]) + list(far_out[3:]))

    def half_columns(array, side):
        return jnp.concatenate(
            [
                lax.dynamic_slice_in_dim(array, (2 * i + side) * shard, shard, 1)
                for i in range(tok_size // 2)
            ],
            1,
        )

    def half_rows(array, side):
        return jnp.concatenate(
            [
                lax.dynamic_slice_in_dim(array, (2 * i + side) * shard, shard, 0)
                for i in range(tok_size // 2)
            ],
            0,
        )

    def reduce_tok(value):
        return lax.psum_scatter(value, "tok", scatter_dimension=0, tiled=True)

    def reduce_half(value):
        return lax.psum_scatter(
            value, "tok", scatter_dimension=0, tiled=True, axis_index_groups=halves
        )

    grad_up = outer(h_blocks, grad_inners, info)
    down_away = outer(cot_blocks, acts, info, 1, many)
    sent_up = reduce_tok(grad_up)
    down_got = swap(down_away, "tok", 1)

    grad_one, grad_two_low, grad_one_low, grad_q_two, grad_kv_two, grad_ctx_one, sums = (
        middle_backward(
            info, grad_h_three, cotangent,
            (unit_two, inv_two, unit_three, inv_three, q_two, ctx_two, log_two),
            norm_rows, w_blocks, kv_two, heads, [grad_up, down_away],
        )
    )
    grad_heads = across_wide(grad_ctx_one.reshape(group * heads, HDIM, rows))
    grad_mid = middle_outer(
        grad_one_low, ctx_one, grad_two_low, ctx_two, h_two, grad_q_two, group
    )
    masks = [1 << bit for bit in range(tok_size.bit_length() - 1)]

    def add_low(value, got):
        return (value.astype(f32) + got.astype(f32)).astype(bf16)

    grad_q_away, grad_k_away, grad_v_away = self_backward(
        info, q, k[1:], v[1:], None, grad_heads, context, log_one, None, grad_mid
    )
    down_got = tie([down_got], [grad_q_away])[0]
    down_sum = outer(cot_blocks, acts, info, 0, many, down_got)
    sent_down = reduce_half(tie([down_sum], [sent_up])[0])
    kv_total = reduce_xor(
        [grad_kv_two[j] for j in range(group)], lambda got: tie([got], [grad_q_away])[0]
    )
    seq_pick = jnp.arange(seq_count) == own_seq
    kv_total = jnp.where(seq_pick[:, None, None, None], kv_total[None], 0.0).astype(bf16)
    grad_mid = reduce_xor(grad_mid, lambda got: tie([got], [grad_q_away])[0])
    mid_got = swap(half_rows(grad_mid, 1 - even).astype(bf16), "tok", 1)
    mid_sum = (half_rows(grad_mid, even) + mid_got.astype(f32)).astype(bf16)
    sent_mid = reduce_half(tie([mid_sum], [sent_down])[0])
    grad_k_got = [swap(grad_k_away[i], "tok", i + 1) for i in range(others - 1)]
    grad_v_got = [swap(grad_v_away[i], "tok", i + 1) for i in range(others - 1)]
    grad_q, grad_k, grad_v = self_backward(
        info, q, k[:1], v[:1], ids, grad_heads, context, log_one, grad_q_away, [down_sum]
    )
    kv_got = swap(kv_total, "tok", masks[0])
    grad_qkv = combine(grad_q, grad_k, grad_v, grad_k_got, grad_v_got, [sent_up, kv_got])
    kv_total = add_low(kv_total, kv_got)
    acts = tie(acts, [grad_q])
    def act_block(index):
        start = index % near * rows
        return acts[index // near][start : start + rows]

    final = reduce_xor([dot(act_block(j), w_down, 1, 1) for j in range(group)])
    output = (resid_two + final + bias[6]).astype(bf16)
    grad_qkv = across_lines(grad_qkv).reshape(3 * width, piece_rows)
    kv_got = swap(kv_total, "tok", masks[1])
    grad_qkv, sent_down, kv_got = tie([grad_qkv, sent_down, kv_got], [])
    kv_total = add_low(kv_total, kv_got)
    for got_mask in masks[2:]:
        kv_total = add_low(kv_total, swap(kv_total, "tok", got_mask))
    kv_flat = kv_total.reshape(seq_count, 2 * width, enc_total)
    own_enc = lax.dynamic_slice_in_dim(enc_all, tok_index * shard, shard, 2)
    sent_cross_kv = sum(dot(own_enc[n], kv_flat[n], 0, 1) for n in range(seq_count))

    def encoder_part(index):
        start = (me ^ index) * enc_rows
        return jnp.stack(
            [
                dot(lax.dynamic_slice_in_dim(kv_flat[n], start, enc_rows, 1), w_cross_kv, 0, 1)
                for n in range(seq_count)
            ]
        )

    grad_encoder = reduce_xor([encoder_part(j) for j in range(group)])

    grad_self = dot(h_one, grad_qkv, 0, 1).astype(bf16)
    sent_self = lax.all_to_all(grad_self, "tok", 0, 0, tiled=True)
    ordered = sent_self
    sent_self = jnp.sum(sent_self.reshape(tok_size, shard, 3 * width).astype(f32), 0)
    sent_self = sent_self.reshape(shard, heads, 3, HDIM)
    sent_self = sent_self.transpose(0, 2, 1, 3).reshape(shard, 3, width)
    grad_qkv = tie([grad_qkv], [grad_self])[0]
    grad_h_one = reduce_xor(
        [
            dot(
                lax.dynamic_slice(grad_qkv, (0, (me ^ j) * rows), (3 * width, rows)), w_self, 0, 1
            )
            for j in range(group)
        ]
    )
    unit_one, inverse_one = normalize(hidden.astype(f32))
    back, gain_one, shift_one = norm_backward(grad_h_one, unit_one, inverse_one, gain[0])
    grad_hidden = grad_one + back

    def place(vector):
        return lax.dynamic_update_slice_in_dim(jnp.zeros((model,), f32), vector, me * width, 0)

    qkv_sums = jnp.sum(grad_qkv.astype(f32), 1).reshape(heads, 3, HDIM)
    once = (tok_index == 0).astype(f32)
    late = jnp.concatenate(
        [
            place(qkv_sums[:, 0].reshape(-1)),
            place(qkv_sums[:, 2].reshape(-1)),
            place(jnp.sum(kv_flat[:, width:].astype(f32), (0, 2)) * once),
            gain_one,
            shift_one,
        ]
    )
    vectors = jnp.concatenate([sums, late.reshape(5, model)], 0)
    vectors = vectors.reshape(13, total_devices, few).transpose(1, 0, 2).reshape(total_devices, -1)
    up_all = lax.dynamic_update_slice_in_dim(
        jnp.zeros((group * ff_local,), f32), up_sums, me * ff_local, 0
    )
    vectors = jnp.concatenate([vectors, up_all.reshape(total_devices, -1)], 1)
    vectors = tie([vectors], [ordered])[0]
    vectors = jnp.sum(lax.all_to_all(vectors, ("tok", "hd"), 0, 0, tiled=True), 0)
    columns = vectors[: 13 * few].reshape(13, few)
    columns = columns[jnp.array([8, 9, 5, 7, 10, 4, 6, 11, 2, 0, 12, 3, 1])].T

    sent_mid = sent_mid.astype(f32)
    sent_mid = [sent_mid[:, j * width : (j + 1) * width] for j in range(3)]
    sent_cross = jnp.concatenate(
        [sent_mid[2][:, None], sent_cross_kv.reshape(shard, 2, width)], 1
    )
    return (
        output,
        grad_hidden,
        grad_encoder,
        sent_self,
        sent_mid[0].T,
        sent_cross,
        sent_mid[1].T,
        sent_up.astype(f32),
        sent_down.astype(f32).T,
        columns[:, :7],
        vectors[13 * few :],
        columns[:, 7:10],
        columns[:, 10:13],
    )


def solution(mesh):
    in_specs = (
        P(("tok", "hd"), None),
        P(None, "hd", None),
        P(("tok", "hd"), None),
        P("tok"),
        P("tok", None, "hd"),
        P("hd", "tok"),
        P("tok", None, "hd"),
        P("hd", "tok"),
        P("tok", "hd"),
        P("hd", "tok"),
        P(("tok", "hd"), None),
        P(("tok", "hd")),
        P(("tok", "hd"), None),
        P(("tok", "hd"), None),
    )
    out_specs = (
        P(("tok", "hd"), None),
        P(("tok", "hd"), None),
        P(None, "hd", None),
        P("tok", None, "hd"),
        P("hd", "tok"),
        P("tok", None, "hd"),
        P("hd", "tok"),
        P("tok", "hd"),
        P("hd", "tok"),
        P(("tok", "hd"), None),
        P(("tok", "hd")),
        P(("tok", "hd"), None),
        P(("tok", "hd"), None),
    )
    return jax.shard_map(local, mesh=mesh, in_specs=in_specs, out_specs=out_specs, check_vma=False)
```
